512 devices in a mesh: gx: 16 (over z), gy: 16 (over x_lo, y, core), gz: 2 (over x_hi).
Axes of the slice: x: 4 (x_hi: 2, x_lo: 2; x = x_hi * 2 + x_lo), y: 4, z: 16, core: 2. Of those that a mesh axis runs over, the one named last changes fastest.
Arguments:
- features: bfloat16 [16, 16, 2, 1, 96, 512], P('gx', 'gy', 'gz'), may hold values from -6 to 6
- cotangent: bfloat16 [16, 16, 2, 1, 96, 512], P('gx', 'gy', 'gz'), may hold values from -6 to 6
- first_weight: bfloat16 [27, 96, 96], replicated, may hold values from -0.1875 to 0.1875
- second_weight: bfloat16 [27, 96, 96], replicated, may hold values from -0.1875 to 0.1875
- slot_position: int32 [16, 16, 2, 1], P('gx', 'gy', 'gz'), may hold values from 0 to 7, as said below
- brick_count: int32 [16, 16, 2], P('gx', 'gy', 'gz'), may hold values from 0 to 1, as said below
- column_code: int32 [16, 16, 2, 1, 64], P('gx', 'gy', 'gz'), may hold values from 0 to 63
Outputs:
- grad_input: bfloat16 [16, 16, 2, 1, 96, 512], P('gx', 'gy', 'gz')
- grad_first: float32 [27, 96, 96], replicated
- grad_second: float32 [27, 96, 96], replicated
The draws below stay inside these ranges and needn't reach their ends.
Inputs may be any that keep to these rules, and one draw needn't show every extreme that they name: `slot_position`: within one device the slots hold distinct positions of 0 to 7. `brick_count`: slots from this number on are empty: their features, cotangents and codes carry no meaning; some device has 1.
All inputs are finite; a program needn't handle non-finite values.
Results may differ from the reference program's by a relative error of at most 0.0034.
Values may be sent and summed in bfloat16 or wider, within the bound.
A program may use at most 64 MiB of HBM per device.

```python
import jax
import jax.numpy as jnp
from jax import lax

C = 96
VOX = 512
RX = 2
RY = 2
RZ = 2
NB = 1
N_GX = 16
N_GY = 16
N_GZ = 2


def draw_slot_position(key, part):
    key = jax.random.fold_in(key, 11)
    region = RX * RY * RZ
    scores = jax.random.randint(key, (N_GX, N_GY, N_GZ, region), 0, 2 ** 20) * region + jnp.arange(region, dtype=jnp.int32)
    return jnp.argsort(scores, axis=-1)[..., :NB].astype(jnp.int32)


def draw_brick_count(key, part):
    key = jax.random.fold_in(key, 23)
    key_busy, key_pick = jax.random.split(key, 2)
    grid_shape = (N_GX, N_GY, N_GZ)
    busy = jax.random.randint(key_busy, grid_shape, 0, 4) != 0
    counts = jnp.where(busy, NB, NB - 1)
    chosen = jax.random.randint(key_pick, (), 0, N_GX * N_GY * N_GZ)
    flat_ids = jnp.arange(N_GX * N_GY * N_GZ, dtype=jnp.int32).reshape(grid_shape)
    return jnp.where(flat_ids == chosen, NB, counts).astype(jnp.int32)


def touch_ends(entries, own_key, smallest, top_value):
    longest = entries.shape.index(max(entries.shape))
    spots = []
    for shift in (0, 1):
        where = [jax.random.randint(jax.random.fold_in(own_key, axis), (), 0, length) for axis, length in enumerate(entries.shape)]
        where[longest] = (where[longest] + shift) % entries.shape[longest]
        spots.append(tuple(where))
    return entries.at[spots[0]].set(smallest).at[spots[1]].set(top_value)


def block_levels(rng, dims, pieces, low, high):
    loudness, own = 1.0, jax.random.fold_in(rng, 6)
    for dim, parts in pieces:
        heights = jnp.exp(jax.random.uniform(jax.random.fold_in(own, dim), (parts,), jnp.float32, low / len(pieces), high / len(pieces)))
        loudness = loudness * jnp.repeat(heights, dims[dim] // parts).reshape([-1 if axis == dim else 1 for axis in range(len(dims))])
    return loudness


def centred(rng, extent, width, bound, shards=(), kind=jnp.bfloat16):
    entries = width * jax.random.normal(rng, extent, jnp.float32)
    if shards:
        entries = entries * block_levels(rng, extent, shards, -0.22, 0.18)
    return jnp.clip(entries, -bound, bound).astype(kind)


def setup_inputs(seed: int = 0) -> dict:
    splits = jax.random.split(jax.random.key(seed), 8)
    return {
        "features": centred(splits[0], (N_GX, N_GY, N_GZ, NB, C, VOX), 1.0, 6.0, ((0, 16), (1, 16), (2, 2))),
        "cotangent": centred(splits[1], (N_GX, N_GY, N_GZ, NB, C, VOX), 1.0, 6.0, ((0, 16), (1, 16), (2, 2))),
        "first_weight": centred(splits[2], (27, C, C), (10 * C) ** -0.5, 0.1875),
        "second_weight": centred(splits[3], (27, C, C), (10 * C) ** -0.5, 0.1875),
        "slot_position": draw_slot_position(jax.random.fold_in(splits[7], 71), 0),
        "brick_count": draw_brick_count(jax.random.fold_in(splits[7], 71), 0),
        "column_code": touch_ends(jax.random.randint(splits[6], (N_GX, N_GY, N_GZ, NB, 64), 0, 64), jax.random.fold_in(splits[6], 1), 0, 63).astype(jnp.int32),
    }


def voxel_mask(column_codes, live_count, slots):
    levels = jnp.arange(8, dtype=jnp.int32)
    lowest = column_codes // 8
    beyond = lowest + column_codes % 8 + 1
    inside = (levels[None, None, :] >= lowest[:, :, None]) & (levels[None, None, :] < beyond[:, :, None])
    living = jnp.arange(slots, dtype=jnp.int32) < live_count
    return (inside & living[:, None, None]).reshape(slots, 512).astype(jnp.float32)


def to_region(bricks, sides):
    side_x, side_y, side_z = sides
    channels = bricks.shape[1]
    blocks = bricks.reshape(side_x, side_y, side_z, channels, 8, 8, 8)
    blocks = blocks.transpose(3, 0, 4, 1, 5, 2, 6)
    return blocks.reshape(channels, side_x * 8, side_y * 8, side_z * 8)


def cut_patches(padded, positions):
    def single(position):
        corner_x = position // (RY * RZ) * 8
        corner_y = position // RZ % RY * 8
        corner_z = position % RZ * 8
        anchor = jnp.zeros((), jnp.int32)
        return lax.dynamic_slice(padded, (anchor, corner_x, corner_y, corner_z), (padded.shape[0], 10, 10, 10))
    return jax.vmap(single)(positions)


def block_cols(patches, step_x, facing):
    gathered = []
    for step_y in (-1, 0, 1):
        for step_z in (-1, 0, 1):
            start_x = 1 + facing * step_x
            start_y = 1 + facing * step_y
            start_z = 1 + facing * step_z
            sliced = patches[:, :, start_x:start_x + 8, start_y:start_y + 8, start_z:start_z + 8]
            gathered.append(sliced.reshape(patches.shape[0], patches.shape[1], 512))
    return jnp.concatenate(gathered, axis=1)


def product(left_side, right_side, formula):
    return jnp.einsum(formula, left_side.astype(jnp.float32), right_side.astype(jnp.float32))


def device_mask(codes_row, count_one):
    return voxel_mask(codes_row, count_one, NB)


def reference(features, cotangent, first_weight, second_weight, slot_position, brick_count, column_code):
    devices = N_GX * N_GY * N_GZ
    total = devices * NB
    scale = total ** -0.5 / 8.0
    masks = jax.vmap(device_mask)(column_code.reshape(devices, NB, 64), brick_count.reshape(devices))
    cut_mask = masks[:, :, None, :].astype(jnp.bfloat16)
    inputs = features.reshape(devices, NB, C, 512) * cut_mask
    upstream = cotangent.reshape(devices, NB, C, 512) * cut_mask
    positions = slot_position.reshape(devices, NB)
    device_ids = jnp.arange(devices, dtype=jnp.int32)
    device_x = device_ids // (N_GY * N_GZ)
    device_y = device_ids // N_GZ % N_GY
    device_z = device_ids % N_GZ
    brick_x = device_x[:, None] * RX + positions // (RY * RZ) + 1
    brick_y = device_y[:, None] * RY + positions // RZ % RY + 1
    brick_z = device_z[:, None] * RZ + positions % RZ + 1
    slot_ids = jnp.arange(total, dtype=jnp.int32).reshape(devices, NB)
    table_ids = jnp.full((N_GX * RX + 2, N_GY * RY + 2, N_GZ * RZ + 2), total, jnp.int32)
    table_ids = table_ids.at[brick_x, brick_y, brick_z].set(slot_ids)

    def padded_region(table, place_x, place_y, place_z):
        near_ids = lax.dynamic_slice(table_ids, (place_x * RX, place_y * RY, place_z * RZ), (RX + 2, RY + 2, RZ + 2))
        bricks = table[near_ids.reshape(-1)]
        whole = to_region(bricks, (RX + 2, RY + 2, RZ + 2))
        return whole[:, 7:RX * 8 + 9, 7:RY * 8 + 9, 7:RZ * 8 + 9]

    joined = jnp.concatenate([inputs, upstream], axis=2).reshape(total, 2 * C, 512)
    joined = jnp.concatenate([joined, jnp.zeros((1, 2 * C, 512), jnp.bfloat16)], axis=0)
    first_blocks = first_weight.reshape(3, 9 * C, C)
    second_back = second_weight.transpose(0, 2, 1).reshape(3, 9 * C, C)
    first_back = first_weight.transpose(0, 2, 1).reshape(3, 9 * C, C)

    def forward_step(sums, carried):
        place_x, place_y, place_z, spots, occupied = carried
        patches = cut_patches(padded_region(joined, place_x, place_y, place_z), spots)
        input_patch = patches[:, :C]
        upstream_patch = patches[:, C:]
        pre_act = jnp.zeros((NB, C, 512), jnp.float32)
        back_act = jnp.zeros((NB, C, 512), jnp.float32)
        for step_x in (-1, 0, 1):
            pre_act = pre_act + product(block_cols(input_patch, step_x, 1), first_blocks[step_x + 1], "sjv,jo->sov")
            back_act = back_act + product(block_cols(upstream_patch, step_x, -1), second_back[step_x + 1], "sjv,jc->scv")
        sigma = jax.nn.sigmoid(pre_act)
        hidden = (pre_act * sigma * occupied[:, None, :]).astype(jnp.bfloat16)
        delta = (back_act * sigma * (1.0 + pre_act * (1.0 - sigma)) * occupied[:, None, :]).astype(jnp.bfloat16)
        first_parts = []
        second_parts = []
        for step_x in (-1, 0, 1):
            first_parts.append(product(block_cols(input_patch, step_x, 1), delta, "sjv,sov->jo").reshape(9, C, C))
            second_term = product(hidden, block_cols(upstream_patch, step_x, -1), "scv,sjv->cj")
            second_parts.append(second_term.reshape(C, 9, C).transpose(1, 0, 2))
        return (sums[0] + jnp.concatenate(first_parts, axis=0), sums[1] + jnp.concatenate(second_parts, axis=0)), delta

    zero_grad = jnp.zeros((27, C, C), jnp.float32)
    sums_out, deltas = lax.scan(forward_step, (zero_grad, zero_grad), (device_x, device_y, device_z, positions, masks))
    delta_table = jnp.concatenate([deltas.reshape(total, C, 512), jnp.zeros((1, C, 512), jnp.bfloat16)], axis=0)

    def backward_step(unused, carried):
        place_x, place_y, place_z, spots, occupied, upstream_slots = carried
        patches = cut_patches(padded_region(delta_table, place_x, place_y, place_z), spots)
        back_input = upstream_slots.astype(jnp.float32)
        for step_x in (-1, 0, 1):
            back_input = back_input + product(block_cols(patches, step_x, -1), first_back[step_x + 1], "sjv,jc->scv")
        return unused, (back_input * occupied[:, None, :]).astype(jnp.bfloat16)

    leftover, grad_slots = lax.scan(backward_step, jnp.zeros((), jnp.float32), (device_x, device_y, device_z, positions, masks, upstream))
    grad_input = grad_slots.reshape(N_GX, N_GY, N_GZ, NB, C, 512)
    return grad_input, sums_out[0] * scale, sums_out[1] * scale
```

```python
import jax
import jax.numpy as jnp
from jax import lax
from jax.experimental import pallas as pl
from jax.experimental.pallas import tpu as pltpu
from jax.sharding import PartitionSpec as P

RX = 2
RY = 2
RZ = 2


MESH = pl.DeviceIdType.MESH
ROWS = 4096
HALF = ROWS // 2
PART = HALF // 16
CELL = PART // 16


def reduce_kernel(d_ref, out_ref, half_out, half_in, total, plane_out, plane_in, cell_src,
                  line_in, line_all, own_part, gathered, pair_sem, plane_send, plane_recv,
                  line_send, line_recv, line_send2, line_recv2, plane_send2, plane_recv2):
    u = lax.axis_index("gx")
    w = lax.axis_index("gy")
    q = lax.axis_index("gz")
    core = w % 2
    y = w // 2 % 4
    x = q * 2 + w // 8
    chip = x * 4 + y
    mate = (u, w + 1 - 2 * core, q)

    def plane_peer(t):
        px = (x + t // 4) % 4
        py = (y + t % 4) % 4
        return px * 4 + py, (u, ((px % 2) * 4 + py) * 2 + core, px // 2)

    def line_peer(t):
        z = (u + t) % 16
        return z, (z, w, q)

    barrier = pltpu.get_barrier_semaphore()
    pl.semaphore_signal(barrier, inc=1, device_id=mate, device_id_type=MESH)

    def greet(t, carry):
        pl.semaphore_signal(barrier, inc=1, device_id=plane_peer(t)[1], device_id_type=MESH)
        pl.semaphore_signal(barrier, inc=1, device_id=line_peer(t)[1], device_id_type=MESH)
        return carry

    lax.fori_loop(1, 16, greet, 0)
    pl.semaphore_wait(barrier, 31)

    other = pl.multiple_of((1 - core) * HALF, HALF)
    own = pl.multiple_of(core * HALF, HALF)
    half_out[...] = d_ref[pl.ds(other, HALF), :].astype(jnp.bfloat16)
    swap = pltpu.make_async_remote_copy(
        src_ref=half_out, dst_ref=half_in, send_sem=pair_sem.at[0], recv_sem=pair_sem.at[1],
        device_id=mate, device_id_type=MESH)
    swap.start()
    swap.wait()
    total[...] = d_ref[pl.ds(own, HALF), :] + half_in[...].astype(jnp.float32)
    plane_out[...] = total[...].astype(jnp.bfloat16)

    def plane_copy(t):
        there, device = plane_peer(t)
        return pltpu.make_async_remote_copy(
            src_ref=plane_out.at[pl.ds(pl.multiple_of(there * PART, PART), PART), :],
            dst_ref=plane_in.at[t], send_sem=plane_send.at[t], recv_sem=plane_recv.at[t],
            device_id=device, device_id_type=MESH)

    def plane_start(t, carry):
        plane_copy(t).start()
        return carry

    lax.fori_loop(1, 16, plane_start, 0)
    mine = pl.multiple_of(chip * PART, PART)

    def plane_add(t, acc):
        plane_copy(t).wait_recv()
        return acc + plane_in[t].astype(jnp.float32)

    cell_src[...] = lax.fori_loop(1, 16, plane_add, total[pl.ds(mine, PART), :])

    def line_copy(t):
        there, device = line_peer(t)
        return pltpu.make_async_remote_copy(
            src_ref=cell_src.at[pl.ds(pl.multiple_of(there * CELL, CELL), CELL), :],
            dst_ref=line_in.at[t], send_sem=line_send.at[t], recv_sem=line_recv.at[t],
            device_id=device, device_id_type=MESH)

    def line_start(t, carry):
        line_copy(t).start()
        return carry

    lax.fori_loop(1, 16, line_start, 0)
    here = pl.multiple_of(u * CELL, CELL)

    def line_add(t, acc):
        line_copy(t).wait_recv()
        return acc + line_in[t]

    line_all[pl.ds(here, CELL), :] = lax.fori_loop(1, 16, line_add, cell_src[pl.ds(here, CELL), :])

    def spread_copy(t):
        there, device = line_peer(t)
        return pltpu.make_async_remote_copy(
            src_ref=line_all.at[pl.ds(here, CELL), :],
            dst_ref=line_all.at[pl.ds(here, CELL), :], send_sem=line_send2.at[t], recv_sem=line_recv2.at[t],
            device_id=device, device_id_type=MESH)

    def arrive_copy(t):
        z = (u - t + 16) % 16
        rows = pl.ds(pl.multiple_of(z * CELL, CELL), CELL)
        return pltpu.make_async_remote_copy(
            src_ref=line_all.at[rows, :],
            dst_ref=line_all.at[rows, :], send_sem=line_send2.at[t], recv_sem=line_recv2.at[t],
            device_id=line_peer(t)[1], device_id_type=MESH)

    def spread_start(t, carry):
        spread_copy(t).start()
        return carry

    def spread_wait(t, carry):
        arrive_copy(t).wait_recv()
        return carry

    lax.fori_loop(1, 16, spread_start, 0)
    lax.fori_loop(1, 16, spread_wait, 0)
    own_part[...] = line_all[...].astype(jnp.bfloat16)

    place = pl.multiple_of(own + mine, PART)
    gathered[pl.ds(place, PART), :] = own_part[...]

    def back_copy(t):
        there, device = plane_peer(t)
        return pltpu.make_async_remote_copy(
            src_ref=own_part,
            dst_ref=gathered.at[pl.ds(place, PART), :], send_sem=plane_send2.at[t], recv_sem=plane_recv2.at[t],
            device_id=device, device_id_type=MESH)

    def back_arrive(t):
        px = (x - t // 4 + 4) % 4
        py = (y - t % 4 + 4) % 4
        rows = pl.ds(pl.multiple_of(own + (px * 4 + py) * PART, PART), PART)
        return pltpu.make_async_remote_copy(
            src_ref=own_part,
            dst_ref=gathered.at[rows, :], send_sem=plane_send2.at[t], recv_sem=plane_recv2.at[t],
            device_id=plane_peer(t)[1], device_id_type=MESH)

    def back_start(t, carry):
        back_copy(t).start()
        return carry

    def back_wait(t, carry):
        back_arrive(t).wait_recv()
        return carry

    lax.fori_loop(1, 16, back_start, 0)
    lax.fori_loop(1, 16, back_wait, 0)

    join = pltpu.make_async_remote_copy(
        src_ref=gathered.at[pl.ds(own, HALF), :], dst_ref=gathered.at[pl.ds(own, HALF), :],
        send_sem=pair_sem.at[2], recv_sem=pair_sem.at[3],
        device_id=mate, device_id_type=MESH)
    join.start()

    def drain(t, carry):
        plane_copy(t).wait_send()
        line_copy(t).wait_send()
        spread_copy(t).wait_send()
        back_copy(t).wait_send()
        return carry

    lax.fori_loop(1, 16, drain, 0)
    join.wait_send()
    arrive = pltpu.make_async_remote_copy(
        src_ref=gathered.at[pl.ds(other, HALF), :], dst_ref=gathered.at[pl.ds(other, HALF), :],
        send_sem=pair_sem.at[2], recv_sem=pair_sem.at[3],
        device_id=mate, device_id_type=MESH)
    arrive.wait_recv()
    out_ref[...] = gathered[...].astype(jnp.float32)


def all_sum(data):
    sems = lambda n: pltpu.SemaphoreType.DMA((n,))
    return pl.pallas_call(
        reduce_kernel,
        out_shape=jax.ShapeDtypeStruct((ROWS, 128), jnp.float32),
        in_specs=[pl.BlockSpec(memory_space=pltpu.VMEM)],
        out_specs=pl.BlockSpec(memory_space=pltpu.VMEM),
        scratch_shapes=[
            pltpu.VMEM((HALF, 128), jnp.bfloat16),
            pltpu.VMEM((HALF, 128), jnp.bfloat16),
            pltpu.VMEM((HALF, 128), jnp.float32),
            pltpu.VMEM((HALF, 128), jnp.bfloat16),
            pltpu.VMEM((16, PART, 128), jnp.bfloat16),
            pltpu.VMEM((PART, 128), jnp.float32),
            pltpu.VMEM((16, CELL, 128), jnp.float32),
            pltpu.VMEM((PART, 128), jnp.float32),
            pltpu.VMEM((PART, 128), jnp.bfloat16),
            pltpu.VMEM((ROWS, 128), jnp.bfloat16),
            sems(4), sems(16), sems(16), sems(16), sems(16), sems(16), sems(16), sems(16), sems(16),
        ],
        compiler_params=pltpu.CompilerParams(
            collective_id=3, has_side_effects=True, vmem_limit_bytes=32 * 2 ** 20),
        name="all_sum",
    )(data)


def padded_2(block, sides, width):
    for axis, dim in sides:
        count = lax.axis_size(axis)
        forward = [(i, i + 1) for i in range(count - 1)]
        backward = [(target, source) for source, target in forward]
        low = lax.ppermute(
            lax.slice_in_dim(block, block.shape[dim] - width, None, axis=dim), axis, forward
        )
        high = lax.ppermute(lax.slice_in_dim(block, 0, width, axis=dim), axis, backward)
        block = jnp.concatenate([low, block, high], axis=dim)
    return block


def voxel_mask(column_codes, live_count, slots):
    levels = jnp.arange(8, dtype=jnp.int32)
    lowest = column_codes // 8
    beyond = lowest + column_codes % 8 + 1
    inside = (levels[None, None, :] >= lowest[:, :, None]) & (
        levels[None, None, :] < beyond[:, :, None]
    )
    living = jnp.arange(slots, dtype=jnp.int32) < live_count
    return (inside & living[:, None, None]).reshape(slots, 512).astype(jnp.float32)


def to_region(bricks):
    channels = bricks.shape[1]
    blocks = bricks.reshape(RX, RY, RZ, channels, 8, 8, 8)
    blocks = blocks.transpose(3, 0, 4, 1, 5, 2, 6)
    return blocks.reshape(channels, RX * 8, RY * 8, RZ * 8)


def cut_patches(padded, positions):

    def single(position):
        corner_x = position // (RY * RZ) * 8
        corner_y = position // RZ % RY * 8
        corner_z = position % RZ * 8
        anchor = jnp.zeros((), jnp.int32)
        return lax.dynamic_slice(
            padded, (anchor, corner_x, corner_y, corner_z), (padded.shape[0], 10, 10, 10)
        )

    return jax.vmap(single)(positions)


def block_cols(patches, step_x, facing):
    gathered = []
    for step_y in (-1, 0, 1):
        for step_z in (-1, 0, 1):
            start_x = 1 + facing * step_x
            start_y = 1 + facing * step_y
            start_z = 1 + facing * step_z
            sliced = patches[
                :, :, start_x : start_x + 8, start_y : start_y + 8, start_z : start_z + 8
            ]
            gathered.append(sliced.reshape(patches.shape[0], patches.shape[1], 512))
    return jnp.concatenate(gathered, axis=1)


def shards(
    features, cotangent, first_weight, second_weight, slot_position, brick_count, column_code
):
    slots = features.shape[3]
    channels = features.shape[4]
    positions = slot_position.reshape(slots)
    occupied = voxel_mask(column_code.reshape(slots, 64), brick_count.reshape(()), slots)
    cut_mask = occupied[:, None, :].astype(jnp.bfloat16)
    inputs = features.reshape(slots, channels, 512) * cut_mask
    upstream = cotangent.reshape(slots, channels, 512) * cut_mask
    placing = (positions[:, None] == jnp.arange(RX * RY * RZ, dtype=jnp.int32)[None, :]).astype(
        jnp.bfloat16
    )
    total = slots * lax.axis_size("gx") * lax.axis_size("gy") * lax.axis_size("gz")
    scale = total ** (-0.5) / 8.0

    def regional(bricks):
        spread = jnp.einsum("sr,scv->rcv", placing, bricks, preferred_element_type=jnp.float32)
        return to_region(spread.astype(jnp.bfloat16))

    joined = regional(jnp.concatenate([inputs, upstream], axis=1))
    padded = padded_2(joined, (("gx", 1), ("gy", 2), ("gz", 3)), 1)
    patches = cut_patches(padded, positions)
    input_patch = patches[:, :channels]
    upstream_patch = patches[:, channels:]
    first_blocks = first_weight.reshape(3, 9 * channels, channels)
    second_back = second_weight.transpose(0, 2, 1).reshape(3, 9 * channels, channels)
    first_back = first_weight.transpose(0, 2, 1).reshape(3, 9 * channels, channels)
    pre_act = jnp.zeros((slots, channels, 512), jnp.float32)
    back_act = jnp.zeros((slots, channels, 512), jnp.float32)
    for step_x in (-1, 0, 1):
        pre_act = pre_act + jnp.einsum(
            "sjv,jo->sov",
            block_cols(input_patch, step_x, 1),
            first_blocks[step_x + 1],
            preferred_element_type=jnp.float32,
        )
        back_act = back_act + jnp.einsum(
            "sjv,jc->scv",
            block_cols(upstream_patch, step_x, -1),
            second_back[step_x + 1],
            preferred_element_type=jnp.float32,
        )
    sigma = jax.nn.sigmoid(pre_act)
    hidden = (pre_act * sigma * occupied[:, None, :]).astype(jnp.bfloat16)
    delta = (back_act * sigma * (1.0 + pre_act * (1.0 - sigma)) * occupied[:, None, :]).astype(
        jnp.bfloat16
    )
    second_parts = []
    hidden_pad = padded_2(regional(hidden), (("gx", 1), ("gy", 2), ("gz", 3)), 1)
    hidden_patch = cut_patches(hidden_pad, positions)
    for step_x in (-1, 0, 1):
        second_term = jnp.einsum(
            "sjv,sov->jo",
            block_cols(hidden_patch, step_x, 1),
            upstream,
            preferred_element_type=jnp.float32,
        )
        second_parts.append(second_term.reshape(9, channels, channels))
    second_local = jnp.concatenate(second_parts, axis=0)
    delta_pad = padded_2(regional(delta), (("gx", 1), ("gy", 2), ("gz", 3)), 1)
    delta_patch = cut_patches(delta_pad, positions)
    back_input = upstream.astype(jnp.float32)
    first_parts = []
    for step_x in (-1, 0, 1):
        back_input = back_input + jnp.einsum(
            "sjv,jc->scv",
            block_cols(delta_patch, step_x, -1),
            first_back[step_x + 1],
            preferred_element_type=jnp.float32,
        )
        first_term = jnp.einsum(
            "sjv,sov->jo",
            block_cols(input_patch, step_x, 1),
            delta,
            preferred_element_type=jnp.float32,
        )
        first_parts.append(first_term.reshape(9, channels, channels))
    first_local = jnp.concatenate(first_parts, axis=0)
    grad_input = (back_input * occupied[:, None, :]).astype(jnp.bfloat16)
    count = 27 * channels * channels
    joined_grads = jnp.concatenate([first_local.reshape(-1), second_local.reshape(-1)]) * scale
    padded_grads = jnp.pad(joined_grads, (0, ROWS * 128 - 2 * count)).reshape(ROWS, 128)
    summed = all_sum(padded_grads).reshape(-1)
    first_grad = summed[:count].reshape(27, channels, channels)
    second_grad = summed[count : 2 * count].reshape(27, channels, channels)
    return (grad_input.reshape(1, 1, 1, slots, channels, 512), first_grad, second_grad)


def solution(mesh):
    placed = (
        P("gx", "gy", "gz", None, None, None),
        P("gx", "gy", "gz", None, None, None),
        P(),
        P(),
        P("gx", "gy", "gz", None),
        P("gx", "gy", "gz"),
        P("gx", "gy", "gz", None, None),
    )
    return jax.shard_map(
        shards,
        mesh=mesh,
        in_specs=placed,
        out_specs=(P("gx", "gy", "gz", None, None, None), P(), P()),
        check_vma=False,
    )
```

```python
import functools

import jax
import jax.numpy as jnp
from jax import lax
from jax.experimental import pallas as pl
from jax.experimental.pallas import tpu as pltpu
from jax.sharding import PartitionSpec as P

MESH = pl.DeviceIdType.MESH
VMEM = pl.BlockSpec(memory_space=pltpu.VMEM)
SMEM = pl.BlockSpec(memory_space=pltpu.SMEM)
C = 96
WIDE = 128
MSG = 512
BF = jnp.bfloat16
F32 = jnp.float32


def message_plan():
    plan = []
    for ix in (0, 1):
        plan.append((ix, 64, (1 - 2 * ix, 0, 0)))
    for iy in (0, 1):
        plan.append((2 + iy, 64, (0, 1 - 2 * iy, 0)))
    plan.append((4, 64, (0, 0, 1)))
    for ix in (0, 1):
        for iy in (0, 1):
            plan.append((5 + 2 * ix + iy, 16, (1 - 2 * ix, 1 - 2 * iy, 0)))
    for ix in (0, 1):
        plan.append((9 + ix, 16, (1 - 2 * ix, 0, 1)))
    for iy in (0, 1):
        plan.append((11 + iy, 16, (0, 1 - 2 * iy, 1)))
    for ix in (0, 1):
        for iy in (0, 1):
            plan.append((13 + 2 * ix + iy, 16, (1 - 2 * ix, 1 - 2 * iy, 1)))
    return plan


def slot_row(slot):
    return slot * 64 if slot < 5 else 320 + (slot - 5) * 16


def pack_messages(wide_ref, msg_ref, q):
    blank = jnp.zeros((8, WIDE), F32)
    only = lax.broadcasted_iota(jnp.int32, (8, WIDE), 0) == 0
    for part in range(wide_ref.shape[0]):

        def rows(*spot, **stride):
            return wide_ref[part, pl.ds(*spot, **stride), :]

        def put(slot, value):
            start = slot_row(slot)
            msg_ref[pl.ds(start, value.shape[0]), pl.ds(part * WIDE, WIDE)] = value.astype(BF)

        def side(low, high):
            return jnp.where(q == 0, high, low)

        for ix in (0, 1):
            put(ix, rows(448 * (1 - ix), 64))
        for iy in (0, 1):
            edge = [rows(64 * i + 56 * (1 - iy), 8) for i in range(8)]
            put(2 + iy, jnp.concatenate(edge, axis=0))
        put(4, side(rows(0, 64, stride=8), rows(7, 64, stride=8)))
        for ix in (0, 1):
            x0 = 448 * (1 - ix)
            for iy in (0, 1):
                column = rows(x0 + 56 * (1 - iy), 8)
                put(5 + 2 * ix + iy, jnp.concatenate([column, blank], axis=0))
                corner = side(column, pltpu.roll(column, 1, 0))
                put(13 + 2 * ix + iy, jnp.concatenate([jnp.where(only, corner, 0.0), blank], axis=0))
            line = side(rows(x0, 8, stride=8), rows(x0 + 7, 8, stride=8))
            put(9 + ix, jnp.concatenate([line, blank], axis=0))
        for iy in (0, 1):
            y0 = 56 * (1 - iy)
            line = side(rows(y0, 8, stride=64), rows(y0 + 7, 8, stride=64))
            put(11 + iy, jnp.concatenate([line, blank], axis=0))


def pack_kernel(place_ref, x_ref, g_ref, code_ref, rows_ref, msg_ref, wide_ref):
    position, count, q = place_ref[0], place_ref[1], place_ref[4]
    column = lax.broadcasted_iota(jnp.int32, (64, 512), 0)
    voxel = lax.broadcasted_iota(jnp.int32, (64, 512), 1)
    spread = jnp.where(column == voxel // 8, 1.0, 0.0).astype(BF)
    codes = jnp.broadcast_to(code_ref[...].astype(F32), (16, 64)).astype(BF)
    code = jnp.dot(codes, spread, preferred_element_type=F32).astype(jnp.int32)[:8]
    low = code // 8
    level = lax.broadcasted_iota(jnp.int32, (8, 512), 1) % 8
    live = (level >= low) & (level <= low + code % 8) & (count > 0)
    mask = jnp.where(live, 1.0, 0.0)
    first = lax.broadcasted_iota(jnp.int32, (8, 512), 0)
    place = jnp.where(first == 0, position.astype(F32), jnp.where(first == 1, mask, 0.0))
    blank = jnp.zeros((24, 512), F32)
    inside = jnp.broadcast_to(mask[:1], (C, 512)) > 0.0
    x = jnp.where(inside, x_ref[...].astype(F32), 0.0)
    g = jnp.where(inside, g_ref[...].astype(F32), 0.0)
    wide_ref[0] = jnp.concatenate([x, place, blank], axis=0).T
    wide_ref[1] = jnp.concatenate([g, jnp.zeros((32, 512), F32)], axis=0).T
    rows_ref[:, :WIDE] = wide_ref[0].astype(BF)
    rows_ref[:, WIDE:] = wide_ref[1].astype(BF)
    pack_messages(wide_ref, msg_ref, q)


def pack(place, x, g, codes):
    return pl.pallas_call(
        pack_kernel,
        out_shape=(jax.ShapeDtypeStruct((512, 2 * WIDE), BF), jax.ShapeDtypeStruct((MSG, 2 * WIDE), BF)),
        in_specs=[SMEM, VMEM, VMEM, VMEM],
        out_specs=(VMEM, VMEM),
        scratch_shapes=[pltpu.VMEM((2, 512, WIDE), F32)],
        name="pack",
    )(place, x, g, codes)


def neighbour(offset):
    u, w, q = lax.axis_index("gx"), lax.axis_index("gy"), lax.axis_index("gz")
    nx, ny = lax.axis_size("gx"), lax.axis_size("gy")
    du, dv, dw = offset
    return ((u + du + nx) % nx, (w + dv + ny) % ny, 1 - q if dw else q)


def halo_copies(msg_ref, into_ref, send_sem, recv_sem):
    copies = []
    for slot, size, offset in message_plan():
        rows = pl.ds(slot_row(slot), size)
        copies.append(pltpu.make_async_remote_copy(
            src_ref=msg_ref.at[rows, :], dst_ref=into_ref.at[rows, :],
            send_sem=send_sem.at[slot], recv_sem=recv_sem.at[slot],
            device_id=neighbour(offset), device_id_type=MESH))
    return copies


def greet_neighbours(barrier):
    for _, _, offset in message_plan():
        pl.semaphore_signal(barrier, inc=1, device_id=neighbour(offset), device_id_type=MESH)


def exchange_kernel(msg_ref, out_ref, into, send_sem, recv_sem):
    barrier = pltpu.get_barrier_semaphore()
    greet_neighbours(barrier)
    pl.semaphore_wait(barrier, 17)
    copies = halo_copies(msg_ref, into, send_sem, recv_sem)
    for copy in copies:
        copy.start()
    for copy in copies:
        copy.wait()
    out_ref[...] = into[...]


def exchange(messages, number):
    return pl.pallas_call(
        exchange_kernel,
        out_shape=jax.ShapeDtypeStruct(messages.shape, messages.dtype),
        in_specs=[VMEM],
        out_specs=VMEM,
        scratch_shapes=[
            pltpu.VMEM(messages.shape, messages.dtype),
            pltpu.SemaphoreType.DMA((17,)), pltpu.SemaphoreType.DMA((17,))],
        compiler_params=pltpu.CompilerParams(collective_id=number, has_side_effects=True),
        name="exchange",
    )(messages)


def pick_messages(place_ref, into_ref):
    position = place_ref[0]
    a, b = position // 4, position // 2 % 2

    def take(start, size):
        return into_ref[pl.ds(pl.multiple_of(start, 16), size), :]

    return jnp.concatenate([
        take(a * 64, 64), take(128 + b * 64, 64), take(256, 64),
        take(320 + (2 * a + b) * 16, 16), take(384 + a * 16, 16), take(416 + b * 16, 16),
        take(448 + (2 * a + b) * 16, 16)], axis=0)


def halo_codes(place_ref, sender):
    position, u, w, q = place_ref[0], place_ref[2], place_ref[3], place_ref[4]
    nx, ny = place_ref[5], place_ref[6]
    own = (position // 4, position // 2 % 2, position % 2)
    theirs = (sender // 4, sender // 2 % 2, sender % 2)
    beyond = (u + 2 * own[0] - 1, w + 2 * own[1] - 1, q + 2 * own[2] - 1)
    sizes = (nx, ny, 2)
    r = lax.broadcasted_iota(jnp.int32, sender.shape, 1)
    face = r < 192
    t = jnp.where(face, r % 64, r % 16)
    high, low = t // 8, t % 8
    past = (
        (r < 64) | ((r >= 192) & (r < 224)) | (r >= 240),
        ((r >= 64) & (r < 128)) | ((r >= 192) & (r < 208)) | (r >= 224),
        ((r >= 128) & (r < 192)) | (r >= 208))
    index = (
        jnp.where(face, high, t),
        jnp.where(r < 64, high, jnp.where(face, low, t)),
        jnp.where(face, low, t))
    valid = face | (t < jnp.where(r < 240, 8, 1))
    spot = []
    for axis in range(3):
        far = 9 * own[axis]
        near = 9 - far
        same = theirs[axis] == own[axis]
        inner = jnp.where(same, 1 + index[axis], near)
        inner_ok = same | (index[axis] == 7 * own[axis])
        there = jnp.zeros_like(r) + beyond[axis]
        outer_ok = (theirs[axis] != own[axis]) & (there >= 0) & (there < sizes[axis])
        spot.append(jnp.where(past[axis], far, inner))
        valid = valid & ((past[axis] & outer_ok) | (jnp.logical_not(past[axis]) & inner_ok))
    return jnp.where(valid, (spot[0] * 10 + spot[1]) * 16 + spot[2], -1)


def build_patch(place_ref, rows, picked, code, level_ref, all_ref, width):
    n = lax.broadcasted_iota(jnp.int32, (800, 256), 0)
    target = n // 8 * 16 + n % 8
    level = lax.broadcasted_iota(jnp.int32, rows.shape, 0) % 8
    for dz in (0, 1, 2):
        pick = jnp.where(target + dz == code, 1.0, 0.0).astype(BF)
        halo = jnp.dot(pick, picked, preferred_element_type=F32)
        if dz == 0:
            mine = jnp.where(level == 0, 0.0, pltpu.roll(rows, 1, 0))
        elif dz == 1:
            mine = rows
        else:
            mine = jnp.where(level == 7, 0.0, pltpu.roll(rows, 511, 0))
        level_ref[...] = halo
        for i in range(8):
            spot = pl.ds(((i + 1) * 10 + 1) * 8, 64)
            level_ref[spot, :] = level_ref[spot, :] + mine[64 * i : 64 * i + 64]
        for dy in (0, 1, 2):
            tap = dy * 3 + dz
            for x in range(10):
                all_ref[pl.ds(64 * x, 64), pl.ds(tap * width, width)] = (
                    level_ref[pl.ds((x * 10 + dy) * 8, 64), :].astype(BF))


def pack_grads(blocks, store):
    lane = lax.broadcasted_iota(jnp.int32, (C, WIDE), 1)
    for group in range(13):
        last = blocks(4 * group + 3)
        for t in range(3):
            shifted = pltpu.roll(last, C - 32 * t, 1)
            store(3 * group + t, jnp.where(lane < C, blocks(4 * group + t), shifted))
    store(39, blocks(52))
    store(40, blocks(53))


def unpack_grads(load, store):
    lane = lax.broadcasted_iota(jnp.int32, (C, WIDE), 1)
    for group in range(13):
        last = jnp.zeros((C, WIDE), F32)
        for t in range(3):
            tile = load(3 * group + t)
            store(4 * group + t, tile)
            moved = pltpu.roll(tile, 32 + 32 * t, 1)
            last = jnp.where((lane >= 32 * t) & (lane < 32 * t + 32), moved, last)
        store(4 * group + 3, last)
    store(52, load(39))
    store(53, load(40))


def forward_kernel(scale, place_ref, rows_ref, into_ref, weight_ref, data_ref, delta_ref, msg_ref, code_out,
                   level_ref, all_ref, grads_ref, wide_ref):
    q = place_ref[4]
    rows = rows_ref[...].astype(F32)
    picked = pick_messages(place_ref, into_ref)
    sender = picked[:, :WIDE].astype(F32).T[C : C + 8].astype(jnp.int32)
    code = halo_codes(place_ref, sender)[:1]
    code_out[...] = jnp.broadcast_to(code, (8, 256))
    build_patch(place_ref, rows, picked, code, level_ref, all_ref, 2 * WIDE)
    acc = jnp.zeros((512, 2 * WIDE), F32)
    for dx in (0, 1, 2):
        acc = acc + jnp.dot(all_ref[pl.ds(64 * dx, 512), :], weight_ref[dx], preferred_element_type=F32)
    pre, back = acc[:, :WIDE], acc[:, WIDE:]
    mask = jnp.broadcast_to(rows[:, C + 1 : C + 2], (512, WIDE))
    sigma = jax.nn.sigmoid(pre)
    hidden = pre * sigma * mask
    delta = (back * sigma * (1.0 + pre * (1.0 - sigma)) * mask).astype(BF)
    delta_ref[...] = delta
    wide_ref[0] = delta.astype(F32)
    pack_messages(wide_ref, msg_ref, q)
    both = jnp.concatenate([hidden.T, delta.astype(F32).T], axis=0).astype(BF)
    for dx in (0, 1, 2):
        grads_ref[dx] = jnp.dot(both, all_ref[pl.ds(64 * dx, 512), :], preferred_element_type=F32)

    def blocks(number):
        if number < 27:
            return grads_ref[number // 9, WIDE : WIDE + C, pl.ds(number % 9 * 2 * WIDE, WIDE)] * scale
        turned = 53 - number
        return grads_ref[turned // 9, 0:C, pl.ds(turned % 9 * 2 * WIDE + WIDE, WIDE)] * scale

    def store(tile, value):
        data_ref[pl.ds(tile * C, C), :] = value

    pack_grads(blocks, store)
    data_ref[pl.ds(41 * C, 4096 - 41 * C), :] = jnp.zeros((4096 - 41 * C, WIDE), F32)


def forward(scale, place, rows, into, weights):
    return pl.pallas_call(
        functools.partial(forward_kernel, scale),
        out_shape=(
            jax.ShapeDtypeStruct((4096, WIDE), F32), jax.ShapeDtypeStruct((512, WIDE), BF),
            jax.ShapeDtypeStruct((MSG, WIDE), BF), jax.ShapeDtypeStruct((8, 256), jnp.int32)),
        in_specs=[SMEM, VMEM, VMEM, VMEM],
        out_specs=(VMEM,) * 4,
        scratch_shapes=[
            pltpu.VMEM((800, 2 * WIDE), F32), pltpu.VMEM((640, 9 * 2 * WIDE), BF),
            pltpu.VMEM((3, 2 * WIDE, 9 * 2 * WIDE), F32), pltpu.VMEM((1, 512, WIDE), F32)],
        compiler_params=pltpu.CompilerParams(vmem_limit_bytes=50 * 2 ** 20),
        name="forward",
    )(place, rows, into, weights)


def backward_kernel(place_ref, rows_ref, code_ref, delta_ref, into_ref, weight_ref, sum_ref,
                    out_ref, first_ref, second_ref, level_ref, all_ref):
    picked = pick_messages(place_ref, into_ref)
    build_patch(place_ref, delta_ref[...].astype(F32), picked, code_ref[0:1, :], level_ref, all_ref, WIDE)
    acc = rows_ref[:, WIDE:].astype(F32)
    for dx in (0, 1, 2):
        acc = acc + jnp.dot(all_ref[pl.ds(64 * dx, 512), :], weight_ref[dx], preferred_element_type=F32)
    mask = jnp.broadcast_to(rows_ref[:, :WIDE].astype(F32)[:, C + 1 : C + 2], (512, WIDE))
    out_ref[...] = (acc * mask).T[:C].astype(BF)

    def load(tile):
        return sum_ref[pl.ds(tile * C, C), :].astype(F32)

    def store(number, value):
        if number < 27:
            first_ref[number] = value.T[:C]
        else:
            second_ref[number - 27] = value[:, :C]

    unpack_grads(load, store)


def backward(place, rows, code, delta, into, weights, summed):
    return pl.pallas_call(
        backward_kernel,
        out_shape=(
            jax.ShapeDtypeStruct((C, 512), BF),
            jax.ShapeDtypeStruct((27, C, C), F32), jax.ShapeDtypeStruct((27, C, C), F32)),
        in_specs=[SMEM] + [VMEM] * 6,
        out_specs=(VMEM,) * 3,
        scratch_shapes=[pltpu.VMEM((800, WIDE), F32), pltpu.VMEM((640, 9 * WIDE), BF)],
        compiler_params=pltpu.CompilerParams(vmem_limit_bytes=50 * 2 ** 20),
        name="backward",
    )(place, rows, code, delta, into, weights, summed)


def both_weights(first, second):
    gap = WIDE - C
    turned = second[::-1].transpose(0, 2, 1)
    top = jnp.pad(first, ((0, 0), (0, gap), (0, WIDE + gap)))
    bottom = jnp.pad(turned, ((0, 0), (0, gap), (WIDE, gap)))
    return jnp.concatenate([top, bottom], axis=1).reshape(3, 9 * 2 * WIDE, 2 * WIDE)


def back_weights(first):
    gap = WIDE - C
    turned = first[::-1].transpose(0, 2, 1)
    return jnp.pad(turned, ((0, 0), (0, gap), (0, gap))).reshape(3, 9 * WIDE, WIDE)


ROWS = 4096
HALF = ROWS // 2
PART = HALF // 16
CELL = PART // 16


def reduce_kernel(d_ref, out_ref, half_out, half_in, total, plane_out, plane_in, cell_src,
                  line_in, line_all, own_part, gathered, pair_sem, plane_send, plane_recv,
                  line_send, line_recv, line_send2, line_recv2, plane_send2, plane_recv2):
    u = lax.axis_index("gx")
    w = lax.axis_index("gy")
    q = lax.axis_index("gz")
    core = w % 2
    y = w // 2 % 4
    x = q * 2 + w // 8
    chip = x * 4 + y
    mate = (u, w + 1 - 2 * core, q)

    def plane_peer(t):
        px = (x + t // 4) % 4
        py = (y + t % 4) % 4
        return px * 4 + py, (u, ((px % 2) * 4 + py) * 2 + core, px // 2)

    def line_peer(t):
        z = (u + t) % 16
        return z, (z, w, q)

    barrier = pltpu.get_barrier_semaphore()
    pl.semaphore_signal(barrier, inc=1, device_id=mate, device_id_type=MESH)

    def greet(t, carry):
        pl.semaphore_signal(barrier, inc=1, device_id=plane_peer(t)[1], device_id_type=MESH)
        pl.semaphore_signal(barrier, inc=1, device_id=line_peer(t)[1], device_id_type=MESH)
        return carry

    lax.fori_loop(1, 16, greet, 0)
    pl.semaphore_wait(barrier, 31)

    other = pl.multiple_of((1 - core) * HALF, HALF)
    own = pl.multiple_of(core * HALF, HALF)
    half_out[...] = d_ref[pl.ds(other, HALF), :].astype(jnp.bfloat16)
    swap = pltpu.make_async_remote_copy(
        src_ref=half_out, dst_ref=half_in, send_sem=pair_sem.at[0], recv_sem=pair_sem.at[1],
        device_id=mate, device_id_type=MESH)
    swap.start()
    swap.wait()
    total[...] = d_ref[pl.ds(own, HALF), :] + half_in[...].astype(jnp.float32)
    plane_out[...] = total[...].astype(jnp.bfloat16)

    def plane_copy(t):
        there, device = plane_peer(t)
        return pltpu.make_async_remote_copy(
            src_ref=plane_out.at[pl.ds(pl.multiple_of(there * PART, PART), PART), :],
            dst_ref=plane_in.at[t], send_sem=plane_send.at[t], recv_sem=plane_recv.at[t],
            device_id=device, device_id_type=MESH)

    def plane_start(t, carry):
        plane_copy(t).start()
        return carry

    lax.fori_loop(1, 16, plane_start, 0)
    mine = pl.multiple_of(chip * PART, PART)

    def plane_add(t, acc):
        plane_copy(t).wait_recv()
        return acc + plane_in[t].astype(jnp.float32)

    cell_src[...] = lax.fori_loop(1, 16, plane_add, total[pl.ds(mine, PART), :])

    def line_copy(t):
        there, device = line_peer(t)
        return pltpu.make_async_remote_copy(
            src_ref=cell_src.at[pl.ds(pl.multiple_of(there * CELL, CELL), CELL), :],
            dst_ref=line_in.at[t], send_sem=line_send.at[t], recv_sem=line_recv.at[t],
            device_id=device, device_id_type=MESH)

    def line_start(t, carry):
        line_copy(t).start()
        return carry

    lax.fori_loop(1, 16, line_start, 0)
    here = pl.multiple_of(u * CELL, CELL)

    def line_add(t, acc):
        line_copy(t).wait_recv()
        return acc + line_in[t]

    line_all[pl.ds(here, CELL), :] = lax.fori_loop(1, 16, line_add, cell_src[pl.ds(here, CELL), :])

    def spread_copy(t):
        there, device = line_peer(t)
        return pltpu.make_async_remote_copy(
            src_ref=line_all.at[pl.ds(here, CELL), :],
            dst_ref=line_all.at[pl.ds(here, CELL), :], send_sem=line_send2.at[t], recv_sem=line_recv2.at[t],
            device_id=device, device_id_type=MESH)

    def arrive_copy(t):
        z = (u - t + 16) % 16
        rows = pl.ds(pl.multiple_of(z * CELL, CELL), CELL)
        return pltpu.make_async_remote_copy(
            src_ref=line_all.at[rows, :],
            dst_ref=line_all.at[rows, :], send_sem=line_send2.at[t], recv_sem=line_recv2.at[t],
            device_id=line_peer(t)[1], device_id_type=MESH)

    def spread_start(t, carry):
        spread_copy(t).start()
        return carry

    def spread_wait(t, carry):
        arrive_copy(t).wait_recv()
        return carry

    lax.fori_loop(1, 16, spread_start, 0)
    lax.fori_loop(1, 16, spread_wait, 0)
    own_part[...] = line_all[...].astype(jnp.bfloat16)

    place = pl.multiple_of(own + mine, PART)
    gathered[pl.ds(place, PART), :] = own_part[...]

    def back_copy(t):
        there, device = plane_peer(t)
        return pltpu.make_async_remote_copy(
            src_ref=own_part,
            dst_ref=gathered.at[pl.ds(place, PART), :], send_sem=plane_send2.at[t], recv_sem=plane_recv2.at[t],
            device_id=device, device_id_type=MESH)

    def back_arrive(t):
        px = (x - t // 4 + 4) % 4
        py = (y - t % 4 + 4) % 4
        rows = pl.ds(pl.multiple_of(own + (px * 4 + py) * PART, PART), PART)
        return pltpu.make_async_remote_copy(
            src_ref=own_part,
            dst_ref=gathered.at[rows, :], send_sem=plane_send2.at[t], recv_sem=plane_recv2.at[t],
            device_id=plane_peer(t)[1], device_id_type=MESH)

    def back_start(t, carry):
        back_copy(t).start()
        return carry

    def back_wait(t, carry):
        back_arrive(t).wait_recv()
        return carry

    lax.fori_loop(1, 16, back_start, 0)
    lax.fori_loop(1, 16, back_wait, 0)

    join = pltpu.make_async_remote_copy(
        src_ref=gathered.at[pl.ds(own, HALF), :], dst_ref=gathered.at[pl.ds(own, HALF), :],
        send_sem=pair_sem.at[2], recv_sem=pair_sem.at[3],
        device_id=mate, device_id_type=MESH)
    join.start()

    def drain(t, carry):
        plane_copy(t).wait_send()
        line_copy(t).wait_send()
        spread_copy(t).wait_send()
        back_copy(t).wait_send()
        return carry

    lax.fori_loop(1, 16, drain, 0)
    join.wait_send()
    arrive = pltpu.make_async_remote_copy(
        src_ref=gathered.at[pl.ds(other, HALF), :], dst_ref=gathered.at[pl.ds(other, HALF), :],
        send_sem=pair_sem.at[2], recv_sem=pair_sem.at[3],
        device_id=mate, device_id_type=MESH)
    arrive.wait_recv()
    out_ref[...] = gathered[...].astype(jnp.float32)


def all_sum(data):
    sems = lambda n: pltpu.SemaphoreType.DMA((n,))
    return pl.pallas_call(
        reduce_kernel,
        out_shape=jax.ShapeDtypeStruct((ROWS, 128), jnp.float32),
        in_specs=[pl.BlockSpec(memory_space=pltpu.VMEM)],
        out_specs=pl.BlockSpec(memory_space=pltpu.VMEM),
        scratch_shapes=[
            pltpu.VMEM((HALF, 128), jnp.bfloat16),
            pltpu.VMEM((HALF, 128), jnp.bfloat16),
            pltpu.VMEM((HALF, 128), jnp.float32),
            pltpu.VMEM((HALF, 128), jnp.bfloat16),
            pltpu.VMEM((16, PART, 128), jnp.bfloat16),
            pltpu.VMEM((PART, 128), jnp.float32),
            pltpu.VMEM((16, CELL, 128), jnp.float32),
            pltpu.VMEM((PART, 128), jnp.float32),
            pltpu.VMEM((PART, 128), jnp.bfloat16),
            pltpu.VMEM((ROWS, 128), jnp.bfloat16),
            sems(4), sems(16), sems(16), sems(16), sems(16), sems(16), sems(16), sems(16), sems(16),
        ],
        compiler_params=pltpu.CompilerParams(
            collective_id=3, has_side_effects=True, vmem_limit_bytes=32 * 2 ** 20),
        name="all_sum",
    )(data)


def shards(features, cotangent, first_weight, second_weight, slot_position, brick_count, column_code):
    nx, ny, nz = (lax.axis_size(axis) for axis in ("gx", "gy", "gz"))
    scale = float((nx * ny * nz) ** -0.5 / 8.0)
    axes = [lax.axis_index(axis) for axis in ("gx", "gy", "gz")]
    place = jnp.stack([slot_position.reshape(()), brick_count.reshape(()), *axes, nx, ny]).astype(jnp.int32)
    rows, messages = pack(place, features.reshape(C, 512), cotangent.reshape(C, 512), column_code.reshape(1, 64))
    into = exchange(messages, 1)
    data, delta, delta_messages, code = forward(scale, place, rows, into, both_weights(first_weight, second_weight))
    delta_into = exchange(delta_messages, 2)
    summed = all_sum(data)
    grad_input, first_grad, second_grad = backward(
        place, rows, code, delta, delta_into, back_weights(first_weight), summed)
    return grad_input.reshape(1, 1, 1, 1, C, 512), first_grad, second_grad


def solution(mesh):
    placed = (
        P("gx", "gy", "gz", None, None, None),
        P("gx", "gy", "gz", None, None, None),
        P(),
        P(),
        P("gx", "gy", "gz", None),
        P("gx", "gy", "gz"),
        P("gx", "gy", "gz", None, None),
    )
    return jax.shard_map(
        shards,
        mesh=mesh,
        in_specs=placed,
        out_specs=(P("gx", "gy", "gz", None, None, None), P(), P()),
        check_vma=False,
    )
```

```python
import functools

import jax
import jax.numpy as jnp
from jax import lax
from jax.experimental import pallas as pl
from jax.experimental.pallas import tpu as pltpu
from jax.sharding import PartitionSpec as P

MESH = pl.DeviceIdType.MESH
VMEM = pl.BlockSpec(memory_space=pltpu.VMEM)
SMEM = pl.BlockSpec(memory_space=pltpu.SMEM)
C = 96
WIDE = 128
MSG = 512
BF = jnp.bfloat16
F32 = jnp.float32


def message_plan():
    plan = []
    for ix in (0, 1):
        plan.append((ix, 64, (1 - 2 * ix, 0, 0)))
    for iy in (0, 1):
        plan.append((2 + iy, 64, (0, 1 - 2 * iy, 0)))
    plan.append((4, 64, (0, 0, 1)))
    for ix in (0, 1):
        for iy in (0, 1):
            plan.append((5 + 2 * ix + iy, 16, (1 - 2 * ix, 1 - 2 * iy, 0)))
    for ix in (0, 1):
        plan.append((9 + ix, 16, (1 - 2 * ix, 0, 1)))
    for iy in (0, 1):
        plan.append((11 + iy, 16, (0, 1 - 2 * iy, 1)))
    for ix in (0, 1):
        for iy in (0, 1):
            plan.append((13 + 2 * ix + iy, 16, (1 - 2 * ix, 1 - 2 * iy, 1)))
    return plan


def slot_row(slot):
    return slot * 64 if slot < 5 else 320 + (slot - 5) * 16


def pack_messages(wide_ref, msg_ref, q):
    blank = jnp.zeros((8, WIDE), F32)
    only = lax.broadcasted_iota(jnp.int32, (8, WIDE), 0) == 0
    for part in range(wide_ref.shape[0]):

        def rows(*spot, **stride):
            return wide_ref[part, pl.ds(*spot, **stride), :]

        def put(slot, value):
            start = slot_row(slot)
            msg_ref[pl.ds(start, value.shape[0]), pl.ds(part * WIDE, WIDE)] = value.astype(BF)

        def side(low, high):
            return jnp.where(q == 0, high, low)

        for ix in (0, 1):
            put(ix, rows(448 * (1 - ix), 64))
        for iy in (0, 1):
            edge = [rows(64 * i + 56 * (1 - iy), 8) for i in range(8)]
            put(2 + iy, jnp.concatenate(edge, axis=0))
        put(4, side(rows(0, 64, stride=8), rows(7, 64, stride=8)))
        for ix in (0, 1):
            x0 = 448 * (1 - ix)
            for iy in (0, 1):
                column = rows(x0 + 56 * (1 - iy), 8)
                put(5 + 2 * ix + iy, jnp.concatenate([column, blank], axis=0))
                corner = side(column, pltpu.roll(column, 1, 0))
                put(13 + 2 * ix + iy, jnp.concatenate([jnp.where(only, corner, 0.0), blank], axis=0))
            line = side(rows(x0, 8, stride=8), rows(x0 + 7, 8, stride=8))
            put(9 + ix, jnp.concatenate([line, blank], axis=0))
        for iy in (0, 1):
            y0 = 56 * (1 - iy)
            line = side(rows(y0, 8, stride=64), rows(y0 + 7, 8, stride=64))
            put(11 + iy, jnp.concatenate([line, blank], axis=0))


def pack_rows(position, count, x_ref, g_ref, code_ref, wide_ref, rows_ref):
    column = lax.broadcasted_iota(jnp.int32, (64, 512), 0)
    voxel = lax.broadcasted_iota(jnp.int32, (64, 512), 1)
    spread = jnp.where(column == voxel // 8, 1.0, 0.0).astype(BF)
    codes = jnp.broadcast_to(code_ref[...].astype(F32), (16, 64)).astype(BF)
    code = jnp.dot(codes, spread, preferred_element_type=F32).astype(jnp.int32)[:8]
    low = code // 8
    level = lax.broadcasted_iota(jnp.int32, (8, 512), 1) % 8
    live = (level >= low) & (level <= low + code % 8) & (count > 0)
    mask = jnp.where(live, 1.0, 0.0)
    first = lax.broadcasted_iota(jnp.int32, (8, 512), 0)
    place = jnp.where(first == 0, position.astype(F32), jnp.where(first == 1, mask, 0.0))
    blank = jnp.zeros((24, 512), F32)
    inside = jnp.broadcast_to(mask[:1], (C, 512)) > 0.0
    x = jnp.where(inside, x_ref[...].astype(F32), 0.0)
    g = jnp.where(inside, g_ref[...].astype(F32), 0.0)
    wide_ref[0] = jnp.concatenate([x, place, blank], axis=0).T
    wide_ref[1] = jnp.concatenate([g, jnp.zeros((32, 512), F32)], axis=0).T
    rows_ref[:, :WIDE] = wide_ref[0].astype(BF)
    rows_ref[:, WIDE:] = wide_ref[1].astype(BF)


def neighbour(offset):
    u, w, q = lax.axis_index("gx"), lax.axis_index("gy"), lax.axis_index("gz")
    nx, ny = lax.axis_size("gx"), lax.axis_size("gy")
    du, dv, dw = offset
    return ((u + du + nx) % nx, (w + dv + ny) % ny, 1 - q if dw else q)


def halo_copies(msg_ref, into_ref, send_sem, recv_sem):
    copies = []
    for slot, size, offset in message_plan():
        rows = pl.ds(slot_row(slot), size)
        copies.append(pltpu.make_async_remote_copy(
            src_ref=msg_ref.at[rows, :], dst_ref=into_ref.at[rows, :],
            send_sem=send_sem.at[slot], recv_sem=recv_sem.at[slot],
            device_id=neighbour(offset), device_id_type=MESH))
    return copies


def greet_neighbours(barrier):
    for _, _, offset in message_plan():
        pl.semaphore_signal(barrier, inc=1, device_id=neighbour(offset), device_id_type=MESH)


def pick_messages(position, into_ref):
    def bit(size, divisor):
        return jnp.zeros((size, into_ref.shape[1]), jnp.int32) + position // divisor % 2 == 0

    def at(slot):
        return into_ref[pl.ds(slot_row(slot), 64 if slot < 5 else 16), :].astype(F32)

    def two(slot, divisor):
        low = at(slot)
        return jnp.where(bit(low.shape[0], divisor), low, at(slot + 1))

    def four(slot):
        return jnp.where(bit(16, 4), two(slot, 2), two(slot + 2, 2))

    return jnp.concatenate(
        [two(0, 4), two(2, 2), at(4), four(5), two(9, 4), two(11, 2), four(13)], axis=0).astype(BF)


def halo_codes(position, sender):
    u, w, q = (lax.axis_index(axis) for axis in ("gx", "gy", "gz"))
    nx, ny = lax.axis_size("gx"), lax.axis_size("gy")
    own = (position // 4, position // 2 % 2, position % 2)
    theirs = (sender // 4, sender // 2 % 2, sender % 2)
    beyond = (u + 2 * own[0] - 1, w + 2 * own[1] - 1, q + 2 * own[2] - 1)
    sizes = (nx, ny, 2)
    r = lax.broadcasted_iota(jnp.int32, sender.shape, 1)
    face = r < 192
    t = jnp.where(face, r % 64, r % 16)
    high, low = t // 8, t % 8
    past = (
        (r < 64) | ((r >= 192) & (r < 224)) | (r >= 240),
        ((r >= 64) & (r < 128)) | ((r >= 192) & (r < 208)) | (r >= 224),
        ((r >= 128) & (r < 192)) | (r >= 208))
    index = (
        jnp.where(face, high, t),
        jnp.where(r < 64, high, jnp.where(face, low, t)),
        jnp.where(face, low, t))
    valid = face | (t < jnp.where(r < 240, 8, 1))
    spot = []
    for axis in range(3):
        far = 9 * own[axis]
        near = 9 - far
        same = theirs[axis] == own[axis]
        inner = jnp.where(same, 1 + index[axis], near)
        inner_ok = same | (index[axis] == 7 * own[axis])
        there = jnp.zeros_like(r) + beyond[axis]
        outer_ok = (theirs[axis] != own[axis]) & (there >= 0) & (there < sizes[axis])
        spot.append(jnp.where(past[axis], far, inner))
        valid = valid & ((past[axis] & outer_ok) | (jnp.logical_not(past[axis]) & inner_ok))
    return jnp.where(valid, (spot[0] * 10 + spot[1]) * 16 + spot[2], -1)


def build_patch(rows, picked, code, level_ref, all_ref, width):
    n = lax.broadcasted_iota(jnp.int32, (800, 256), 0)
    target = n // 8 * 16 + n % 8
    level = lax.broadcasted_iota(jnp.int32, rows.shape, 0) % 8
    for dz in (0, 1, 2):
        pick = jnp.where(target + dz == code, 1.0, 0.0).astype(BF)
        halo = jnp.dot(pick, picked, preferred_element_type=F32)
        if dz == 0:
            mine = jnp.where(level == 0, 0.0, pltpu.roll(rows, 1, 0))
        elif dz == 1:
            mine = rows
        else:
            mine = jnp.where(level == 7, 0.0, pltpu.roll(rows, 511, 0))
        level_ref[...] = halo
        for i in range(8):
            spot = pl.ds(((i + 1) * 10 + 1) * 8, 64)
            level_ref[spot, :] = level_ref[spot, :] + mine[64 * i : 64 * i + 64]
        for dy in (0, 1, 2):
            tap = dy * 3 + dz
            for x in range(10):
                all_ref[pl.ds(64 * x, 64), pl.ds(tap * width, width)] = (
                    level_ref[pl.ds((x * 10 + dy) * 8, 64), :].astype(BF))


def pack_grads(block, store):
    lane = lax.broadcasted_iota(jnp.int32, (C, WIDE), 1)
    for group in range(6):
        last = block(4 * group + 3)
        for t in range(3):
            shifted = pltpu.roll(last, C - 32 * t, 1)
            store(3 * group + t, jnp.where(lane < C, block(4 * group + t), shifted))
    for t in range(3):
        store(18 + t, block(24 + t))


def unpack_grads(load, store):
    lane = lax.broadcasted_iota(jnp.int32, (C, WIDE), 1)
    for group in range(6):
        last = jnp.zeros((C, WIDE), F32)
        for t in range(3):
            tile = load(3 * group + t)
            store(4 * group + t, tile)
            moved = pltpu.roll(tile, 32 + 32 * t, 1)
            last = jnp.where((lane >= 32 * t) & (lane < 32 * t + 32), moved, last)
        store(4 * group + 3, last)
    for t in range(3):
        store(24 + t, load(18 + t))


def square(block):
    gap = WIDE - C
    wide = jnp.concatenate([block.astype(F32), jnp.zeros((C, gap), F32)], axis=1)
    return jnp.concatenate([wide, jnp.zeros((gap, WIDE), F32)], axis=0)


def lay_weights(first_ref, second_ref, weight_ref):
    none = jnp.zeros((WIDE, WIDE), BF)

    def step(k, carry):
        top = pl.ds(pl.multiple_of(k % 9 * 2 * WIDE, WIDE), WIDE)
        bottom = pl.ds(pl.multiple_of(k % 9 * 2 * WIDE + WIDE, WIDE), WIDE)
        weight_ref[k // 9, top, :WIDE] = square(first_ref[k]).astype(BF)
        weight_ref[k // 9, top, WIDE:] = none
        weight_ref[k // 9, bottom, :WIDE] = none
        weight_ref[k // 9, bottom, WIDE:] = square(second_ref[26 - k]).T.astype(BF)
        return carry

    lax.fori_loop(0, 27, step, 0)


def lay_back_weights(first_ref, weight_ref):
    def step(k, carry):
        rows = pl.ds(pl.multiple_of(k % 9 * WIDE, WIDE), WIDE)
        weight_ref[k // 9, rows, :] = square(first_ref[26 - k]).T.astype(BF)
        return carry

    lax.fori_loop(0, 27, step, 0)


ROWS = 4096
HALF = ROWS // 2
PART = HALF // 16
CELL = PART // 16


def places():
    u = lax.axis_index("gx")
    w = lax.axis_index("gy")
    q = lax.axis_index("gz")
    core = w % 2
    y = w // 2 % 4
    x = q * 2 + w // 8
    mate = (u, w + 1 - 2 * core, q)

    def plane_peer(t):
        px = (x + t // 4) % 4
        py = (y + t % 4) % 4
        return px * 4 + py, (u, ((px % 2) * 4 + py) * 2 + core, px // 2)

    def line_peer(t):
        z = (u + t) % 16
        return z, (z, w, q)
    return u, w, q, core, x, y, x * 4 + y, mate, plane_peer, line_peer


def greet_sharers(barrier):
    u, w, q, core, x, y, chip, mate, plane_peer, line_peer = places()
    pl.semaphore_signal(barrier, inc=1, device_id=mate, device_id_type=MESH)

    def greet(t, carry):
        pl.semaphore_signal(barrier, inc=1, device_id=plane_peer(t)[1], device_id_type=MESH)
        pl.semaphore_signal(barrier, inc=1, device_id=line_peer(t)[1], device_id_type=MESH)
        return carry

    lax.fori_loop(1, 16, greet, 0)


def all_sum(between, data_ref, sum_ref, gathered, half_out, half_in, total, plane_out, plane_in,
            cell_src, line_in, line_all, own_part, pair_sem, plane_send, plane_recv,
            line_send, line_recv, line_send2, line_recv2, plane_send2, plane_recv2):
    u, w, q, core, x, y, chip, mate, plane_peer, line_peer = places()
    other = pl.multiple_of((1 - core) * HALF, HALF)
    own = pl.multiple_of(core * HALF, HALF)
    half_out[...] = data_ref[pl.ds(other, HALF), :].astype(jnp.bfloat16)
    swap = pltpu.make_async_remote_copy(
        src_ref=half_out, dst_ref=half_in, send_sem=pair_sem.at[0], recv_sem=pair_sem.at[1],
        device_id=mate, device_id_type=MESH)
    swap.start()
    swap.wait()
    total[...] = data_ref[pl.ds(own, HALF), :] + half_in[...].astype(jnp.float32)
    plane_out[...] = total[...].astype(jnp.bfloat16)

    def plane_copy(t):
        there, device = plane_peer(t)
        return pltpu.make_async_remote_copy(
            src_ref=plane_out.at[pl.ds(pl.multiple_of(there * PART, PART), PART), :],
            dst_ref=plane_in.at[t], send_sem=plane_send.at[t], recv_sem=plane_recv.at[t],
            device_id=device, device_id_type=MESH)

    def plane_start(t, carry):
        plane_copy(t).start()
        return carry

    lax.fori_loop(1, 16, plane_start, 0)
    between()
    mine = pl.multiple_of(chip * PART, PART)

    def plane_add(t, acc):
        plane_copy(t).wait_recv()
        return acc + plane_in[t].astype(jnp.float32)

    cell_src[...] = lax.fori_loop(1, 16, plane_add, total[pl.ds(mine, PART), :])

    def line_copy(t):
        there, device = line_peer(t)
        return pltpu.make_async_remote_copy(
            src_ref=cell_src.at[pl.ds(pl.multiple_of(there * CELL, CELL), CELL), :],
            dst_ref=line_in.at[t], send_sem=line_send.at[t], recv_sem=line_recv.at[t],
            device_id=device, device_id_type=MESH)

    def line_start(t, carry):
        line_copy(t).start()
        return carry

    lax.fori_loop(1, 16, line_start, 0)
    here = pl.multiple_of(u * CELL, CELL)

    def line_add(t, acc):
        line_copy(t).wait_recv()
        return acc + line_in[t]

    line_all[pl.ds(here, CELL), :] = lax.fori_loop(1, 16, line_add, cell_src[pl.ds(here, CELL), :])

    def spread_copy(t):
        there, device = line_peer(t)
        return pltpu.make_async_remote_copy(
            src_ref=line_all.at[pl.ds(here, CELL), :],
            dst_ref=line_all.at[pl.ds(here, CELL), :], send_sem=line_send2.at[t], recv_sem=line_recv2.at[t],
            device_id=device, device_id_type=MESH)

    def arrive_copy(t):
        z = (u - t + 16) % 16
        rows = pl.ds(pl.multiple_of(z * CELL, CELL), CELL)
        return pltpu.make_async_remote_copy(
            src_ref=line_all.at[rows, :],
            dst_ref=line_all.at[rows, :], send_sem=line_send2.at[t], recv_sem=line_recv2.at[t],
            device_id=line_peer(t)[1], device_id_type=MESH)

    def spread_start(t, carry):
        spread_copy(t).start()
        return carry

    def spread_wait(t, carry):
        arrive_copy(t).wait_recv()
        return carry

    lax.fori_loop(1, 16, spread_start, 0)
    lax.fori_loop(1, 16, spread_wait, 0)
    own_part[...] = line_all[...].astype(jnp.bfloat16)

    place = pl.multiple_of(own + mine, PART)
    gathered[pl.ds(place, PART), :] = own_part[...]

    def back_copy(t):
        there, device = plane_peer(t)
        return pltpu.make_async_remote_copy(
            src_ref=own_part,
            dst_ref=gathered.at[pl.ds(place, PART), :], send_sem=plane_send2.at[t], recv_sem=plane_recv2.at[t],
            device_id=device, device_id_type=MESH)

    def back_arrive(t):
        px = (x - t // 4 + 4) % 4
        py = (y - t % 4 + 4) % 4
        rows = pl.ds(pl.multiple_of(own + (px * 4 + py) * PART, PART), PART)
        return pltpu.make_async_remote_copy(
            src_ref=own_part,
            dst_ref=gathered.at[rows, :], send_sem=plane_send2.at[t], recv_sem=plane_recv2.at[t],
            device_id=plane_peer(t)[1], device_id_type=MESH)

    def back_start(t, carry):
        back_copy(t).start()
        return carry

    def back_wait(t, carry):
        back_arrive(t).wait_recv()
        return carry

    lax.fori_loop(1, 16, back_start, 0)
    lax.fori_loop(1, 16, back_wait, 0)

    join = pltpu.make_async_remote_copy(
        src_ref=gathered.at[pl.ds(own, HALF), :], dst_ref=gathered.at[pl.ds(own, HALF), :],
        send_sem=pair_sem.at[2], recv_sem=pair_sem.at[3],
        device_id=mate, device_id_type=MESH)
    join.start()

    def drain(t, carry):
        plane_copy(t).wait_send()
        line_copy(t).wait_send()
        spread_copy(t).wait_send()
        back_copy(t).wait_send()
        return carry

    lax.fori_loop(1, 16, drain, 0)
    join.wait_send()
    arrive = pltpu.make_async_remote_copy(
        src_ref=gathered.at[pl.ds(other, HALF), :], dst_ref=gathered.at[pl.ds(other, HALF), :],
        send_sem=pair_sem.at[2], recv_sem=pair_sem.at[3],
        device_id=mate, device_id_type=MESH)
    arrive.wait_recv()
    sum_ref[...] = gathered[...]


def whole_kernel(scale, position_ref, count_ref, x_ref, g_ref, code_ref, first_ref, second_ref,
                 out_ref, sum_ref, wide_ref, rows_ref, msg_ref, into_ref, back_msg_ref, back_into_ref,
                 weight_ref, back_weight_ref, level_ref, all_ref, back_level_ref, back_all_ref,
                 grads_ref, data_ref, delta_ref, send_sem, recv_sem, back_send_sem, back_recv_sem, *reduce_refs):
    q = lax.axis_index("gz")
    position = position_ref[0]
    barrier = pltpu.get_barrier_semaphore()
    greet_neighbours(barrier)
    greet_sharers(barrier)

    pack_rows(position, count_ref[0], x_ref, g_ref, code_ref, wide_ref, rows_ref)
    pack_messages(wide_ref, msg_ref, q)
    pl.semaphore_wait(barrier, 17 + 31)
    copies = halo_copies(msg_ref, into_ref, send_sem, recv_sem)
    for copy in copies:
        copy.start()
    lay_weights(first_ref, second_ref, weight_ref)
    for copy in copies:
        copy.wait()

    rows = rows_ref[...].astype(F32)
    picked = pick_messages(position, into_ref)
    sender = picked[:, :WIDE].astype(F32).T[C : C + 8].astype(jnp.int32)
    code = halo_codes(position, sender)[:1]
    build_patch(rows, picked, code, level_ref, all_ref, 2 * WIDE)
    acc = jnp.zeros((512, 2 * WIDE), F32)
    for dx in (0, 1, 2):
        acc = acc + jnp.dot(all_ref[pl.ds(64 * dx, 512), :], weight_ref[dx], preferred_element_type=F32)
    pre, back = acc[:, :WIDE], acc[:, WIDE:]
    mask = jnp.broadcast_to(rows[:, C + 1 : C + 2], (512, WIDE))
    sigma = jax.nn.sigmoid(pre)
    hidden = pre * sigma * mask
    delta = (back * sigma * (1.0 + pre * (1.0 - sigma)) * mask).astype(BF)
    delta_ref[...] = delta
    wide_ref[0] = delta.astype(F32)
    pack_messages(wide_ref.at[pl.ds(0, 1)], back_msg_ref, q)
    back_copies = halo_copies(back_msg_ref, back_into_ref, back_send_sem, back_recv_sem)
    for copy in back_copies:
        copy.start()
    both = jnp.concatenate([hidden.T, delta.astype(F32).T], axis=0).astype(BF)
    for dx in (0, 1, 2):
        grads_ref[dx] = jnp.dot(both, all_ref[pl.ds(64 * dx, 512), :], preferred_element_type=F32)

    def first_block(k):
        return grads_ref[k // 9, WIDE : WIDE + C, pl.ds(k % 9 * 2 * WIDE, WIDE)] * scale

    def second_block(k):
        turned = 26 - k
        return grads_ref[turned // 9, 0:C, pl.ds(turned % 9 * 2 * WIDE + WIDE, WIDE)] * scale

    for half, block in ((0, first_block), (1, second_block)):

        def store(tile, value):
            data_ref[pl.ds(half * HALF + tile * C, C), :] = value

        pack_grads(block, store)
        data_ref[pl.ds(half * HALF + 21 * C, HALF - 21 * C), :] = jnp.zeros((HALF - 21 * C, WIDE), F32)

    def backward():
        lay_back_weights(first_ref, back_weight_ref)
        for copy in back_copies:
            copy.wait()
        back_picked = pick_messages(position, back_into_ref)
        build_patch(delta_ref[...].astype(F32), back_picked, code, back_level_ref, back_all_ref, WIDE)
        grad = rows_ref[:, WIDE:].astype(F32)
        for dx in (0, 1, 2):
            grad = grad + jnp.dot(
                back_all_ref[pl.ds(64 * dx, 512), :], back_weight_ref[dx], preferred_element_type=F32)
        out_ref[...] = (grad * mask).T[:C].astype(BF)

    all_sum(backward, data_ref, sum_ref, *reduce_refs)


def whole(scale, position, count, x, g, codes, first, second):
    sems = lambda n: pltpu.SemaphoreType.DMA((n,))
    return pl.pallas_call(
        functools.partial(whole_kernel, scale),
        out_shape=(jax.ShapeDtypeStruct((C, 512), BF), jax.ShapeDtypeStruct((ROWS, WIDE), BF)),
        in_specs=[SMEM, SMEM] + [VMEM] * 5,
        out_specs=(VMEM, VMEM),
        scratch_shapes=[
            pltpu.VMEM((2, 512, WIDE), F32), pltpu.VMEM((512, 2 * WIDE), BF),
            pltpu.VMEM((MSG, 2 * WIDE), BF), pltpu.VMEM((MSG, 2 * WIDE), BF),
            pltpu.VMEM((MSG, WIDE), BF), pltpu.VMEM((MSG, WIDE), BF),
            pltpu.VMEM((3, 9 * 2 * WIDE, 2 * WIDE), BF), pltpu.VMEM((3, 9 * WIDE, WIDE), BF),
            pltpu.VMEM((800, 2 * WIDE), F32), pltpu.VMEM((640, 9 * 2 * WIDE), BF),
            pltpu.VMEM((800, WIDE), F32), pltpu.VMEM((640, 9 * WIDE), BF),
            pltpu.VMEM((3, 2 * WIDE, 9 * 2 * WIDE), F32), pltpu.VMEM((ROWS, WIDE), F32),
            pltpu.VMEM((512, WIDE), BF),
            sems(17), sems(17), sems(17), sems(17),
            pltpu.VMEM((ROWS, WIDE), BF),
            pltpu.VMEM((HALF, WIDE), BF), pltpu.VMEM((HALF, WIDE), BF),
            pltpu.VMEM((HALF, WIDE), F32), pltpu.VMEM((HALF, WIDE), BF),
            pltpu.VMEM((16, PART, WIDE), BF), pltpu.VMEM((PART, WIDE), F32),
            pltpu.VMEM((16, CELL, WIDE), F32), pltpu.VMEM((PART, WIDE), F32),
            pltpu.VMEM((PART, WIDE), BF),
            sems(4), sems(16), sems(16), sems(16), sems(16), sems(16), sems(16), sems(16), sems(16),
        ],
        compiler_params=pltpu.CompilerParams(
            collective_id=1, has_side_effects=True, vmem_limit_bytes=56 * 2 ** 20),
        name="whole",
    )(position, count, x, g, codes, first, second)


def finish_kernel(grad_ref, sum_ref, out_ref, first_ref, second_ref):
    out_ref[...] = grad_ref[...]

    def load_first(tile):
        return sum_ref[pl.ds(tile * C, C), :].astype(F32)

    def load_second(tile):
        return sum_ref[pl.ds(HALF + tile * C, C), :].astype(F32)

    def store_first(k, value):
        first_ref[k] = value.T[:C]

    def store_second(k, value):
        second_ref[k] = value[:, :C]

    unpack_grads(load_first, store_first)
    unpack_grads(load_second, store_second)


def finish(grad, summed):
    return pl.pallas_call(
        finish_kernel,
        out_shape=(
            jax.ShapeDtypeStruct((C, 512), BF),
            jax.ShapeDtypeStruct((27, C, C), F32), jax.ShapeDtypeStruct((27, C, C), F32)),
        in_specs=[VMEM, VMEM],
        out_specs=(VMEM,) * 3,
        compiler_params=pltpu.CompilerParams(vmem_limit_bytes=32 * 2 ** 20),
        name="finish",
    )(grad, summed)


def shards(features, cotangent, first_weight, second_weight, slot_position, brick_count, column_code):
    devices = lax.axis_size("gx") * lax.axis_size("gy") * lax.axis_size("gz")
    scale = float(devices ** -0.5 / 8.0)
    grad, summed = whole(
        scale, slot_position.reshape(1), brick_count.reshape(1), features.reshape(C, 512),
        cotangent.reshape(C, 512), column_code.reshape(1, 64), first_weight, second_weight)
    grad_input, first_grad, second_grad = finish(grad, summed)
    return grad_input.reshape(1, 1, 1, 1, C, 512), first_grad, second_grad


def solution(mesh):
    placed = (
        P("gx", "gy", "gz", None, None, None),
        P("gx", "gy", "gz", None, None, None),
        P(),
        P(),
        P("gx", "gy", "gz", None),
        P("gx", "gy", "gz"),
        P("gx", "gy", "gz", None, None),
    )
    return jax.shard_map(
        shards,
        mesh=mesh,
        in_specs=placed,
        out_specs=(P("gx", "gy", "gz", None, None, None), P(), P()),
        check_vma=False,
    )
```

```python
import functools

import jax
import jax.numpy as jnp
from jax import lax
from jax.experimental import pallas as pl
from jax.experimental.pallas import tpu as pltpu
from jax.sharding import PartitionSpec as P

MESH = pl.DeviceIdType.MESH
VMEM = pl.BlockSpec(memory_space=pltpu.VMEM)
SMEM = pl.BlockSpec(memory_space=pltpu.SMEM)
C = 96
WIDE = 128
MSG = 512
BF = jnp.bfloat16
F32 = jnp.float32


def message_plan():
    plan = []
    for ix in (0, 1):
        plan.append((ix, 64, (1 - 2 * ix, 0, 0)))
    for iy in (0, 1):
        plan.append((2 + iy, 64, (0, 1 - 2 * iy, 0)))
    plan.append((4, 64, (0, 0, 1)))
    for ix in (0, 1):
        for iy in (0, 1):
            plan.append((5 + 2 * ix + iy, 16, (1 - 2 * ix, 1 - 2 * iy, 0)))
    for ix in (0, 1):
        plan.append((9 + ix, 16, (1 - 2 * ix, 0, 1)))
    for iy in (0, 1):
        plan.append((11 + iy, 16, (0, 1 - 2 * iy, 1)))
    for ix in (0, 1):
        for iy in (0, 1):
            plan.append((13 + 2 * ix + iy, 16, (1 - 2 * ix, 1 - 2 * iy, 1)))
    return plan


def slot_row(slot):
    return slot * 64 if slot < 5 else 320 + (slot - 5) * 16


def pack_messages(wide_ref, msg_ref, q):
    blank = jnp.zeros((8, WIDE), F32)
    only = lax.broadcasted_iota(jnp.int32, (8, WIDE), 0) == 0
    for part in range(wide_ref.shape[0]):

        def rows(*spot, **stride):
            return wide_ref[part, pl.ds(*spot, **stride), :]

        def put(slot, value):
            start = slot_row(slot)
            msg_ref[pl.ds(start, value.shape[0]), pl.ds(part * WIDE, WIDE)] = value.astype(BF)

        def side(low, high):
            return jnp.where(q == 0, high, low)

        for ix in (0, 1):
            put(ix, rows(448 * (1 - ix), 64))
        for iy in (0, 1):
            edge = [rows(64 * i + 56 * (1 - iy), 8) for i in range(8)]
            put(2 + iy, jnp.concatenate(edge, axis=0))
        put(4, side(rows(0, 64, stride=8), rows(7, 64, stride=8)))
        for ix in (0, 1):
            x0 = 448 * (1 - ix)
            for iy in (0, 1):
                column = rows(x0 + 56 * (1 - iy), 8)
                put(5 + 2 * ix + iy, jnp.concatenate([column, blank], axis=0))
                corner = side(column, pltpu.roll(column, 1, 0))
                put(13 + 2 * ix + iy, jnp.concatenate([jnp.where(only, corner, 0.0), blank], axis=0))
            line = side(rows(x0, 8, stride=8), rows(x0 + 7, 8, stride=8))
            put(9 + ix, jnp.concatenate([line, blank], axis=0))
        for iy in (0, 1):
            y0 = 56 * (1 - iy)
            line = side(rows(y0, 8, stride=64), rows(y0 + 7, 8, stride=64))
            put(11 + iy, jnp.concatenate([line, blank], axis=0))


def pack_rows(position, count, x_ref, g_ref, code_ref, wide_ref, rows_ref):
    column = lax.broadcasted_iota(jnp.int32, (64, 512), 0)
    voxel = lax.broadcasted_iota(jnp.int32, (64, 512), 1)
    spread = jnp.where(column == voxel // 8, 1.0, 0.0).astype(BF)
    codes = jnp.broadcast_to(code_ref[...].astype(F32), (16, 64)).astype(BF)
    code = jnp.dot(codes, spread, preferred_element_type=F32).astype(jnp.int32)[:8]
    low = code // 8
    level = lax.broadcasted_iota(jnp.int32, (8, 512), 1) % 8
    live = (level >= low) & (level <= low + code % 8) & (count > 0)
    mask = jnp.where(live, 1.0, 0.0)
    first = lax.broadcasted_iota(jnp.int32, (8, 512), 0)
    place = jnp.where(first == 0, position.astype(F32), jnp.where(first == 1, mask, 0.0))
    blank = jnp.zeros((24, 512), F32)
    inside = jnp.broadcast_to(mask[:1], (C, 512)) > 0.0
    x = jnp.where(inside, x_ref[...].astype(F32), 0.0)
    g = jnp.where(inside, g_ref[...].astype(F32), 0.0)
    wide_ref[0] = jnp.concatenate([x, place, blank], axis=0).T
    wide_ref[1] = jnp.concatenate([g, jnp.zeros((32, 512), F32)], axis=0).T
    rows_ref[:, :WIDE] = wide_ref[0].astype(BF)
    rows_ref[:, WIDE:] = wide_ref[1].astype(BF)


def neighbour(offset):
    u, w, q = lax.axis_index("gx"), lax.axis_index("gy"), lax.axis_index("gz")
    nx, ny = lax.axis_size("gx"), lax.axis_size("gy")
    du, dv, dw = offset
    return ((u + du + nx) % nx, (w + dv + ny) % ny, 1 - q if dw else q)


def halo_copies(msg_ref, into_ref, send_sem, recv_sem):
    copies = []
    for slot, size, offset in message_plan():
        rows = pl.ds(slot_row(slot), size)
        copies.append(pltpu.make_async_remote_copy(
            src_ref=msg_ref.at[rows, :], dst_ref=into_ref.at[rows, :],
            send_sem=send_sem.at[slot], recv_sem=recv_sem.at[slot],
            device_id=neighbour(offset), device_id_type=MESH))
    return copies


def greet_neighbours(barrier):
    for _, _, offset in message_plan():
        pl.semaphore_signal(barrier, inc=1, device_id=neighbour(offset), device_id_type=MESH)


def pick_messages(position, into_ref):
    def bit(size, divisor):
        return jnp.zeros((size, into_ref.shape[1]), jnp.int32) + position // divisor % 2 == 0

    def at(slot):
        return into_ref[pl.ds(slot_row(slot), 64 if slot < 5 else 16), :].astype(F32)

    def two(slot, divisor):
        low = at(slot)
        return jnp.where(bit(low.shape[0], divisor), low, at(slot + 1))

    def four(slot):
        return jnp.where(bit(16, 4), two(slot, 2), two(slot + 2, 2))

    return jnp.concatenate(
        [two(0, 4), two(2, 2), at(4), four(5), two(9, 4), two(11, 2), four(13)], axis=0).astype(BF)


def halo_codes(position, sender):
    u, w, q = (lax.axis_index(axis) for axis in ("gx", "gy", "gz"))
    nx, ny = lax.axis_size("gx"), lax.axis_size("gy")
    own = (position // 4, position // 2 % 2, position % 2)
    theirs = (sender // 4, sender // 2 % 2, sender % 2)
    beyond = (u + 2 * own[0] - 1, w + 2 * own[1] - 1, q + 2 * own[2] - 1)
    sizes = (nx, ny, 2)
    r = lax.broadcasted_iota(jnp.int32, sender.shape, 1)
    face = r < 192
    t = jnp.where(face, r % 64, r % 16)
    high, low = t // 8, t % 8
    past = (
        (r < 64) | ((r >= 192) & (r < 224)) | (r >= 240),
        ((r >= 64) & (r < 128)) | ((r >= 192) & (r < 208)) | (r >= 224),
        ((r >= 128) & (r < 192)) | (r >= 208))
    index = (
        jnp.where(face, high, t),
        jnp.where(r < 64, high, jnp.where(face, low, t)),
        jnp.where(face, low, t))
    valid = face | (t < jnp.where(r < 240, 8, 1))
    spot = []
    for axis in range(3):
        far = 9 * own[axis]
        near = 9 - far
        same = theirs[axis] == own[axis]
        inner = jnp.where(same, 1 + index[axis], near)
        inner_ok = same | (index[axis] == 7 * own[axis])
        there = jnp.zeros_like(r) + beyond[axis]
        outer_ok = (theirs[axis] != own[axis]) & (there >= 0) & (there < sizes[axis])
        spot.append(jnp.where(past[axis], far, inner))
        valid = valid & ((past[axis] & outer_ok) | (jnp.logical_not(past[axis]) & inner_ok))
    return jnp.where(valid, (spot[0] * 10 + spot[1]) * 16 + spot[2], -1)


def build_patch(rows, picked, code, level_ref, patch_refs):
    n = lax.broadcasted_iota(jnp.int32, (800, 256), 0)
    target = n // 8 * 16 + n % 8
    level = lax.broadcasted_iota(jnp.int32, rows.shape, 0) % 8
    for dz in (0, 1, 2):
        pick = jnp.where(target + dz == code, 1.0, 0.0).astype(BF)
        halo = jnp.dot(pick, picked, preferred_element_type=F32)
        if dz == 0:
            mine = jnp.where(level == 0, 0.0, pltpu.roll(rows, 1, 0))
        elif dz == 1:
            mine = rows
        else:
            mine = jnp.where(level == 7, 0.0, pltpu.roll(rows, 511, 0))
        level_ref[...] = halo
        for i in range(8):
            spot = pl.ds(((i + 1) * 10 + 1) * 8, 64)
            level_ref[spot, :] = level_ref[spot, :] + mine[64 * i : 64 * i + 64]
        for part, patch_ref in enumerate(patch_refs):
            for dy in (0, 1, 2):
                tap = dy * 3 + dz
                for x in range(10):
                    patch_ref[pl.ds(64 * x, 64), pl.ds(tap * WIDE, WIDE)] = (
                        level_ref[pl.ds((x * 10 + dy) * 8, 64), pl.ds(part * WIDE, WIDE)].astype(BF))


def convolve(start, patch_ref, weight_ref):
    total = start
    for dx in (0, 1, 2):
        total = total + jnp.dot(patch_ref[pl.ds(64 * dx, 512), :], weight_ref[dx], preferred_element_type=F32)
    return total


def pack_grads(block, store):
    lane = lax.broadcasted_iota(jnp.int32, (C, WIDE), 1)
    for group in range(2):
        last = block(4 * group + 3)
        for t in range(3):
            shifted = pltpu.roll(last, C - 32 * t, 1)
            store(3 * group + t, jnp.where(lane < C, block(4 * group + t), shifted))
    store(6, block(8))


def unpack_grads(load, store):
    lane = lax.broadcasted_iota(jnp.int32, (C, WIDE), 1)
    for group in range(2):
        last = jnp.zeros((C, WIDE), F32)
        for t in range(3):
            tile = load(3 * group + t)
            store(4 * group + t, tile)
            moved = pltpu.roll(tile, 32 + 32 * t, 1)
            last = jnp.where((lane >= 32 * t) & (lane < 32 * t + 32), moved, last)
        store(4 * group + 3, last)
    store(8, load(6))


def square(block):
    gap = WIDE - C
    wide = jnp.concatenate([block.astype(F32), jnp.zeros((C, gap), F32)], axis=1)
    return jnp.concatenate([wide, jnp.zeros((gap, WIDE), F32)], axis=0)


def lay_weights(kernel_ref, weight_ref, turned):
    def step(k, carry):
        rows = pl.ds(pl.multiple_of(k % 9 * WIDE, WIDE), WIDE)
        block = square(kernel_ref[26 - k]).T if turned else square(kernel_ref[k])
        weight_ref[k // 9, rows, :] = block.astype(BF)
        return carry

    lax.fori_loop(0, 27, step, 0)


ROWS = 4096
HALF = ROWS // 2
STRIP = 7 * C
PART = HALF // 16
CELL = PART // 4


def places():
    u = lax.axis_index("gx")
    w = lax.axis_index("gy")
    q = lax.axis_index("gz")
    core = w % 2
    y = w // 2 % 4
    x = q * 2 + w // 8
    mate = (u, w + 1 - 2 * core, q)

    def plane_peer(t):
        px = (x + t // 4) % 4
        py = (y + t % 4) % 4
        return px * 4 + py, (u, ((px % 2) * 4 + py) * 2 + core, px // 2)

    def near_peer(t):
        r = (u % 4 + t) % 4
        return r, (u // 4 * 4 + r, w, q)

    def far_peer(t):
        g = (u // 4 + t) % 4
        return g, (g * 4 + u % 4, w, q)

    return core, x, y, mate, plane_peer, near_peer, far_peer


def greet_sharers(barrier):
    core, x, y, mate, plane_peer, near_peer, far_peer = places()

    def greet(t, carry):
        pl.semaphore_signal(barrier, inc=1, device_id=plane_peer(t)[1], device_id_type=MESH)
        return carry

    def greet_line(t, carry):
        pl.semaphore_signal(barrier, inc=1, device_id=far_peer(t)[1], device_id_type=MESH)
        pl.semaphore_signal(barrier, inc=1, device_id=near_peer(t)[1], device_id_type=MESH)
        return carry

    lax.fori_loop(1, 4, greet_line, 0)
    lax.fori_loop(1, 16, greet, 0)
    pl.semaphore_signal(barrier, inc=1, device_id=mate, device_id_type=MESH)


def remote(src, dst, sends, recvs, index, device):
    return pltpu.make_async_remote_copy(
        src_ref=src, dst_ref=dst, send_sem=sends.at[index], recv_sem=recvs.at[index],
        device_id=device, device_id_type=MESH)


def swap_copy(strip, half_out, half_in, swap_send, swap_recv):
    rows = pl.ds(strip * STRIP, STRIP)
    return remote(half_out.at[rows, :], half_in.at[rows, :], swap_send, swap_recv, strip, places()[3])


def start_swap(strip, data_ref, half_out, half_in, swap_send, swap_recv):
    core = places()[0]
    theirs = pl.multiple_of((1 - core) * HALF + strip * STRIP, 16)
    half_out[pl.ds(strip * STRIP, STRIP), :] = data_ref[pl.ds(theirs, STRIP), :].astype(BF)
    swap_copy(strip, half_out, half_in, swap_send, swap_recv).start()


def all_sum(fill_plane, fill_line, data_ref, sum_ref, gathered, half_out, half_in, total, plane_out, plane_in,
            near_src, near_in, far_all, own_part, swap_send, swap_recv, plane_send, plane_recv,
            near_send, near_recv, far_send, far_recv, near_send2, near_recv2, plane_send2, plane_recv2,
            join_send, join_recv, out_sem):
    core, x, y, mate, plane_peer, near_peer, far_peer = places()
    u = lax.axis_index("gx")
    chip = x * 4 + y
    own = pl.multiple_of(core * HALF, HALF)
    other = pl.multiple_of((1 - core) * HALF, HALF)

    for strip in range(3):
        rows = pl.ds(strip * STRIP, STRIP)
        swap_copy(strip, half_out, half_in, swap_send, swap_recv).wait()
        mine = data_ref[pl.ds(pl.multiple_of(own + strip * STRIP, 16), STRIP), :]
        both = mine + half_in[rows, :].astype(F32)
        total[rows, :] = both
        plane_out[rows, :] = both.astype(BF)
    rest = pl.ds(3 * STRIP, HALF - 3 * STRIP)
    total[rest, :] = jnp.zeros((HALF - 3 * STRIP, WIDE), F32)
    plane_out[rest, :] = jnp.zeros((HALF - 3 * STRIP, WIDE), BF)

    def plane_copy(t):
        there, device = plane_peer(t)
        rows = pl.ds(pl.multiple_of(there * PART, PART), PART)
        return remote(plane_out.at[rows, :], plane_in.at[t], plane_send, plane_recv, t, device)

    def plane_start(t, carry):
        plane_copy(t).start()
        return carry

    lax.fori_loop(1, 16, plane_start, 0)
    fill_plane()

    def plane_add(t, acc):
        plane_copy(t).wait_recv()
        return acc + plane_in[t].astype(F32)

    part = pl.multiple_of(chip * PART, PART)
    near_src[...] = lax.fori_loop(1, 16, plane_add, total[pl.ds(part, PART), :])

    def near_copy(t):
        there, device = near_peer(t)
        rows = pl.ds(pl.multiple_of(there * CELL, CELL), CELL)
        return remote(near_src.at[rows, :], near_in.at[t], near_send, near_recv, t, device)

    for t in (1, 2, 3):
        near_copy(t).start()
    cell = pl.multiple_of(u % 4 * CELL, CELL)
    cell_sum = near_src[pl.ds(cell, CELL), :]
    for t in (1, 2, 3):
        near_copy(t).wait_recv()
        cell_sum = cell_sum + near_in[t]

    group = u // 4
    far_all[group] = cell_sum

    def far_copy(t, slot):
        return remote(far_all.at[group], far_all.at[slot], far_send, far_recv, t, far_peer(t)[1])

    for t in (1, 2, 3):
        far_copy(t, group).start()
    fill_line()
    for t in (1, 2, 3):
        far_copy(t, (group - t + 4) % 4).wait_recv()
    final = (far_all[0] + far_all[1]) + (far_all[2] + far_all[3])
    own_part[pl.ds(cell, CELL), :] = final.astype(BF)

    def near_back(t, owner):
        rows = pl.ds(pl.multiple_of(owner * CELL, CELL), CELL)
        return remote(own_part.at[rows, :], own_part.at[rows, :], near_send2, near_recv2, t, near_peer(t)[1])

    for t in (1, 2, 3):
        near_back(t, u % 4).start()
    for t in (1, 2, 3):
        near_back(t, (u % 4 - t + 4) % 4).wait_recv()

    place = pl.multiple_of(own + part, PART)

    def plane_back(t):
        return remote(own_part, gathered.at[pl.ds(place, PART), :], plane_send2, plane_recv2, t, plane_peer(t)[1])

    def plane_back_start(t, carry):
        plane_back(t).start()
        return carry

    def source_rows(t, base):
        px = (x - t // 4 + 4) % 4
        py = (y - t % 4 + 4) % 4
        return pl.ds(pl.multiple_of(base + (px * 4 + py) * PART, PART), PART)

    def join_copy(t, base):
        rows = source_rows(t, base)
        return remote(gathered.at[rows, :], gathered.at[rows, :], join_send, join_recv, t, mate)

    lax.fori_loop(1, 16, plane_back_start, 0)
    gathered[pl.ds(place, PART), :] = own_part[...]
    join_copy(0, own).start()

    def plane_back_wait(t, carry):
        remote(own_part, gathered.at[source_rows(t, own), :], plane_send2, plane_recv2, t,
               plane_peer(t)[1]).wait_recv()
        join_copy(t, own).start()
        return carry

    lax.fori_loop(1, 16, plane_back_wait, 0)
    first_out = pltpu.make_async_copy(
        gathered.at[pl.ds(own, HALF), :], sum_ref.at[pl.ds(own, HALF), :], out_sem.at[0])
    first_out.start()

    def join_wait(t, carry):
        join_copy(t, other).wait_recv()
        return carry

    lax.fori_loop(0, 16, join_wait, 0)
    second_out = pltpu.make_async_copy(
        gathered.at[pl.ds(other, HALF), :], sum_ref.at[pl.ds(other, HALF), :], out_sem.at[1])
    second_out.start()

    def drain(t, carry):
        plane_copy(t).wait_send()
        plane_back(t).wait_send()
        join_copy(t, own).wait_send()
        return carry

    lax.fori_loop(1, 16, drain, 0)
    join_copy(0, own).wait_send()
    for t in (1, 2, 3):
        near_copy(t).wait_send()
        far_copy(t, group).wait_send()
        near_back(t, u % 4).wait_send()
    first_out.wait()
    second_out.wait()


SHARERS = 1 + 15 + 3 + 3


def whole_kernel(scale, position_ref, count_ref, x_hbm, g_hbm, code_hbm, first_hbm, second_hbm,
                 out_ref, sum_ref, x_ref, g_ref, code_ref, first_ref, second_ref, load_sem,
                 wide_ref, rows_ref, msg_ref, into_ref, back_msg_ref, back_into_ref,
                 x_weight_ref, g_weight_ref, back_weight_ref, level_ref, x_patch_ref, g_patch_ref,
                 back_level_ref, back_patch_ref, grads_ref, data_ref, delta_ref,
                 send_sem, recv_sem, back_send_sem, back_recv_sem, *reduce_refs):
    q = lax.axis_index("gz")
    position = position_ref[0]
    barrier = pltpu.get_barrier_semaphore()
    greet_sharers(barrier)
    greet_neighbours(barrier)
    loads = [
        pltpu.make_async_copy(src, dst, load_sem.at[i])
        for i, (src, dst) in enumerate((
            (x_hbm, x_ref), (g_hbm, g_ref), (code_hbm, code_ref), (first_hbm, first_ref), (second_hbm, second_ref)))]
    for load in loads:
        load.start()
    for load in loads[:3]:
        load.wait()
    pack_rows(position, count_ref[0], x_ref, g_ref, code_ref, wide_ref, rows_ref)
    pack_messages(wide_ref, msg_ref, q)
    pl.semaphore_wait(barrier, 17 + SHARERS)
    copies = halo_copies(msg_ref, into_ref, send_sem, recv_sem)
    for copy in copies:
        copy.start()
    for load in loads[3:]:
        load.wait()
    lay_weights(first_ref, x_weight_ref, False)
    lay_weights(second_ref, g_weight_ref, True)
    for copy in copies:
        copy.wait()

    rows = rows_ref[...].astype(F32)
    picked = pick_messages(position, into_ref)
    sender = picked[:, :WIDE].astype(F32).T[C : C + 8].astype(jnp.int32)
    code = halo_codes(position, sender)[:1]
    build_patch(rows, picked, code, level_ref, (x_patch_ref, g_patch_ref))
    nothing = jnp.zeros((512, WIDE), F32)
    pre = convolve(nothing, x_patch_ref, x_weight_ref)
    back = convolve(nothing, g_patch_ref, g_weight_ref)
    mask = jnp.broadcast_to(rows[:, C + 1 : C + 2], (512, WIDE))
    sigma = jax.nn.sigmoid(pre)
    hidden = pre * sigma * mask
    delta = (back * sigma * (1.0 + pre * (1.0 - sigma)) * mask).astype(BF)
    delta_ref[...] = delta
    wide_ref[0] = delta.astype(F32)
    pack_messages(wide_ref.at[pl.ds(0, 1)], back_msg_ref, q)
    back_copies = halo_copies(back_msg_ref, back_into_ref, back_send_sem, back_recv_sem)
    for copy in back_copies:
        copy.start()

    turned = (delta.astype(F32).T[:C].astype(BF), hidden.T[:C].astype(BF))
    for dx in (0, 1, 2):
        for half, patch_ref in ((0, x_patch_ref), (1, g_patch_ref)):
            grads_ref[half] = jnp.dot(
                turned[half], patch_ref[pl.ds(64 * dx, 512), :], preferred_element_type=F32)

            def block(tap):
                return grads_ref[half, :, pl.ds(tap * WIDE, WIDE)] * scale

            def store(tile, value):
                data_ref[pl.ds(half * HALF + dx * STRIP + tile * C, C), :] = value

            pack_grads(block, store)
        start_swap(dx, data_ref, *reduce_refs[1:3], *reduce_refs[10:12])

    def fill_plane():
        lay_weights(first_ref, back_weight_ref, True)

    def fill_line():
        for copy in back_copies:
            copy.wait()
        back_picked = pick_messages(position, back_into_ref)
        build_patch(delta_ref[...].astype(F32), back_picked, code, back_level_ref, (back_patch_ref,))
        grad = convolve(rows_ref[:, WIDE:].astype(F32), back_patch_ref, back_weight_ref)
        out_ref[...] = (grad * mask).T[:C].astype(BF)

    all_sum(fill_plane, fill_line, data_ref, sum_ref, *reduce_refs)


def whole(scale, position, count, x, g, codes, first, second):
    sems = lambda n: pltpu.SemaphoreType.DMA((n,))
    taps = 9 * WIDE
    anywhere = pl.BlockSpec(memory_space=pl.ANY)
    return pl.pallas_call(
        functools.partial(whole_kernel, scale),
        out_shape=(jax.ShapeDtypeStruct((C, 512), BF), jax.ShapeDtypeStruct((ROWS, WIDE), BF)),
        in_specs=[SMEM, SMEM] + [anywhere] * 5,
        out_specs=(VMEM, anywhere),
        scratch_shapes=[
            pltpu.VMEM((C, 512), BF), pltpu.VMEM((C, 512), BF), pltpu.VMEM((1, 64), jnp.int32),
            pltpu.VMEM((27, C, C), BF), pltpu.VMEM((27, C, C), BF), sems(5),
            pltpu.VMEM((2, 512, WIDE), F32), pltpu.VMEM((512, 2 * WIDE), BF),
            pltpu.VMEM((MSG, 2 * WIDE), BF), pltpu.VMEM((MSG, 2 * WIDE), BF),
            pltpu.VMEM((MSG, WIDE), BF), pltpu.VMEM((MSG, WIDE), BF),
            pltpu.VMEM((3, taps, WIDE), BF), pltpu.VMEM((3, taps, WIDE), BF), pltpu.VMEM((3, taps, WIDE), BF),
            pltpu.VMEM((800, 2 * WIDE), F32), pltpu.VMEM((640, taps), BF), pltpu.VMEM((640, taps), BF),
            pltpu.VMEM((800, WIDE), F32), pltpu.VMEM((640, taps), BF),
            pltpu.VMEM((2, C, taps), F32), pltpu.VMEM((ROWS, WIDE), F32), pltpu.VMEM((512, WIDE), BF),
            sems(17), sems(17), sems(17), sems(17),
            pltpu.VMEM((ROWS, WIDE), BF),
            pltpu.VMEM((HALF, WIDE), BF), pltpu.VMEM((HALF, WIDE), BF),
            pltpu.VMEM((HALF, WIDE), F32), pltpu.VMEM((HALF, WIDE), BF),
            pltpu.VMEM((16, PART, WIDE), BF), pltpu.VMEM((PART, WIDE), F32),
            pltpu.VMEM((4, CELL, WIDE), F32), pltpu.VMEM((4, CELL, WIDE), F32),
            pltpu.VMEM((PART, WIDE), BF),
            sems(3), sems(3), sems(16), sems(16), sems(4), sems(4), sems(4), sems(4), sems(4), sems(4),
            sems(16), sems(16), sems(16), sems(16), sems(2),
        ],
        compiler_params=pltpu.CompilerParams(
            collective_id=1, has_side_effects=True, vmem_limit_bytes=60 * 2 ** 20),
        name="whole",
    )(position, count, x, g, codes, first, second)


def finish_kernel(grad_ref, first_sum_ref, second_sum_ref, out_ref, first_ref, second_ref):
    out_ref[...] = grad_ref[...]

    def load_first(tile):
        return first_sum_ref[0, pl.ds(tile * C, C), :].astype(F32)

    def load_second(tile):
        return second_sum_ref[0, pl.ds(tile * C, C), :].astype(F32)

    def store_first(tap, value):
        first_ref[tap] = value.T[:C]

    def store_second(tap, value):
        second_ref[8 - tap] = value[:, :C]

    unpack_grads(load_first, store_first)
    unpack_grads(load_second, store_second)


def finish(grad, summed):
    halves = summed.reshape(2, HALF, WIDE)
    return pl.pallas_call(
        finish_kernel,
        grid=(3,),
        out_shape=(
            jax.ShapeDtypeStruct((C, 512), BF),
            jax.ShapeDtypeStruct((27, C, C), F32), jax.ShapeDtypeStruct((27, C, C), F32)),
        in_specs=[
            pl.BlockSpec((C, 512), lambda i: (0, 0)),
            pl.BlockSpec((1, STRIP, WIDE), lambda i: (0, i, 0)),
            pl.BlockSpec((1, STRIP, WIDE), lambda i: (1, 2 - i, 0))],
        out_specs=(
            pl.BlockSpec((C, 512), lambda i: (0, 0)),
            pl.BlockSpec((9, C, C), lambda i: (i, 0, 0)),
            pl.BlockSpec((9, C, C), lambda i: (i, 0, 0))),
        compiler_params=pltpu.CompilerParams(vmem_limit_bytes=60 * 2 ** 20),
        name="finish",
    )(grad, halves, halves)


def shards(features, cotangent, first_weight, second_weight, slot_position, brick_count, column_code):
    devices = lax.axis_size("gx") * lax.axis_size("gy") * lax.axis_size("gz")
    scale = float(devices ** -0.5 / 8.0)
    grad, summed = whole(
        scale, slot_position.reshape(1), brick_count.reshape(1), features.reshape(C, 512),
        cotangent.reshape(C, 512), column_code.reshape(1, 64), first_weight, second_weight)
    grad_input, first_grad, second_grad = finish(grad, summed)
    return grad_input.reshape(1, 1, 1, 1, C, 512), first_grad, second_grad


def solution(mesh):
    placed = (
        P("gx", "gy", "gz", None, None, None),
        P("gx", "gy", "gz", None, None, None),
        P(),
        P(),
        P("gx", "gy", "gz", None),
        P("gx", "gy", "gz"),
        P("gx", "gy", "gz", None, None),
    )
    return jax.shard_map(
        shards,
        mesh=mesh,
        in_specs=placed,
        out_specs=(P("gx", "gy", "gz", None, None, None), P(), P()),
        check_vma=False,
    )
```

```python
import functools

import jax
import jax.numpy as jnp
from jax import lax
from jax.experimental import pallas as pl
from jax.experimental.pallas import tpu as pltpu
from jax.sharding import PartitionSpec as P

MESH = pl.DeviceIdType.MESH
VMEM = pl.BlockSpec(memory_space=pltpu.VMEM)
SMEM = pl.BlockSpec(memory_space=pltpu.SMEM)
C = 96
WIDE = 128
MSG = 512
BF = jnp.bfloat16
F32 = jnp.float32


def message_plan():
    plan = []
    for ix in (0, 1):
        for iy in (0, 1):
            plan.append((13 + 2 * ix + iy, 16, (1 - 2 * ix, 1 - 2 * iy, 1)))
    for iy in (0, 1):
        plan.append((11 + iy, 16, (0, 1 - 2 * iy, 1)))
    for ix in (0, 1):
        plan.append((9 + ix, 16, (1 - 2 * ix, 0, 1)))
    for ix in (0, 1):
        for iy in (0, 1):
            plan.append((5 + 2 * ix + iy, 16, (1 - 2 * ix, 1 - 2 * iy, 0)))
    plan.append((4, 64, (0, 0, 1)))
    for iy in (0, 1):
        plan.append((2 + iy, 64, (0, 1 - 2 * iy, 0)))
    for ix in (0, 1):
        plan.append((ix, 64, (1 - 2 * ix, 0, 0)))
    return plan


def slot_row(slot):
    return slot * 64 if slot < 5 else 320 + (slot - 5) * 16


def pack_messages(wide_ref, msg_ref, q):
    blank = jnp.zeros((8, WIDE), F32)
    only = lax.broadcasted_iota(jnp.int32, (8, WIDE), 0) == 0
    for part in range(wide_ref.shape[0]):

        def rows(*spot, **stride):
            return wide_ref[part, pl.ds(*spot, **stride), :]

        def put(slot, value):
            start = slot_row(slot)
            msg_ref[pl.ds(start, value.shape[0]), pl.ds(part * WIDE, WIDE)] = value.astype(BF)

        def side(low, high):
            return jnp.where(q == 0, high, low)

        for ix in (0, 1):
            put(ix, rows(448 * (1 - ix), 64))
        for iy in (0, 1):
            edge = [rows(64 * i + 56 * (1 - iy), 8) for i in range(8)]
            put(2 + iy, jnp.concatenate(edge, axis=0))
        put(4, side(rows(0, 64, stride=8), rows(7, 64, stride=8)))
        for ix in (0, 1):
            x0 = 448 * (1 - ix)
            for iy in (0, 1):
                column = rows(x0 + 56 * (1 - iy), 8)
                put(5 + 2 * ix + iy, jnp.concatenate([column, blank], axis=0))
                corner = side(column, pltpu.roll(column, 1, 0))
                put(13 + 2 * ix + iy, jnp.concatenate([jnp.where(only, corner, 0.0), blank], axis=0))
            line = side(rows(x0, 8, stride=8), rows(x0 + 7, 8, stride=8))
            put(9 + ix, jnp.concatenate([line, blank], axis=0))
        for iy in (0, 1):
            y0 = 56 * (1 - iy)
            line = side(rows(y0, 8, stride=64), rows(y0 + 7, 8, stride=64))
            put(11 + iy, jnp.concatenate([line, blank], axis=0))


def pack_rows(position, count, x_ref, g_ref, code_ref, wide_ref, rows_ref):
    column = lax.broadcasted_iota(jnp.int32, (64, 512), 0)
    voxel = lax.broadcasted_iota(jnp.int32, (64, 512), 1)
    spread = jnp.where(column == voxel // 8, 1.0, 0.0).astype(BF)
    codes = jnp.broadcast_to(code_ref[...].astype(F32), (16, 64)).astype(BF)
    code = jnp.dot(codes, spread, preferred_element_type=F32).astype(jnp.int32)[:8]
    low = code // 8
    level = lax.broadcasted_iota(jnp.int32, (8, 512), 1) % 8
    live = (level >= low) & (level <= low + code % 8) & (count > 0)
    mask = jnp.where(live, 1.0, 0.0)
    first = lax.broadcasted_iota(jnp.int32, (8, 512), 0)
    place = jnp.where(first == 0, position.astype(F32), jnp.where(first == 1, mask, 0.0))
    blank = jnp.zeros((24, 512), F32)
    inside = jnp.broadcast_to(mask[:1], (C, 512)) > 0.0
    x = jnp.where(inside, x_ref[...].astype(F32), 0.0)
    g = jnp.where(inside, g_ref[...].astype(F32), 0.0)
    wide_ref[0] = jnp.concatenate([x, place, blank], axis=0).T
    wide_ref[1] = jnp.concatenate([g, jnp.zeros((32, 512), F32)], axis=0).T
    rows_ref[:, :WIDE] = wide_ref[0].astype(BF)
    rows_ref[:, WIDE:] = wide_ref[1].astype(BF)


def neighbour(offset):
    u, w, q = lax.axis_index("gx"), lax.axis_index("gy"), lax.axis_index("gz")
    nx, ny = lax.axis_size("gx"), lax.axis_size("gy")
    du, dv, dw = offset
    return ((u + du + nx) % nx, (w + dv + ny) % ny, 1 - q if dw else q)


def halo_copies(msg_ref, into_ref, send_sem, recv_sem):
    copies = []
    for slot, size, offset in message_plan():
        rows = pl.ds(slot_row(slot), size)
        copies.append(pltpu.make_async_remote_copy(
            src_ref=msg_ref.at[rows, :], dst_ref=into_ref.at[rows, :],
            send_sem=send_sem.at[slot], recv_sem=recv_sem.at[slot],
            device_id=neighbour(offset), device_id_type=MESH))
    return copies


def greet_neighbours(barrier):
    for _, _, offset in message_plan():
        pl.semaphore_signal(barrier, inc=1, device_id=neighbour(offset), device_id_type=MESH)


def pick_messages(position, into_ref):
    def bit(size, divisor):
        return jnp.zeros((size, into_ref.shape[1]), jnp.int32) + position // divisor % 2 == 0

    def at(slot):
        return into_ref[pl.ds(slot_row(slot), 64 if slot < 5 else 16), :].astype(F32)

    def two(slot, divisor):
        low = at(slot)
        return jnp.where(bit(low.shape[0], divisor), low, at(slot + 1))

    def four(slot):
        return jnp.where(bit(16, 4), two(slot, 2), two(slot + 2, 2))

    return jnp.concatenate(
        [two(0, 4), two(2, 2), at(4), four(5), two(9, 4), two(11, 2), four(13)], axis=0).astype(BF)


def halo_codes(position, sender):
    u, w, q = (lax.axis_index(axis) for axis in ("gx", "gy", "gz"))
    nx, ny = lax.axis_size("gx"), lax.axis_size("gy")
    own = (position // 4, position // 2 % 2, position % 2)
    theirs = (sender // 4, sender // 2 % 2, sender % 2)
    beyond = (u + 2 * own[0] - 1, w + 2 * own[1] - 1, q + 2 * own[2] - 1)
    sizes = (nx, ny, 2)
    r = lax.broadcasted_iota(jnp.int32, sender.shape, 1)
    face = r < 192
    t = jnp.where(face, r % 64, r % 16)
    high, low = t // 8, t % 8
    past = (
        (r < 64) | ((r >= 192) & (r < 224)) | (r >= 240),
        ((r >= 64) & (r < 128)) | ((r >= 192) & (r < 208)) | (r >= 224),
        ((r >= 128) & (r < 192)) | (r >= 208))
    index = (
        jnp.where(face, high, t),
        jnp.where(r < 64, high, jnp.where(face, low, t)),
        jnp.where(face, low, t))
    valid = face | (t < jnp.where(r < 240, 8, 1))
    spot = []
    for axis in range(3):
        far = 9 * own[axis]
        near = 9 - far
        same = theirs[axis] == own[axis]
        inner = jnp.where(same, 1 + index[axis], near)
        inner_ok = same | (index[axis] == 7 * own[axis])
        there = jnp.zeros_like(r) + beyond[axis]
        outer_ok = (theirs[axis] != own[axis]) & (there >= 0) & (there < sizes[axis])
        spot.append(jnp.where(past[axis], far, inner))
        valid = valid & ((past[axis] & outer_ok) | (jnp.logical_not(past[axis]) & inner_ok))
    return jnp.where(valid, (spot[0] * 10 + spot[1]) * 16 + spot[2], -1)


def build_patch(rows, picked, code, level_ref, patch_refs):
    n = lax.broadcasted_iota(jnp.int32, (800, 256), 0)
    target = n // 8 * 16 + n % 8
    level = lax.broadcasted_iota(jnp.int32, rows.shape, 0) % 8
    for dz in (0, 1, 2):
        pick = jnp.where(target + dz == code, 1.0, 0.0).astype(BF)
        halo = jnp.dot(pick, picked, preferred_element_type=F32)
        if dz == 0:
            mine = jnp.where(level == 0, 0.0, pltpu.roll(rows, 1, 0))
        elif dz == 1:
            mine = rows
        else:
            mine = jnp.where(level == 7, 0.0, pltpu.roll(rows, 511, 0))
        level_ref[...] = halo
        for i in range(8):
            spot = pl.ds(((i + 1) * 10 + 1) * 8, 64)
            level_ref[spot, :] = level_ref[spot, :] + mine[64 * i : 64 * i + 64]
        for part, patch_ref in enumerate(patch_refs):
            for dy in (0, 1, 2):
                tap = dy * 3 + dz
                for x in range(10):
                    patch_ref[pl.ds(64 * x, 64), pl.ds(tap * WIDE, WIDE)] = (
                        level_ref[pl.ds((x * 10 + dy) * 8, 64), pl.ds(part * WIDE, WIDE)].astype(BF))


def convolve(start, patch_ref, weight_ref):
    total = start
    for dx in (0, 1, 2):
        total = total + jnp.dot(patch_ref[pl.ds(64 * dx, 512), :], weight_ref[dx], preferred_element_type=F32)
    return total


def pack_grads(block, store):
    lane = lax.broadcasted_iota(jnp.int32, (C, WIDE), 1)
    for group in range(2):
        last = block(4 * group + 3)
        for t in range(3):
            shifted = pltpu.roll(last, C - 32 * t, 1)
            store(3 * group + t, jnp.where(lane < C, block(4 * group + t), shifted))
    store(6, block(8))


def unpack_grads(load, store):
    lane = lax.broadcasted_iota(jnp.int32, (C, WIDE), 1)
    for group in range(2):
        last = jnp.zeros((C, WIDE), F32)
        for t in range(3):
            tile = load(3 * group + t)
            store(4 * group + t, tile)
            moved = pltpu.roll(tile, 32 + 32 * t, 1)
            last = jnp.where((lane >= 32 * t) & (lane < 32 * t + 32), moved, last)
        store(4 * group + 3, last)
    store(8, load(6))


def square(block):
    gap = WIDE - C
    wide = jnp.concatenate([block.astype(F32), jnp.zeros((C, gap), F32)], axis=1)
    return jnp.concatenate([wide, jnp.zeros((gap, WIDE), F32)], axis=0)


def lay_weights(kernel_ref, weight_ref, turned):
    def step(k, carry):
        rows = pl.ds(pl.multiple_of(k % 9 * WIDE, WIDE), WIDE)
        block = square(kernel_ref[26 - k]).T if turned else square(kernel_ref[k])
        weight_ref[k // 9, rows, :] = block.astype(BF)
        return carry

    lax.fori_loop(0, 27, step, 0)


ROWS = 4096
HALF = ROWS // 2
STRIP = 7 * C
PART = HALF // 16
CELL = PART // 4


def ring(distance, size):
    return min(distance, size - distance)


PLANE = sorted(range(1, 16), key=lambda t: -ring(t // 4, 4) - ring(t % 4, 4))
LINE = sorted(range(1, 16), key=lambda t: -ring(t, 16))


def places():
    u = lax.axis_index("gx")
    w = lax.axis_index("gy")
    q = lax.axis_index("gz")
    core = w % 2
    y = w // 2 % 4
    x = q * 2 + w // 8
    mate = (u, w + 1 - 2 * core, q)

    def plane_peer(t):
        px = (x + t // 4) % 4
        py = (y + t % 4) % 4
        return px * 4 + py, (u, ((px % 2) * 4 + py) * 2 + core, px // 2)

    def near_peer(t):
        r = (u % 4 + t) % 4
        return r, (u // 4 * 4 + r, w, q)

    def line_peer(t):
        return (u + t) % 16, w, q

    return core, x, y, mate, plane_peer, near_peer, line_peer


def greet_sharers(barrier):
    core, x, y, mate, plane_peer, near_peer, line_peer = places()
    for t in LINE:
        pl.semaphore_signal(barrier, inc=1, device_id=line_peer(t), device_id_type=MESH)
    for t in PLANE:
        pl.semaphore_signal(barrier, inc=1, device_id=plane_peer(t)[1], device_id_type=MESH)
    pl.semaphore_signal(barrier, inc=1, device_id=mate, device_id_type=MESH)


def remote(src, dst, sends, recvs, index, device):
    return pltpu.make_async_remote_copy(
        src_ref=src, dst_ref=dst, send_sem=sends.at[index], recv_sem=recvs.at[index],
        device_id=device, device_id_type=MESH)


def swap_copy(strip, half_out, half_in, swap_send, swap_recv):
    rows = pl.ds(strip * STRIP, STRIP)
    return remote(half_out.at[rows, :], half_in.at[rows, :], swap_send, swap_recv, strip, places()[3])


def start_swap(strip, data_ref, half_out, half_in, swap_send, swap_recv):
    core = places()[0]
    theirs = pl.multiple_of((1 - core) * HALF + strip * STRIP, 16)
    half_out[pl.ds(strip * STRIP, STRIP), :] = data_ref[pl.ds(theirs, STRIP), :]
    swap_copy(strip, half_out, half_in, swap_send, swap_recv).start()


def all_sum(fill_plane, fill_line, data_ref, sum_ref, gathered, half_out, half_in, total, plane_out, plane_in,
            near_src, near_in, line_in, own_part, swap_send, swap_recv, plane_send, plane_recv,
            near_send, near_recv, line_send, line_recv, plane_send2, plane_recv2,
            join_send, join_recv, out_sem):
    core, x, y, mate, plane_peer, near_peer, line_peer = places()
    u = lax.axis_index("gx")
    chip = x * 4 + y
    own = pl.multiple_of(core * HALF, HALF)
    other = pl.multiple_of((1 - core) * HALF, HALF)

    swaps = [swap_copy(strip, half_out, half_in, swap_send, swap_recv) for strip in range(3)]
    for strip in range(3):
        rows = pl.ds(strip * STRIP, STRIP)
        swaps[strip].wait_recv()
        mine = data_ref[pl.ds(pl.multiple_of(own + strip * STRIP, 16), STRIP), :]
        both = mine + half_in[rows, :]
        total[rows, :] = both
        plane_out[rows, :] = both.astype(BF)
    rest = pl.ds(3 * STRIP, HALF - 3 * STRIP)
    total[rest, :] = jnp.zeros((HALF - 3 * STRIP, WIDE), F32)
    plane_out[rest, :] = jnp.zeros((HALF - 3 * STRIP, WIDE), BF)

    def plane_copy(t):
        there, device = plane_peer(t)
        rows = pl.ds(pl.multiple_of(there * PART, PART), PART)
        return remote(plane_out.at[rows, :], plane_in.at[t], plane_send, plane_recv, t, device)

    plane_copies = [plane_copy(t) for t in PLANE]
    for copy in plane_copies:
        copy.start()
    fill_plane()
    part = pl.multiple_of(chip * PART, PART)
    part_sum = total[pl.ds(part, PART), :]
    for t, copy in zip(reversed(PLANE), reversed(plane_copies)):
        copy.wait_recv()
        part_sum = part_sum + plane_in[t].astype(F32)
    near_src[...] = part_sum

    def near_copy(t):
        there, device = near_peer(t)
        rows = pl.ds(pl.multiple_of(there * CELL, CELL), CELL)
        return remote(near_src.at[rows, :], near_in.at[t], near_send, near_recv, t, device)

    near_copies = [near_copy(t) for t in (1, 2, 3)]
    for copy in near_copies:
        copy.start()
    cell_sum = near_src[pl.ds(pl.multiple_of(u % 4 * CELL, CELL), CELL), :]
    for t, copy in zip((1, 2, 3), near_copies):
        copy.wait_recv()
        cell_sum = cell_sum + near_in[t]

    line_in[u] = cell_sum.astype(BF)

    def line_copy(t, slot):
        return remote(line_in.at[u], line_in.at[slot], line_send, line_recv, t, line_peer(t))

    line_copies = [line_copy(t, u) for t in LINE]
    for copy in line_copies:
        copy.start()
    fill_line()
    for t in reversed(LINE):
        line_copy(t, (u - t + 16) % 16).wait_recv()
    for r in range(4):
        cells = [line_in[4 * group + r].astype(F32) for group in range(4)]
        own_part[pl.ds(r * CELL, CELL), :] = ((cells[0] + cells[1]) + (cells[2] + cells[3])).astype(BF)

    place = pl.multiple_of(own + part, PART)

    def plane_back(t):
        return remote(own_part, gathered.at[pl.ds(place, PART), :], plane_send2, plane_recv2, t, plane_peer(t)[1])

    def source_rows(t, base):
        px = (x - t // 4 + 4) % 4
        py = (y - t % 4 + 4) % 4
        return pl.ds(pl.multiple_of(base + (px * 4 + py) * PART, PART), PART)

    def plane_arrive(t):
        return remote(own_part, gathered.at[source_rows(t, own), :], plane_send2, plane_recv2, t, plane_peer(t)[1])

    def join_copy(t, base):
        rows = source_rows(t, base)
        return remote(gathered.at[rows, :], gathered.at[rows, :], join_send, join_recv, t, mate)

    backs = [plane_back(t) for t in PLANE]
    for copy in backs:
        copy.start()
    gathered[pl.ds(place, PART), :] = own_part[...]
    joins = [join_copy(0, own)]
    joins[0].start()
    for t in reversed(PLANE):
        plane_arrive(t).wait_recv()
        joins.append(join_copy(t, own))
        joins[-1].start()
    first_out = pltpu.make_async_copy(
        gathered.at[pl.ds(own, HALF), :], sum_ref.at[pl.ds(own, HALF), :], out_sem.at[0])
    first_out.start()
    for t in [0, *reversed(PLANE)]:
        join_copy(t, other).wait_recv()
    second_out = pltpu.make_async_copy(
        gathered.at[pl.ds(other, HALF), :], sum_ref.at[pl.ds(other, HALF), :], out_sem.at[1])
    second_out.start()
    for copy in [*swaps, *plane_copies, *near_copies, *line_copies, *backs, *joins]:
        copy.wait_send()
    first_out.wait()
    second_out.wait()


SHARERS = 1 + 15 + 15


def whole_kernel(scale, position_ref, count_ref, x_hbm, g_hbm, code_hbm, first_hbm, second_hbm,
                 out_ref, sum_ref, x_ref, g_ref, code_ref, first_ref, second_ref, load_sem,
                 wide_ref, rows_ref, msg_ref, into_ref, back_msg_ref, back_into_ref,
                 x_weight_ref, g_weight_ref, back_weight_ref, level_ref, x_patch_ref, g_patch_ref,
                 back_level_ref, back_patch_ref, grads_ref, data_ref, delta_ref,
                 send_sem, recv_sem, back_send_sem, back_recv_sem, *reduce_refs):
    q = lax.axis_index("gz")
    position = position_ref[0]
    barrier = pltpu.get_barrier_semaphore()
    greet_sharers(barrier)
    greet_neighbours(barrier)
    loads = [
        pltpu.make_async_copy(src, dst, load_sem.at[i])
        for i, (src, dst) in enumerate((
            (x_hbm, x_ref), (g_hbm, g_ref), (code_hbm, code_ref), (first_hbm, first_ref), (second_hbm, second_ref)))]
    for load in loads:
        load.start()
    for load in loads[:3]:
        load.wait()
    pack_rows(position, count_ref[0], x_ref, g_ref, code_ref, wide_ref, rows_ref)
    pack_messages(wide_ref, msg_ref, q)
    pl.semaphore_wait(barrier, 17 + SHARERS)
    copies = halo_copies(msg_ref, into_ref, send_sem, recv_sem)
    for copy in copies:
        copy.start()
    for load in loads[3:]:
        load.wait()
    lay_weights(first_ref, x_weight_ref, False)
    lay_weights(second_ref, g_weight_ref, True)
    for copy in copies:
        copy.wait()

    rows = rows_ref[...].astype(F32)
    picked = pick_messages(position, into_ref)
    sender = picked[:, :WIDE].astype(F32).T[C : C + 8].astype(jnp.int32)
    code = halo_codes(position, sender)[:1]
    build_patch(rows, picked, code, level_ref, (x_patch_ref, g_patch_ref))
    nothing = jnp.zeros((512, WIDE), F32)
    pre = convolve(nothing, x_patch_ref, x_weight_ref)
    back = convolve(nothing, g_patch_ref, g_weight_ref)
    mask = jnp.broadcast_to(rows[:, C + 1 : C + 2], (512, WIDE))
    sigma = jax.nn.sigmoid(pre)
    hidden = pre * sigma * mask
    delta = (back * sigma * (1.0 + pre * (1.0 - sigma)) * mask).astype(BF)
    delta_ref[...] = delta
    wide_ref[0] = delta.astype(F32)
    back_copies = halo_copies(back_msg_ref, back_into_ref, back_send_sem, back_recv_sem)

    turned = (delta.astype(F32).T[:C].astype(BF), hidden.T[:C].astype(BF))
    for dx in (0, 1, 2):
        for half, patch_ref in ((0, x_patch_ref), (1, g_patch_ref)):
            grads_ref[half] = jnp.dot(
                turned[half], patch_ref[pl.ds(64 * dx, 512), :], preferred_element_type=F32)

            def block(tap):
                return grads_ref[half, :, pl.ds(tap * WIDE, WIDE)] * scale

            def store(tile, value):
                data_ref[pl.ds(half * HALF + dx * STRIP + tile * C, C), :] = value

            pack_grads(block, store)
        start_swap(dx, data_ref, *reduce_refs[1:3], *reduce_refs[10:12])

    def fill_plane():
        pack_messages(wide_ref.at[pl.ds(0, 1)], back_msg_ref, q)
        for copy in back_copies:
            copy.start()
        lay_weights(first_ref, back_weight_ref, True)

    def fill_line():
        for copy in back_copies:
            copy.wait()
        back_picked = pick_messages(position, back_into_ref)
        build_patch(delta_ref[...].astype(F32), back_picked, code, back_level_ref, (back_patch_ref,))
        grad = convolve(rows_ref[:, WIDE:].astype(F32), back_patch_ref, back_weight_ref)
        out_ref[...] = (grad * mask).T[:C].astype(BF)

    all_sum(fill_plane, fill_line, data_ref, sum_ref, *reduce_refs)


def whole(scale, position, count, x, g, codes, first, second):
    sems = lambda n: pltpu.SemaphoreType.DMA((n,))
    taps = 9 * WIDE
    anywhere = pl.BlockSpec(memory_space=pl.ANY)
    return pl.pallas_call(
        functools.partial(whole_kernel, scale),
        out_shape=(jax.ShapeDtypeStruct((C, 512), BF), jax.ShapeDtypeStruct((ROWS, WIDE), BF)),
        in_specs=[SMEM, SMEM] + [anywhere] * 5,
        out_specs=(VMEM, anywhere),
        scratch_shapes=[
            pltpu.VMEM((C, 512), BF), pltpu.VMEM((C, 512), BF), pltpu.VMEM((1, 64), jnp.int32),
            pltpu.VMEM((27, C, C), BF), pltpu.VMEM((27, C, C), BF), sems(5),
            pltpu.VMEM((2, 512, WIDE), F32), pltpu.VMEM((512, 2 * WIDE), BF),
            pltpu.VMEM((MSG, 2 * WIDE), BF), pltpu.VMEM((MSG, 2 * WIDE), BF),
            pltpu.VMEM((MSG, WIDE), BF), pltpu.VMEM((MSG, WIDE), BF),
            pltpu.VMEM((3, taps, WIDE), BF), pltpu.VMEM((3, taps, WIDE), BF), pltpu.VMEM((3, taps, WIDE), BF),
            pltpu.VMEM((800, 2 * WIDE), F32), pltpu.VMEM((640, taps), BF), pltpu.VMEM((640, taps), BF),
            pltpu.VMEM((800, WIDE), F32), pltpu.VMEM((640, taps), BF),
            pltpu.VMEM((2, C, taps), F32), pltpu.VMEM((ROWS, WIDE), F32), pltpu.VMEM((512, WIDE), BF),
            sems(17), sems(17), sems(17), sems(17),
            pltpu.VMEM((ROWS, WIDE), BF),
            pltpu.VMEM((HALF, WIDE), F32), pltpu.VMEM((HALF, WIDE), F32),
            pltpu.VMEM((HALF, WIDE), F32), pltpu.VMEM((HALF, WIDE), BF),
            pltpu.VMEM((16, PART, WIDE), BF), pltpu.VMEM((PART, WIDE), F32),
            pltpu.VMEM((4, CELL, WIDE), F32), pltpu.VMEM((16, CELL, WIDE), BF),
            pltpu.VMEM((PART, WIDE), BF),
            sems(3), sems(3), sems(16), sems(16), sems(4), sems(4), sems(16), sems(16),
            sems(16), sems(16), sems(16), sems(16), sems(2),
        ],
        compiler_params=pltpu.CompilerParams(
            collective_id=1, has_side_effects=True, vmem_limit_bytes=60 * 2 ** 20),
        name="whole",
    )(position, count, x, g, codes, first, second)


def finish_kernel(grad_hbm, sum_hbm, out_hbm, first_hbm, second_hbm, sum_ref, first_ref, second_ref, in_sem, out_sem):
    keep = pltpu.make_async_copy(grad_hbm, out_hbm, out_sem.at[6])
    keep.start()
    strips = [(half, dx) for dx in (0, 1, 2) for half in (0, 1)]
    loads = []
    for i, (half, dx) in enumerate(strips):
        rows = pl.ds(half * HALF + dx * STRIP, STRIP)
        loads.append(pltpu.make_async_copy(sum_hbm.at[rows, :], sum_ref.at[i], in_sem.at[i]))
        loads[-1].start()
    stores = []
    for i, (half, dx) in enumerate(strips):
        loads[i].wait()

        def load(tile):
            return sum_ref[i, pl.ds(tile * C, C), :].astype(F32)

        def store(tap, value):
            if half == 0:
                first_ref[9 * dx + tap] = value.T[:C]
            else:
                second_ref[26 - 9 * dx - tap] = value[:, :C]

        unpack_grads(load, store)
        done = (first_ref, first_hbm, 9 * dx) if half == 0 else (second_ref, second_hbm, 18 - 9 * dx)
        taps = pl.ds(done[2], 9)
        stores.append(pltpu.make_async_copy(done[0].at[taps], done[1].at[taps], out_sem.at[i]))
        stores[-1].start()
    for copy in stores:
        copy.wait()
    keep.wait()


def finish(grad, summed):
    anywhere = pl.BlockSpec(memory_space=pl.ANY)
    return pl.pallas_call(
        finish_kernel,
        out_shape=(
            jax.ShapeDtypeStruct((C, 512), BF),
            jax.ShapeDtypeStruct((27, C, C), F32), jax.ShapeDtypeStruct((27, C, C), F32)),
        in_specs=[anywhere, anywhere],
        out_specs=(anywhere,) * 3,
        scratch_shapes=[
            pltpu.VMEM((6, STRIP, WIDE), BF), pltpu.VMEM((27, C, C), F32), pltpu.VMEM((27, C, C), F32),
            pltpu.SemaphoreType.DMA((6,)), pltpu.SemaphoreType.DMA((7,))],
        compiler_params=pltpu.CompilerParams(vmem_limit_bytes=60 * 2 ** 20),
        name="finish",
    )(grad, summed)


def shards(features, cotangent, first_weight, second_weight, slot_position, brick_count, column_code):
    devices = lax.axis_size("gx") * lax.axis_size("gy") * lax.axis_size("gz")
    scale = float(devices ** -0.5 / 8.0)
    grad, summed = whole(
        scale, slot_position.reshape(1), brick_count.reshape(1), features.reshape(C, 512),
        cotangent.reshape(C, 512), column_code.reshape(1, 64), first_weight, second_weight)
    grad_input, first_grad, second_grad = finish(grad, summed)
    return grad_input.reshape(1, 1, 1, 1, C, 512), first_grad, second_grad


def solution(mesh):
    placed = (
        P("gx", "gy", "gz", None, None, None),
        P("gx", "gy", "gz", None, None, None),
        P(),
        P(),
        P("gx", "gy", "gz", None),
        P("gx", "gy", "gz"),
        P("gx", "gy", "gz", None, None),
    )
    return jax.shard_map(
        shards,
        mesh=mesh,
        in_specs=placed,
        out_specs=(P("gx", "gy", "gz", None, None, None), P(), P()),
        check_vma=False,
    )
```

```python
import functools

import jax
import jax.numpy as jnp
from jax import lax
from jax.experimental import pallas as pl
from jax.experimental.pallas import tpu as pltpu
from jax.sharding import PartitionSpec as P

MESH = pl.DeviceIdType.MESH
VMEM = pl.BlockSpec(memory_space=pltpu.VMEM)
SMEM = pl.BlockSpec(memory_space=pltpu.SMEM)
C = 96
WIDE = 128
MSG = 512
BF = jnp.bfloat16
F32 = jnp.float32


def message_plan():
    plan = []
    for ix in (0, 1):
        for iy in (0, 1):
            plan.append((13 + 2 * ix + iy, 16, (1 - 2 * ix, 1 - 2 * iy, 1)))
    for iy in (0, 1):
        plan.append((11 + iy, 16, (0, 1 - 2 * iy, 1)))
    for ix in (0, 1):
        plan.append((9 + ix, 16, (1 - 2 * ix, 0, 1)))
    for ix in (0, 1):
        for iy in (0, 1):
            plan.append((5 + 2 * ix + iy, 16, (1 - 2 * ix, 1 - 2 * iy, 0)))
    plan.append((4, 64, (0, 0, 1)))
    for iy in (0, 1):
        plan.append((2 + iy, 64, (0, 1 - 2 * iy, 0)))
    for ix in (0, 1):
        plan.append((ix, 64, (1 - 2 * ix, 0, 0)))
    return plan


def slot_row(slot):
    return slot * 64 if slot < 5 else 320 + (slot - 5) * 16


def pack_messages(wide_ref, msg_ref, q):
    blank = jnp.zeros((8, WIDE), F32)
    only = lax.broadcasted_iota(jnp.int32, (8, WIDE), 0) == 0
    for part in range(wide_ref.shape[0]):

        def rows(*spot, **stride):
            return wide_ref[part, pl.ds(*spot, **stride), :]

        def put(slot, value):
            start = slot_row(slot)
            msg_ref[pl.ds(start, value.shape[0]), pl.ds(part * WIDE, WIDE)] = value.astype(BF)

        def side(low, high):
            return jnp.where(q == 0, high, low)

        for ix in (0, 1):
            put(ix, rows(448 * (1 - ix), 64))
        for iy in (0, 1):
            edge = [rows(64 * i + 56 * (1 - iy), 8) for i in range(8)]
            put(2 + iy, jnp.concatenate(edge, axis=0))
        put(4, side(rows(0, 64, stride=8), rows(7, 64, stride=8)))
        for ix in (0, 1):
            x0 = 448 * (1 - ix)
            for iy in (0, 1):
                column = rows(x0 + 56 * (1 - iy), 8)
                put(5 + 2 * ix + iy, jnp.concatenate([column, blank], axis=0))
                corner = side(column, pltpu.roll(column, 1, 0))
                put(13 + 2 * ix + iy, jnp.concatenate([jnp.where(only, corner, 0.0), blank], axis=0))
            line = side(rows(x0, 8, stride=8), rows(x0 + 7, 8, stride=8))
            put(9 + ix, jnp.concatenate([line, blank], axis=0))
        for iy in (0, 1):
            y0 = 56 * (1 - iy)
            line = side(rows(y0, 8, stride=64), rows(y0 + 7, 8, stride=64))
            put(11 + iy, jnp.concatenate([line, blank], axis=0))


def pack_rows(position, count, x_ref, g_ref, code_ref, wide_ref, rows_ref):
    column = lax.broadcasted_iota(jnp.int32, (64, 512), 0)
    voxel = lax.broadcasted_iota(jnp.int32, (64, 512), 1)
    spread = jnp.where(column == voxel // 8, 1.0, 0.0).astype(BF)
    codes = jnp.broadcast_to(code_ref[...].astype(F32), (16, 64)).astype(BF)
    code = jnp.dot(codes, spread, preferred_element_type=F32).astype(jnp.int32)[:8]
    low = code // 8
    level = lax.broadcasted_iota(jnp.int32, (8, 512), 1) % 8
    live = (level >= low) & (level <= low + code % 8) & (count > 0)
    mask = jnp.where(live, 1.0, 0.0)
    first = lax.broadcasted_iota(jnp.int32, (8, 512), 0)
    place = jnp.where(first == 0, position.astype(F32), jnp.where(first == 1, mask, 0.0))
    blank = jnp.zeros((24, 512), F32)
    inside = jnp.broadcast_to(mask[:1], (C, 512)) > 0.0
    x = jnp.where(inside, x_ref[...].astype(F32), 0.0)
    g = jnp.where(inside, g_ref[...].astype(F32), 0.0)
    wide_ref[0] = jnp.concatenate([x, place, blank], axis=0).T
    wide_ref[1] = jnp.concatenate([g, jnp.zeros((32, 512), F32)], axis=0).T
    rows_ref[:, :WIDE] = wide_ref[0].astype(BF)
    rows_ref[:, WIDE:] = wide_ref[1].astype(BF)


def neighbour(offset):
    u, w, q = lax.axis_index("gx"), lax.axis_index("gy"), lax.axis_index("gz")
    nx, ny = lax.axis_size("gx"), lax.axis_size("gy")
    du, dv, dw = offset
    return ((u + du + nx) % nx, (w + dv + ny) % ny, 1 - q if dw else q)


def halo_copies(msg_ref, into_ref, send_sem, recv_sem):
    copies = []
    for slot, size, offset in message_plan():
        rows = pl.ds(slot_row(slot), size)
        copies.append(pltpu.make_async_remote_copy(
            src_ref=msg_ref.at[rows, :], dst_ref=into_ref.at[rows, :],
            send_sem=send_sem.at[slot], recv_sem=recv_sem.at[slot],
            device_id=neighbour(offset), device_id_type=MESH))
    return copies


def greet_neighbours(barrier):
    for _, _, offset in message_plan():
        pl.semaphore_signal(barrier, inc=1, device_id=neighbour(offset), device_id_type=MESH)


def pick_messages(position, into_ref):
    def bit(size, divisor):
        return jnp.zeros((size, into_ref.shape[1]), jnp.int32) + position // divisor % 2 == 0

    def at(slot):
        return into_ref[pl.ds(slot_row(slot), 64 if slot < 5 else 16), :].astype(F32)

    def two(slot, divisor):
        low = at(slot)
        return jnp.where(bit(low.shape[0], divisor), low, at(slot + 1))

    def four(slot):
        return jnp.where(bit(16, 4), two(slot, 2), two(slot + 2, 2))

    return jnp.concatenate(
        [two(0, 4), two(2, 2), at(4), four(5), two(9, 4), two(11, 2), four(13)], axis=0).astype(BF)


def halo_codes(position, sender):
    u, w, q = (lax.axis_index(axis) for axis in ("gx", "gy", "gz"))
    nx, ny = lax.axis_size("gx"), lax.axis_size("gy")
    own = (position // 4, position // 2 % 2, position % 2)
    theirs = (sender // 4, sender // 2 % 2, sender % 2)
    beyond = (u + 2 * own[0] - 1, w + 2 * own[1] - 1, q + 2 * own[2] - 1)
    sizes = (nx, ny, 2)
    r = lax.broadcasted_iota(jnp.int32, sender.shape, 1)
    face = r < 192
    t = jnp.where(face, r % 64, r % 16)
    high, low = t // 8, t % 8
    past = (
        (r < 64) | ((r >= 192) & (r < 224)) | (r >= 240),
        ((r >= 64) & (r < 128)) | ((r >= 192) & (r < 208)) | (r >= 224),
        ((r >= 128) & (r < 192)) | (r >= 208))
    index = (
        jnp.where(face, high, t),
        jnp.where(r < 64, high, jnp.where(face, low, t)),
        jnp.where(face, low, t))
    valid = face | (t < jnp.where(r < 240, 8, 1))
    spot = []
    for axis in range(3):
        far = 9 * own[axis]
        near = 9 - far
        same = theirs[axis] == own[axis]
        inner = jnp.where(same, 1 + index[axis], near)
        inner_ok = same | (index[axis] == 7 * own[axis])
        there = jnp.zeros_like(r) + beyond[axis]
        outer_ok = (theirs[axis] != own[axis]) & (there >= 0) & (there < sizes[axis])
        spot.append(jnp.where(past[axis], far, inner))
        valid = valid & ((past[axis] & outer_ok) | (jnp.logical_not(past[axis]) & inner_ok))
    return jnp.where(valid, (spot[0] * 10 + spot[1]) * 16 + spot[2], -1)


def build_patch(rows, picked, code, level_ref, patch_refs):
    n = lax.broadcasted_iota(jnp.int32, (800, 256), 0)
    target = n // 8 * 16 + n % 8
    level = lax.broadcasted_iota(jnp.int32, rows.shape, 0) % 8
    for dz in (0, 1, 2):
        pick = jnp.where(target + dz == code, 1.0, 0.0).astype(BF)
        halo = jnp.dot(pick, picked, preferred_element_type=F32)
        if dz == 0:
            mine = jnp.where(level == 0, 0.0, pltpu.roll(rows, 1, 0))
        elif dz == 1:
            mine = rows
        else:
            mine = jnp.where(level == 7, 0.0, pltpu.roll(rows, 511, 0))
        level_ref[...] = halo
        for i in range(8):
            spot = pl.ds(((i + 1) * 10 + 1) * 8, 64)
            level_ref[spot, :] = level_ref[spot, :] + mine[64 * i : 64 * i + 64]
        for part, patch_ref in enumerate(patch_refs):
            for dy in (0, 1, 2):
                tap = dy * 3 + dz
                for x in range(10):
                    patch_ref[pl.ds(64 * x, 64), pl.ds(tap * WIDE, WIDE)] = (
                        level_ref[pl.ds((x * 10 + dy) * 8, 64), pl.ds(part * WIDE, WIDE)].astype(BF))


def convolve(start, patch_ref, weight_ref):
    total = start
    for dx in (0, 1, 2):
        total = total + jnp.dot(patch_ref[pl.ds(64 * dx, 512), :], weight_ref[dx], preferred_element_type=F32)
    return total


def pack_grads(block, store):
    lane = lax.broadcasted_iota(jnp.int32, (C, WIDE), 1)
    for group in range(2):
        last = block(4 * group + 3)
        for t in range(3):
            shifted = pltpu.roll(last, C - 32 * t, 1)
            store(3 * group + t, jnp.where(lane < C, block(4 * group + t), shifted))
    store(6, block(8))


def unpack_grads(load, store):
    lane = lax.broadcasted_iota(jnp.int32, (C, WIDE), 1)
    for group in range(2):
        last = jnp.zeros((C, WIDE), F32)
        for t in range(3):
            tile = load(3 * group + t)
            store(4 * group + t, tile)
            moved = pltpu.roll(tile, 32 + 32 * t, 1)
            last = jnp.where((lane >= 32 * t) & (lane < 32 * t + 32), moved, last)
        store(4 * group + 3, last)
    store(8, load(6))


def square(block):
    gap = WIDE - C
    wide = jnp.concatenate([block.astype(F32), jnp.zeros((C, gap), F32)], axis=1)
    return jnp.concatenate([wide, jnp.zeros((gap, WIDE), F32)], axis=0)


def lay_weights(kernel_ref, weight_ref, turned):
    def step(k, carry):
        rows = pl.ds(pl.multiple_of(k % 9 * WIDE, WIDE), WIDE)
        block = square(kernel_ref[26 - k]).T if turned else square(kernel_ref[k])
        weight_ref[k // 9, rows, :] = block.astype(BF)
        return carry

    lax.fori_loop(0, 27, step, 0)


ROWS = 4096
HALF = ROWS // 2
STRIP = 7 * C
SIDE = HALF // 2
SLAB = SIDE // 4
PIECE = SLAB // 4
PART = 2 * PIECE
CELL = PART // 4


def ring(distance, size):
    return min(distance, size - distance)


ROW = (2, 1, 3)
LINE = sorted(range(1, 16), key=lambda t: -ring(t, 16))


def places():
    u = lax.axis_index("gx")
    w = lax.axis_index("gy")
    q = lax.axis_index("gz")
    core = w % 2
    y = w // 2 % 4
    x = q * 2 + w // 8
    mate = (u, w + 1 - 2 * core, q)

    def at(px, py):
        return u, ((px % 2) * 4 + py) * 2 + core, px // 2

    def x_peer(t):
        return (x + t) % 4, at((x + t) % 4, y)

    def y_peer(t):
        return (y + t) % 4, at(x, (y + t) % 4)

    def near_peer(t):
        r = (u % 4 + t) % 4
        return r, (u // 4 * 4 + r, w, q)

    def line_peer(t):
        return (u + t) % 16, w, q

    return core, x, y, mate, x_peer, y_peer, near_peer, line_peer


def greet_sharers(barrier):
    core, x, y, mate, x_peer, y_peer, near_peer, line_peer = places()
    for t in LINE:
        pl.semaphore_signal(barrier, inc=1, device_id=line_peer(t), device_id_type=MESH)
    for t in ROW:
        pl.semaphore_signal(barrier, inc=1, device_id=x_peer(t)[1], device_id_type=MESH)
        pl.semaphore_signal(barrier, inc=1, device_id=y_peer(t)[1], device_id_type=MESH)
    pl.semaphore_signal(barrier, inc=1, device_id=mate, device_id_type=MESH)


def remote(src, dst, sends, recvs, index, device):
    return pltpu.make_async_remote_copy(
        src_ref=src, dst_ref=dst, send_sem=sends.at[index], recv_sem=recvs.at[index],
        device_id=device, device_id_type=MESH)


def swap_copy(strip, half_out, half_in, swap_send, swap_recv):
    rows = pl.ds(strip * STRIP, STRIP)
    return remote(half_out.at[rows, :], half_in.at[rows, :], swap_send, swap_recv, strip, places()[3])


def start_swap(strip, data_ref, half_out, half_in, swap_send, swap_recv):
    core = places()[0]
    theirs = pl.multiple_of((1 - core) * HALF + strip * STRIP, 16)
    half_out[pl.ds(strip * STRIP, STRIP), :] = data_ref[pl.ds(theirs, STRIP), :]
    swap_copy(strip, half_out, half_in, swap_send, swap_recv).start()


def block(start, size):
    return pl.ds(pl.multiple_of(start, 16), size)


def all_sum(fill_plane, fill_line, data_ref, sum_ref, gathered, half_out, half_in, total, plane_out, slab_in,
            slab_sum, piece_in, near_src, near_in, line_in, own_part, swap_send, swap_recv, slab_send, slab_recv,
            piece_send, piece_recv, near_send, near_recv, line_send, line_recv, piece_send2, piece_recv2,
            slab_send2, slab_recv2, join_send, join_recv):
    core, x, y, mate, x_peer, y_peer, near_peer, line_peer = places()
    u = lax.axis_index("gx")
    own = pl.multiple_of(core * HALF, HALF)
    other = pl.multiple_of((1 - core) * HALF, HALF)

    swaps = [swap_copy(strip, half_out, half_in, swap_send, swap_recv) for strip in range(3)]
    for strip in range(3):
        rows = pl.ds(strip * STRIP, STRIP)
        swaps[strip].wait_recv()
        mine = data_ref[pl.ds(pl.multiple_of(own + strip * STRIP, 16), STRIP), :]
        both = mine + half_in[rows, :]
        total[rows, :] = both
        plane_out[rows, :] = both.astype(BF)
    rest = pl.ds(3 * STRIP, HALF - 3 * STRIP)
    total[rest, :] = jnp.zeros((HALF - 3 * STRIP, WIDE), F32)
    plane_out[rest, :] = jnp.zeros((HALF - 3 * STRIP, WIDE), BF)

    ways = ((y, y_peer, x, x_peer), (x, x_peer, y, y_peer))
    slab_copies, piece_copies = [], []
    for t in ROW:
        for side, (_, first_peer, _, _) in enumerate(ways):
            there, device = first_peer(t)
            slab_copies.append((side, t, remote(
                plane_out.at[block(side * SIDE + there * SLAB, SLAB), :], slab_in.at[side, t],
                slab_send, slab_recv, (side, t), device)))
            slab_copies[-1][2].start()
    fill_plane()
    slab_sums = [total[block(side * SIDE + ways[side][0] * SLAB, SLAB), :] for side in (0, 1)]
    for side, t, copy in reversed(slab_copies):
        copy.wait_recv()
        slab_sums[side] = slab_sums[side] + slab_in[side, t].astype(F32)
    for side in (0, 1):
        slab_sum[side] = slab_sums[side]
    for t in ROW:
        for side, (_, _, _, second_peer) in enumerate(ways):
            there, device = second_peer(t)
            piece_copies.append((side, t, remote(
                slab_sum.at[side, block(there * PIECE, PIECE), :], piece_in.at[side, t],
                piece_send, piece_recv, (side, t), device)))
            piece_copies[-1][2].start()
    pieces = [slab_sum[side, block(ways[side][2] * PIECE, PIECE), :] for side in (0, 1)]
    for side, t, copy in reversed(piece_copies):
        copy.wait_recv()
        pieces[side] = pieces[side] + piece_in[side, t]
    for side in (0, 1):
        near_src[pl.ds(side * PIECE, PIECE), :] = pieces[side]

    def near_copy(t):
        there, device = near_peer(t)
        rows = pl.ds(pl.multiple_of(there * CELL, CELL), CELL)
        return remote(near_src.at[rows, :], near_in.at[t], near_send, near_recv, t, device)

    near_copies = [near_copy(t) for t in (1, 2, 3)]
    for copy in near_copies:
        copy.start()
    cell_sum = near_src[pl.ds(pl.multiple_of(u % 4 * CELL, CELL), CELL), :]
    for t, copy in zip((1, 2, 3), near_copies):
        copy.wait_recv()
        cell_sum = cell_sum + near_in[t]

    line_in[u] = cell_sum.astype(BF)

    def line_copy(t, slot):
        return remote(line_in.at[u], line_in.at[slot], line_send, line_recv, t, line_peer(t))

    line_copies = [line_copy(t, u) for t in LINE]
    for copy in line_copies:
        copy.start()
    fill_line()
    for t in reversed(LINE):
        line_copy(t, (u - t + 16) % 16).wait_recv()
    for r in range(4):
        cells = [line_in[4 * group + r].astype(F32) for group in range(4)]
        own_part[pl.ds(r * CELL, CELL), :] = ((cells[0] + cells[1]) + (cells[2] + cells[3])).astype(BF)

    def slab_rows(base, side, place):
        return block(base + side * SIDE + place * SLAB, SLAB)

    def piece_rows(side, place, inner):
        return block(own + side * SIDE + place * SLAB + inner * PIECE, PIECE)

    def join_copy(rows, index):
        return remote(gathered.at[rows, :], gathered.at[rows, :], join_send, join_recv, index, mate)

    backs, joins = [], []
    for side, (place, _, inner, _) in enumerate(ways):
        gathered[piece_rows(side, place, inner), :] = own_part[pl.ds(side * PIECE, PIECE), :]
    for t in ROW:
        for side, (place, _, inner, second_peer) in enumerate(ways):
            rows = piece_rows(side, place, inner)
            backs.append(remote(own_part.at[pl.ds(side * PIECE, PIECE), :], gathered.at[rows, :],
                                piece_send2, piece_recv2, (side, t), second_peer(t)[1]))
            backs[-1].start()
    for t in reversed(ROW):
        for side, (place, _, inner, second_peer) in enumerate(ways):
            rows = piece_rows(side, place, (inner - t + 4) % 4)
            remote(own_part.at[pl.ds(side * PIECE, PIECE), :], gathered.at[rows, :],
                   piece_send2, piece_recv2, (side, t), second_peer(t)[1]).wait_recv()
    for t in ROW:
        for side, (place, first_peer, _, _) in enumerate(ways):
            rows = slab_rows(own, side, place)
            backs.append(remote(gathered.at[rows, :], gathered.at[rows, :],
                                slab_send2, slab_recv2, (side, t), first_peer(t)[1]))
            backs[-1].start()
    for side in (0, 1):
        joins.append(join_copy(slab_rows(own, side, ways[side][0]), (side, 0)))
        joins[-1].start()
    for t in reversed(ROW):
        for side, (place, first_peer, _, _) in enumerate(ways):
            rows = slab_rows(own, side, (place - t + 4) % 4)
            remote(gathered.at[rows, :], gathered.at[rows, :],
                   slab_send2, slab_recv2, (side, t), first_peer(t)[1]).wait_recv()
            joins.append(join_copy(rows, (side, t)))
            joins[-1].start()
    sum_ref[pl.ds(own, HALF), :] = gathered[pl.ds(own, HALF), :]
    for t in (0, *reversed(ROW)):
        for side in (0, 1):
            rows = slab_rows(other, side, (ways[side][0] - t + 4) % 4)
            join_copy(rows, (side, t)).wait_recv()
            sum_ref[rows, :] = gathered[rows, :]
    reduced = [copy for _, _, copy in slab_copies + piece_copies]
    for copy in [*swaps, *reduced, *near_copies, *line_copies, *backs, *joins]:
        copy.wait_send()


SHARERS = 1 + 6 + 15


def whole_kernel(scale, position_ref, count_ref, x_hbm, g_hbm, code_hbm, first_hbm, second_hbm,
                 out_ref, sum_ref, x_ref, g_ref, code_ref, first_ref, second_ref, load_sem,
                 wide_ref, rows_ref, msg_ref, into_ref, back_msg_ref, back_into_ref,
                 x_weight_ref, g_weight_ref, back_weight_ref, level_ref, x_patch_ref, g_patch_ref,
                 back_level_ref, back_patch_ref, grads_ref, data_ref, delta_ref,
                 send_sem, recv_sem, back_send_sem, back_recv_sem, *reduce_refs):
    q = lax.axis_index("gz")
    position = position_ref[0]
    barrier = pltpu.get_barrier_semaphore()
    greet_sharers(barrier)
    greet_neighbours(barrier)
    loads = [
        pltpu.make_async_copy(src, dst, load_sem.at[i])
        for i, (src, dst) in enumerate((
            (x_hbm, x_ref), (g_hbm, g_ref), (code_hbm, code_ref), (first_hbm, first_ref), (second_hbm, second_ref)))]
    for load in loads:
        load.start()
    for load in loads[:3]:
        load.wait()
    pack_rows(position, count_ref[0], x_ref, g_ref, code_ref, wide_ref, rows_ref)
    pack_messages(wide_ref, msg_ref, q)
    pl.semaphore_wait(barrier, 17 + SHARERS)
    copies = halo_copies(msg_ref, into_ref, send_sem, recv_sem)
    for copy in copies:
        copy.start()
    for load in loads[3:]:
        load.wait()
    lay_weights(first_ref, x_weight_ref, False)
    lay_weights(second_ref, g_weight_ref, True)
    for copy in copies:
        copy.wait()

    rows = rows_ref[...].astype(F32)
    picked = pick_messages(position, into_ref)
    sender = picked[:, :WIDE].astype(F32).T[C : C + 8].astype(jnp.int32)
    code = halo_codes(position, sender)[:1]
    build_patch(rows, picked, code, level_ref, (x_patch_ref, g_patch_ref))
    nothing = jnp.zeros((512, WIDE), F32)
    pre = convolve(nothing, x_patch_ref, x_weight_ref)
    back = convolve(nothing, g_patch_ref, g_weight_ref)
    mask = jnp.broadcast_to(rows[:, C + 1 : C + 2], (512, WIDE))
    sigma = jax.nn.sigmoid(pre)
    hidden = pre * sigma * mask
    delta = (back * sigma * (1.0 + pre * (1.0 - sigma)) * mask).astype(BF)
    delta_ref[...] = delta
    wide_ref[0] = delta.astype(F32)
    back_copies = halo_copies(back_msg_ref, back_into_ref, back_send_sem, back_recv_sem)

    turned = (delta.astype(F32).T[:C].astype(BF), hidden.T[:C].astype(BF))
    for dx in (0, 1, 2):
        for half, patch_ref in ((0, x_patch_ref), (1, g_patch_ref)):
            grads_ref[half] = jnp.dot(
                turned[half], patch_ref[pl.ds(64 * dx, 512), :], preferred_element_type=F32)

            def block(tap):
                return grads_ref[half, :, pl.ds(tap * WIDE, WIDE)] * scale

            def store(tile, value):
                data_ref[pl.ds(half * HALF + dx * STRIP + tile * C, C), :] = value

            pack_grads(block, store)
        start_swap(dx, data_ref, *reduce_refs[1:3], *reduce_refs[12:14])

    def fill_plane():
        pack_messages(wide_ref.at[pl.ds(0, 1)], back_msg_ref, q)
        for copy in back_copies:
            copy.start()
        lay_weights(first_ref, back_weight_ref, True)

    def fill_line():
        for copy in back_copies:
            copy.wait()
        back_picked = pick_messages(position, back_into_ref)
        build_patch(delta_ref[...].astype(F32), back_picked, code, back_level_ref, (back_patch_ref,))
        grad = convolve(rows_ref[:, WIDE:].astype(F32), back_patch_ref, back_weight_ref)
        out_ref[...] = (grad * mask).T[:C].astype(BF)

    all_sum(fill_plane, fill_line, data_ref, sum_ref, *reduce_refs)


def whole(scale, position, count, x, g, codes, first, second):
    sems = lambda *n: pltpu.SemaphoreType.DMA(n)
    taps = 9 * WIDE
    anywhere = pl.BlockSpec(memory_space=pl.ANY)
    return pl.pallas_call(
        functools.partial(whole_kernel, scale),
        out_shape=(pltpu.VMEM((C, 512), BF), pltpu.VMEM((ROWS, WIDE), BF)),
        in_specs=[SMEM, SMEM] + [anywhere] * 5,
        out_specs=(VMEM, VMEM),
        scratch_shapes=[
            pltpu.VMEM((C, 512), BF), pltpu.VMEM((C, 512), BF), pltpu.VMEM((1, 64), jnp.int32),
            pltpu.VMEM((27, C, C), BF), pltpu.VMEM((27, C, C), BF), sems(5),
            pltpu.VMEM((2, 512, WIDE), F32), pltpu.VMEM((512, 2 * WIDE), BF),
            pltpu.VMEM((MSG, 2 * WIDE), BF), pltpu.VMEM((MSG, 2 * WIDE), BF),
            pltpu.VMEM((MSG, WIDE), BF), pltpu.VMEM((MSG, WIDE), BF),
            pltpu.VMEM((3, taps, WIDE), BF), pltpu.VMEM((3, taps, WIDE), BF), pltpu.VMEM((3, taps, WIDE), BF),
            pltpu.VMEM((800, 2 * WIDE), F32), pltpu.VMEM((640, taps), BF), pltpu.VMEM((640, taps), BF),
            pltpu.VMEM((800, WIDE), F32), pltpu.VMEM((640, taps), BF),
            pltpu.VMEM((2, C, taps), F32), pltpu.VMEM((ROWS, WIDE), F32), pltpu.VMEM((512, WIDE), BF),
            sems(17), sems(17), sems(17), sems(17),
            pltpu.VMEM((ROWS, WIDE), BF),
            pltpu.VMEM((HALF, WIDE), F32), pltpu.VMEM((HALF, WIDE), F32),
            pltpu.VMEM((HALF, WIDE), F32), pltpu.VMEM((HALF, WIDE), BF),
            pltpu.VMEM((2, 4, SLAB, WIDE), BF), pltpu.VMEM((2, SLAB, WIDE), F32),
            pltpu.VMEM((2, 4, PIECE, WIDE), F32), pltpu.VMEM((PART, WIDE), F32),
            pltpu.VMEM((4, CELL, WIDE), F32), pltpu.VMEM((16, CELL, WIDE), BF),
            pltpu.VMEM((PART, WIDE), BF),
            sems(3), sems(3), sems(2, 4), sems(2, 4), sems(2, 4), sems(2, 4), sems(4), sems(4), sems(16), sems(16),
            sems(2, 4), sems(2, 4), sems(2, 4), sems(2, 4), sems(2, 4), sems(2, 4),
        ],
        compiler_params=pltpu.CompilerParams(
            collective_id=1, has_side_effects=True, vmem_limit_bytes=48 * 2 ** 20),
        name="whole",
    )(position, count, *(pltpu.with_memory_space_constraint(a, pltpu.HBM) for a in (x, g, codes, first, second)))


def finish_kernel(grad_ref, sum_ref, out_hbm, first_hbm, second_hbm, first_ref, second_ref, out_sem):
    stores = [pltpu.make_async_copy(grad_ref, out_hbm, out_sem.at[6])]
    stores[0].start()
    for dx in (0, 1, 2):
        for half in (0, 1):

            def load(tile):
                return sum_ref[pl.ds(half * HALF + dx * STRIP + tile * C, C), :].astype(F32)

            def store(tap, value):
                if half == 0:
                    first_ref[9 * dx + tap] = value.T[:C]
                else:
                    second_ref[26 - 9 * dx - tap] = value[:, :C]

            unpack_grads(load, store)
            here, there, start = (first_ref, first_hbm, 9 * dx) if half == 0 else (second_ref, second_hbm, 18 - 9 * dx)
            taps = pl.ds(start, 9)
            stores.append(pltpu.make_async_copy(here.at[taps], there.at[taps], out_sem.at[2 * dx + half]))
            stores[-1].start()
    for copy in stores:
        copy.wait()


def finish(grad, summed):
    anywhere = pl.BlockSpec(memory_space=pl.ANY)
    return pl.pallas_call(
        finish_kernel,
        out_shape=(
            jax.ShapeDtypeStruct((C, 512), BF),
            jax.ShapeDtypeStruct((27, C, C), F32), jax.ShapeDtypeStruct((27, C, C), F32)),
        in_specs=[VMEM, VMEM],
        out_specs=(anywhere,) * 3,
        scratch_shapes=[
            pltpu.VMEM((27, C, C), F32), pltpu.VMEM((27, C, C), F32), pltpu.SemaphoreType.DMA((7,))],
        compiler_params=pltpu.CompilerParams(vmem_limit_bytes=16 * 2 ** 20),
        name="finish",
    )(
        pltpu.with_memory_space_constraint(grad, pltpu.VMEM),
        pltpu.with_memory_space_constraint(summed, pltpu.VMEM))


def shards(features, cotangent, first_weight, second_weight, slot_position, brick_count, column_code):
    devices = lax.axis_size("gx") * lax.axis_size("gy") * lax.axis_size("gz")
    scale = float(devices ** -0.5 / 8.0)
    grad, summed = whole(
        scale, slot_position.reshape(1), brick_count.reshape(1), features.reshape(C, 512),
        cotangent.reshape(C, 512), column_code.reshape(1, 64), first_weight, second_weight)
    grad_input, first_grad, second_grad = finish(grad, summed)
    return grad_input.reshape(1, 1, 1, 1, C, 512), first_grad, second_grad


def solution(mesh):
    placed = (
        P("gx", "gy", "gz", None, None, None),
        P("gx", "gy", "gz", None, None, None),
        P(),
        P(),
        P("gx", "gy", "gz", None),
        P("gx", "gy", "gz"),
        P("gx", "gy", "gz", None, None),
    )
    return jax.shard_map(
        shards,
        mesh=mesh,
        in_specs=placed,
        out_specs=(P("gx", "gy", "gz", None, None, None), P(), P()),
        check_vma=False,
    )
```

```python
import functools

import jax
import jax.numpy as jnp
from jax import lax
from jax.experimental import pallas as pl
from jax.experimental.pallas import tpu as pltpu
from jax.sharding import PartitionSpec as P

MESH = pl.DeviceIdType.MESH
VMEM = pl.BlockSpec(memory_space=pltpu.VMEM)
SMEM = pl.BlockSpec(memory_space=pltpu.SMEM)
C = 96
WIDE = 128
MSG = 512
BF = jnp.bfloat16
F32 = jnp.float32


def message_plan():
    plan = []
    for ix in (0, 1):
        for iy in (0, 1):
            plan.append((13 + 2 * ix + iy, 16, (1 - 2 * ix, 1 - 2 * iy, 1)))
    for iy in (0, 1):
        plan.append((11 + iy, 16, (0, 1 - 2 * iy, 1)))
    for ix in (0, 1):
        plan.append((9 + ix, 16, (1 - 2 * ix, 0, 1)))
    for ix in (0, 1):
        for iy in (0, 1):
            plan.append((5 + 2 * ix + iy, 16, (1 - 2 * ix, 1 - 2 * iy, 0)))
    plan.append((4, 64, (0, 0, 1)))
    for iy in (0, 1):
        plan.append((2 + iy, 64, (0, 1 - 2 * iy, 0)))
    for ix in (0, 1):
        plan.append((ix, 64, (1 - 2 * ix, 0, 0)))
    return plan


def slot_row(slot):
    return slot * 64 if slot < 5 else 320 + (slot - 5) * 16


def pack_messages(wide_ref, msg_ref, q):
    blank = jnp.zeros((8, WIDE), F32)
    only = lax.broadcasted_iota(jnp.int32, (8, WIDE), 0) == 0
    for part in range(wide_ref.shape[0]):

        def rows(*spot, **stride):
            return wide_ref[part, pl.ds(*spot, **stride), :]

        def put(slot, value):
            start = slot_row(slot)
            msg_ref[pl.ds(start, value.shape[0]), pl.ds(part * WIDE, WIDE)] = value.astype(BF)

        def side(low, high):
            return jnp.where(q == 0, high, low)

        for ix in (0, 1):
            put(ix, rows(448 * (1 - ix), 64))
        for iy in (0, 1):
            edge = [rows(64 * i + 56 * (1 - iy), 8) for i in range(8)]
            put(2 + iy, jnp.concatenate(edge, axis=0))
        put(4, side(rows(0, 64, stride=8), rows(7, 64, stride=8)))
        for ix in (0, 1):
            x0 = 448 * (1 - ix)
            for iy in (0, 1):
                column = rows(x0 + 56 * (1 - iy), 8)
                put(5 + 2 * ix + iy, jnp.concatenate([column, blank], axis=0))
                corner = side(column, pltpu.roll(column, 1, 0))
                put(13 + 2 * ix + iy, jnp.concatenate([jnp.where(only, corner, 0.0), blank], axis=0))
            line = side(rows(x0, 8, stride=8), rows(x0 + 7, 8, stride=8))
            put(9 + ix, jnp.concatenate([line, blank], axis=0))
        for iy in (0, 1):
            y0 = 56 * (1 - iy)
            line = side(rows(y0, 8, stride=64), rows(y0 + 7, 8, stride=64))
            put(11 + iy, jnp.concatenate([line, blank], axis=0))


def pack_rows(position, count, x_ref, g_ref, code_ref, wide_ref, rows_ref):
    column = lax.broadcasted_iota(jnp.int32, (64, 512), 0)
    voxel = lax.broadcasted_iota(jnp.int32, (64, 512), 1)
    spread = jnp.where(column == voxel // 8, 1.0, 0.0).astype(BF)
    codes = jnp.broadcast_to(code_ref[...].astype(F32), (16, 64)).astype(BF)
    code = jnp.dot(codes, spread, preferred_element_type=F32).astype(jnp.int32)[:8]
    low = code // 8
    level = lax.broadcasted_iota(jnp.int32, (8, 512), 1) % 8
    live = (level >= low) & (level <= low + code % 8) & (count > 0)
    mask = jnp.where(live, 1.0, 0.0)
    first = lax.broadcasted_iota(jnp.int32, (8, 512), 0)
    place = jnp.where(first == 0, position.astype(F32), jnp.where(first == 1, mask, 0.0))
    blank = jnp.zeros((24, 512), F32)
    inside = jnp.broadcast_to(mask[:1], (C, 512)) > 0.0
    x = jnp.where(inside, x_ref[...].astype(F32), 0.0)
    g = jnp.where(inside, g_ref[...].astype(F32), 0.0)
    wide_ref[0] = jnp.concatenate([x, place, blank], axis=0).T
    wide_ref[1] = jnp.concatenate([g, jnp.zeros((32, 512), F32)], axis=0).T
    rows_ref[:, :WIDE] = wide_ref[0].astype(BF)
    rows_ref[:, WIDE:] = wide_ref[1].astype(BF)


def neighbour(offset):
    u, w, q = lax.axis_index("gx"), lax.axis_index("gy"), lax.axis_index("gz")
    nx, ny = lax.axis_size("gx"), lax.axis_size("gy")
    du, dv, dw = offset
    return ((u + du + nx) % nx, (w + dv + ny) % ny, 1 - q if dw else q)


def halo_copies(msg_ref, into_ref, send_sem, recv_sem):
    copies = []
    for slot, size, offset in message_plan():
        rows = pl.ds(slot_row(slot), size)
        copies.append(pltpu.make_async_remote_copy(
            src_ref=msg_ref.at[rows, :], dst_ref=into_ref.at[rows, :],
            send_sem=send_sem.at[slot], recv_sem=recv_sem.at[slot],
            device_id=neighbour(offset), device_id_type=MESH))
    return copies


def greet_neighbours(barrier):
    for _, _, offset in message_plan():
        pl.semaphore_signal(barrier, inc=1, device_id=neighbour(offset), device_id_type=MESH)


def pick_messages(position, into_ref):
    def bit(size, divisor):
        return jnp.zeros((size, into_ref.shape[1]), jnp.int32) + position // divisor % 2 == 0

    def at(slot):
        return into_ref[pl.ds(slot_row(slot), 64 if slot < 5 else 16), :].astype(F32)

    def two(slot, divisor):
        low = at(slot)
        return jnp.where(bit(low.shape[0], divisor), low, at(slot + 1))

    def four(slot):
        return jnp.where(bit(16, 4), two(slot, 2), two(slot + 2, 2))

    return jnp.concatenate(
        [two(0, 4), two(2, 2), at(4), four(5), two(9, 4), two(11, 2), four(13)], axis=0).astype(BF)


def halo_codes(position, sender):
    u, w, q = (lax.axis_index(axis) for axis in ("gx", "gy", "gz"))
    nx, ny = lax.axis_size("gx"), lax.axis_size("gy")
    own = (position // 4, position // 2 % 2, position % 2)
    theirs = (sender // 4, sender // 2 % 2, sender % 2)
    beyond = (u + 2 * own[0] - 1, w + 2 * own[1] - 1, q + 2 * own[2] - 1)
    sizes = (nx, ny, 2)
    r = lax.broadcasted_iota(jnp.int32, sender.shape, 1)
    face = r < 192
    t = jnp.where(face, r % 64, r % 16)
    high, low = t // 8, t % 8
    past = (
        (r < 64) | ((r >= 192) & (r < 224)) | (r >= 240),
        ((r >= 64) & (r < 128)) | ((r >= 192) & (r < 208)) | (r >= 224),
        ((r >= 128) & (r < 192)) | (r >= 208))
    index = (
        jnp.where(face, high, t),
        jnp.where(r < 64, high, jnp.where(face, low, t)),
        jnp.where(face, low, t))
    valid = face | (t < jnp.where(r < 240, 8, 1))
    spot = []
    for axis in range(3):
        far = 9 * own[axis]
        near = 9 - far
        same = theirs[axis] == own[axis]
        inner = jnp.where(same, 1 + index[axis], near)
        inner_ok = same | (index[axis] == 7 * own[axis])
        there = jnp.zeros_like(r) + beyond[axis]
        outer_ok = (theirs[axis] != own[axis]) & (there >= 0) & (there < sizes[axis])
        spot.append(jnp.where(past[axis], far, inner))
        valid = valid & ((past[axis] & outer_ok) | (jnp.logical_not(past[axis]) & inner_ok))
    return jnp.where(valid, (spot[0] * 10 + spot[1]) * 16 + spot[2], -1)


def build_patch(rows, picked, code, level_ref, patch_refs):
    n = lax.broadcasted_iota(jnp.int32, (800, 256), 0)
    target = n // 8 * 16 + n % 8
    level = lax.broadcasted_iota(jnp.int32, rows.shape, 0) % 8
    for dz in (0, 1, 2):
        pick = jnp.where(target + dz == code, 1.0, 0.0).astype(BF)
        halo = jnp.dot(pick, picked, preferred_element_type=F32)
        if dz == 0:
            mine = jnp.where(level == 0, 0.0, pltpu.roll(rows, 1, 0))
        elif dz == 1:
            mine = rows
        else:
            mine = jnp.where(level == 7, 0.0, pltpu.roll(rows, 511, 0))
        level_ref[...] = halo
        for i in range(8):
            spot = pl.ds(((i + 1) * 10 + 1) * 8, 64)
            level_ref[spot, :] = level_ref[spot, :] + mine[64 * i : 64 * i + 64]
        for part, patch_ref in enumerate(patch_refs):
            for dy in (0, 1, 2):
                tap = dy * 3 + dz
                for x in range(10):
                    patch_ref[pl.ds(64 * x, 64), pl.ds(tap * WIDE, WIDE)] = (
                        level_ref[pl.ds((x * 10 + dy) * 8, 64), pl.ds(part * WIDE, WIDE)].astype(BF))


def convolve(start, patch_ref, weight_ref):
    total = start
    for dx in (0, 1, 2):
        total = total + jnp.dot(patch_ref[pl.ds(64 * dx, 512), :], weight_ref[dx], preferred_element_type=F32)
    return total


def pack_grads(block, store):
    lane = lax.broadcasted_iota(jnp.int32, (C, WIDE), 1)
    for group in range(2):
        last = block(4 * group + 3)
        for t in range(3):
            shifted = pltpu.roll(last, C - 32 * t, 1)
            store(3 * group + t, jnp.where(lane < C, block(4 * group + t), shifted))
    store(6, block(8))


def unpack_grads(load, store):
    lane = lax.broadcasted_iota(jnp.int32, (C, WIDE), 1)
    for group in range(2):
        last = jnp.zeros((C, WIDE), F32)
        for t in range(3):
            tile = load(3 * group + t)
            store(4 * group + t, tile)
            moved = pltpu.roll(tile, 32 + 32 * t, 1)
            last = jnp.where((lane >= 32 * t) & (lane < 32 * t + 32), moved, last)
        store(4 * group + 3, last)
    store(8, load(6))


def square(block):
    gap = WIDE - C
    wide = jnp.concatenate([block.astype(F32), jnp.zeros((C, gap), F32)], axis=1)
    return jnp.concatenate([wide, jnp.zeros((gap, WIDE), F32)], axis=0)


def lay_weights(kernel_ref, weight_ref, turned):
    def step(k, carry):
        rows = pl.ds(pl.multiple_of(k % 9 * WIDE, WIDE), WIDE)
        block = square(kernel_ref[26 - k]).T if turned else square(kernel_ref[k])
        weight_ref[k // 9, rows, :] = block.astype(BF)
        return carry

    lax.fori_loop(0, 27, step, 0)


ROWS = 4096
HALF = ROWS // 2
STRIP = 7 * C
PART = HALF // 16
CELL = PART // 4


def ring(distance, size):
    return min(distance, size - distance)


PLANE = sorted(range(1, 16), key=lambda t: -ring(t // 4, 4) - ring(t % 4, 4))
LINE = sorted(range(1, 16), key=lambda t: -ring(t, 16))


def places():
    u = lax.axis_index("gx")
    w = lax.axis_index("gy")
    q = lax.axis_index("gz")
    core = w % 2
    y = w // 2 % 4
    x = q * 2 + w // 8
    mate = (u, w + 1 - 2 * core, q)

    def plane_peer(t):
        px = (x + t // 4) % 4
        py = (y + t % 4) % 4
        return px * 4 + py, (u, ((px % 2) * 4 + py) * 2 + core, px // 2)

    def near_peer(t):
        r = (u % 4 + t) % 4
        return r, (u // 4 * 4 + r, w, q)

    def line_peer(t):
        return (u + t) % 16, w, q

    return core, x, y, mate, plane_peer, near_peer, line_peer


def greet_sharers(barrier):
    core, x, y, mate, plane_peer, near_peer, line_peer = places()
    for t in LINE:
        pl.semaphore_signal(barrier, inc=1, device_id=line_peer(t), device_id_type=MESH)
    for t in PLANE:
        pl.semaphore_signal(barrier, inc=1, device_id=plane_peer(t)[1], device_id_type=MESH)
    pl.semaphore_signal(barrier, inc=1, device_id=mate, device_id_type=MESH)


def remote(src, dst, sends, recvs, index, device):
    return pltpu.make_async_remote_copy(
        src_ref=src, dst_ref=dst, send_sem=sends.at[index], recv_sem=recvs.at[index],
        device_id=device, device_id_type=MESH)


def swap_copy(strip, half_out, half_in, swap_send, swap_recv):
    rows = pl.ds(strip * STRIP, STRIP)
    return remote(half_out.at[rows, :], half_in.at[rows, :], swap_send, swap_recv, strip, places()[3])


def start_swap(strip, data_ref, half_out, half_in, swap_send, swap_recv):
    core = places()[0]
    theirs = pl.multiple_of((1 - core) * HALF + strip * STRIP, 16)
    half_out[pl.ds(strip * STRIP, STRIP), :] = data_ref[pl.ds(theirs, STRIP), :]
    swap_copy(strip, half_out, half_in, swap_send, swap_recv).start()


def all_sum(fill_plane, fill_line, data_ref, sum_ref, gathered, half_out, half_in, total, plane_out, plane_in,
            near_src, near_in, line_in, own_part, swap_send, swap_recv, plane_send, plane_recv,
            near_send, near_recv, line_send, line_recv, plane_send2, plane_recv2,
            join_send, join_recv):
    core, x, y, mate, plane_peer, near_peer, line_peer = places()
    u = lax.axis_index("gx")
    chip = x * 4 + y
    own = pl.multiple_of(core * HALF, HALF)
    other = pl.multiple_of((1 - core) * HALF, HALF)

    swaps = [swap_copy(strip, half_out, half_in, swap_send, swap_recv) for strip in range(3)]
    for strip in range(3):
        rows = pl.ds(strip * STRIP, STRIP)
        swaps[strip].wait_recv()
        mine = data_ref[pl.ds(pl.multiple_of(own + strip * STRIP, 16), STRIP), :]
        both = mine + half_in[rows, :]
        total[rows, :] = both
        plane_out[rows, :] = both.astype(BF)
    rest = pl.ds(3 * STRIP, HALF - 3 * STRIP)
    total[rest, :] = jnp.zeros((HALF - 3 * STRIP, WIDE), F32)
    plane_out[rest, :] = jnp.zeros((HALF - 3 * STRIP, WIDE), BF)

    def plane_copy(t):
        there, device = plane_peer(t)
        rows = pl.ds(pl.multiple_of(there * PART, PART), PART)
        return remote(plane_out.at[rows, :], plane_in.at[t], plane_send, plane_recv, t, device)

    plane_copies = [plane_copy(t) for t in PLANE]
    for copy in plane_copies:
        copy.start()
    fill_plane()
    part = pl.multiple_of(chip * PART, PART)
    part_sum = total[pl.ds(part, PART), :]
    for t, copy in zip(reversed(PLANE), reversed(plane_copies)):
        copy.wait_recv()
        part_sum = part_sum + plane_in[t].astype(F32)
    near_src[...] = part_sum

    def near_copy(t):
        there, device = near_peer(t)
        rows = pl.ds(pl.multiple_of(there * CELL, CELL), CELL)
        return remote(near_src.at[rows, :], near_in.at[t], near_send, near_recv, t, device)

    near_copies = [near_copy(t) for t in (1, 2, 3)]
    for copy in near_copies:
        copy.start()
    cell_sum = near_src[pl.ds(pl.multiple_of(u % 4 * CELL, CELL), CELL), :]
    for t, copy in zip((1, 2, 3), near_copies):
        copy.wait_recv()
        cell_sum = cell_sum + near_in[t]

    line_in[u] = cell_sum.astype(BF)

    def line_copy(t, slot):
        return remote(line_in.at[u], line_in.at[slot], line_send, line_recv, t, line_peer(t))

    line_copies = [line_copy(t, u) for t in LINE]
    for copy in line_copies:
        copy.start()
    fill_line()
    for t in reversed(LINE):
        line_copy(t, (u - t + 16) % 16).wait_recv()
    for r in range(4):
        cells = [line_in[4 * group + r].astype(F32) for group in range(4)]
        own_part[pl.ds(r * CELL, CELL), :] = ((cells[0] + cells[1]) + (cells[2] + cells[3])).astype(BF)

    place = pl.multiple_of(own + part, PART)

    def plane_back(t):
        return remote(own_part, gathered.at[pl.ds(place, PART), :], plane_send2, plane_recv2, t, plane_peer(t)[1])

    def source_rows(t, base):
        px = (x - t // 4 + 4) % 4
        py = (y - t % 4 + 4) % 4
        return pl.ds(pl.multiple_of(base + (px * 4 + py) * PART, PART), PART)

    def plane_arrive(t):
        return remote(own_part, gathered.at[source_rows(t, own), :], plane_send2, plane_recv2, t, plane_peer(t)[1])

    def join_copy(t, base):
        rows = source_rows(t, base)
        return remote(gathered.at[rows, :], gathered.at[rows, :], join_send, join_recv, t, mate)

    backs = [plane_back(t) for t in PLANE]
    for copy in backs:
        copy.start()
    gathered[pl.ds(place, PART), :] = own_part[...]
    joins = [join_copy(0, own)]
    joins[0].start()
    for t in reversed(PLANE):
        plane_arrive(t).wait_recv()
        joins.append(join_copy(t, own))
        joins[-1].start()
    sum_ref[pl.ds(own, HALF), :] = gathered[pl.ds(own, HALF), :]
    for t in [0, *reversed(PLANE)]:
        join_copy(t, other).wait_recv()
    sum_ref[pl.ds(other, HALF), :] = gathered[pl.ds(other, HALF), :]
    for copy in [*swaps, *plane_copies, *near_copies, *line_copies, *backs, *joins]:
        copy.wait_send()


SHARERS = 1 + 15 + 15


def whole_kernel(scale, position_ref, count_ref, x_hbm, g_hbm, code_hbm, first_hbm, second_hbm,
                 out_ref, sum_ref, x_ref, g_ref, code_ref, first_ref, second_ref, load_sem,
                 wide_ref, rows_ref, msg_ref, into_ref, back_msg_ref, back_into_ref,
                 x_weight_ref, g_weight_ref, back_weight_ref, level_ref, x_patch_ref, g_patch_ref,
                 back_level_ref, back_patch_ref, grads_ref, data_ref, delta_ref,
                 send_sem, recv_sem, back_send_sem, back_recv_sem, *reduce_refs):
    q = lax.axis_index("gz")
    position = position_ref[0]
    barrier = pltpu.get_barrier_semaphore()
    greet_sharers(barrier)
    greet_neighbours(barrier)
    loads = [
        pltpu.make_async_copy(src, dst, load_sem.at[i])
        for i, (src, dst) in enumerate((
            (x_hbm, x_ref), (g_hbm, g_ref), (code_hbm, code_ref), (first_hbm, first_ref), (second_hbm, second_ref)))]
    for load in loads:
        load.start()
    for load in loads[:3]:
        load.wait()
    pack_rows(position, count_ref[0], x_ref, g_ref, code_ref, wide_ref, rows_ref)
    pack_messages(wide_ref, msg_ref, q)
    pl.semaphore_wait(barrier, 17 + SHARERS)
    copies = halo_copies(msg_ref, into_ref, send_sem, recv_sem)
    for copy in copies:
        copy.start()
    for load in loads[3:]:
        load.wait()
    lay_weights(first_ref, x_weight_ref, False)
    lay_weights(second_ref, g_weight_ref, True)
    for copy in copies:
        copy.wait()

    rows = rows_ref[...].astype(F32)
    picked = pick_messages(position, into_ref)
    sender = picked[:, :WIDE].astype(F32).T[C : C + 8].astype(jnp.int32)
    code = halo_codes(position, sender)[:1]
    build_patch(rows, picked, code, level_ref, (x_patch_ref, g_patch_ref))
    nothing = jnp.zeros((512, WIDE), F32)
    pre = convolve(nothing, x_patch_ref, x_weight_ref)
    back = convolve(nothing, g_patch_ref, g_weight_ref)
    mask = jnp.broadcast_to(rows[:, C + 1 : C + 2], (512, WIDE))
    sigma = jax.nn.sigmoid(pre)
    hidden = pre * sigma * mask
    delta = (back * sigma * (1.0 + pre * (1.0 - sigma)) * mask).astype(BF)
    delta_ref[...] = delta
    wide_ref[0] = delta.astype(F32)
    back_copies = halo_copies(back_msg_ref, back_into_ref, back_send_sem, back_recv_sem)

    turned = (delta.astype(F32).T[:C].astype(BF), hidden.T[:C].astype(BF))
    for dx in (0, 1, 2):
        for half, patch_ref in ((0, x_patch_ref), (1, g_patch_ref)):
            grads_ref[half] = jnp.dot(
                turned[half], patch_ref[pl.ds(64 * dx, 512), :], preferred_element_type=F32)

            def block(tap):
                return grads_ref[half, :, pl.ds(tap * WIDE, WIDE)] * scale

            def store(tile, value):
                data_ref[pl.ds(half * HALF + dx * STRIP + tile * C, C), :] = value

            pack_grads(block, store)
        start_swap(dx, data_ref, *reduce_refs[1:3], *reduce_refs[10:12])

    def fill_plane():
        pack_messages(wide_ref.at[pl.ds(0, 1)], back_msg_ref, q)
        for copy in back_copies:
            copy.start()
        lay_weights(first_ref, back_weight_ref, True)

    def fill_line():
        for copy in back_copies:
            copy.wait()
        back_picked = pick_messages(position, back_into_ref)
        build_patch(delta_ref[...].astype(F32), back_picked, code, back_level_ref, (back_patch_ref,))
        grad = convolve(rows_ref[:, WIDE:].astype(F32), back_patch_ref, back_weight_ref)
        out_ref[...] = (grad * mask).T[:C].astype(BF)

    all_sum(fill_plane, fill_line, data_ref, sum_ref, *reduce_refs)


def whole(scale, position, count, x, g, codes, first, second):
    sems = lambda n: pltpu.SemaphoreType.DMA((n,))
    taps = 9 * WIDE
    anywhere = pl.BlockSpec(memory_space=pl.ANY)
    return pl.pallas_call(
        functools.partial(whole_kernel, scale),
        out_shape=(pltpu.VMEM((C, 512), BF), pltpu.VMEM((ROWS, WIDE), BF)),
        in_specs=[SMEM, SMEM] + [anywhere] * 5,
        out_specs=(VMEM, VMEM),
        scratch_shapes=[
            pltpu.VMEM((C, 512), BF), pltpu.VMEM((C, 512), BF), pltpu.VMEM((1, 64), jnp.int32),
            pltpu.VMEM((27, C, C), BF), pltpu.VMEM((27, C, C), BF), sems(5),
            pltpu.VMEM((2, 512, WIDE), F32), pltpu.VMEM((512, 2 * WIDE), BF),
            pltpu.VMEM((MSG, 2 * WIDE), BF), pltpu.VMEM((MSG, 2 * WIDE), BF),
            pltpu.VMEM((MSG, WIDE), BF), pltpu.VMEM((MSG, WIDE), BF),
            pltpu.VMEM((3, taps, WIDE), BF), pltpu.VMEM((3, taps, WIDE), BF), pltpu.VMEM((3, taps, WIDE), BF),
            pltpu.VMEM((800, 2 * WIDE), F32), pltpu.VMEM((640, taps), BF), pltpu.VMEM((640, taps), BF),
            pltpu.VMEM((800, WIDE), F32), pltpu.VMEM((640, taps), BF),
            pltpu.VMEM((2, C, taps), F32), pltpu.VMEM((ROWS, WIDE), F32), pltpu.VMEM((512, WIDE), BF),
            sems(17), sems(17), sems(17), sems(17),
            pltpu.VMEM((ROWS, WIDE), BF),
            pltpu.VMEM((HALF, WIDE), F32), pltpu.VMEM((HALF, WIDE), F32),
            pltpu.VMEM((HALF, WIDE), F32), pltpu.VMEM((HALF, WIDE), BF),
            pltpu.VMEM((16, PART, WIDE), BF), pltpu.VMEM((PART, WIDE), F32),
            pltpu.VMEM((4, CELL, WIDE), F32), pltpu.VMEM((16, CELL, WIDE), BF),
            pltpu.VMEM((PART, WIDE), BF),
            sems(3), sems(3), sems(16), sems(16), sems(4), sems(4), sems(16), sems(16),
            sems(16), sems(16), sems(16), sems(16),
        ],
        compiler_params=pltpu.CompilerParams(
            collective_id=1, has_side_effects=True, vmem_limit_bytes=48 * 2 ** 20),
        name="whole",
    )(position, count, *(pltpu.with_memory_space_constraint(a, pltpu.HBM) for a in (x, g, codes, first, second)))


def finish_kernel(grad_ref, sum_ref, out_hbm, first_hbm, second_hbm, first_ref, second_ref, out_sem):
    stores = [pltpu.make_async_copy(grad_ref, out_hbm, out_sem.at[6])]
    stores[0].start()
    for dx in (0, 1, 2):
        for half in (0, 1):

            def load(tile):
                return sum_ref[pl.ds(half * HALF + dx * STRIP + tile * C, C), :].astype(F32)

            def store(tap, value):
                if half == 0:
                    first_ref[9 * dx + tap] = value.T[:C]
                else:
                    second_ref[26 - 9 * dx - tap] = value[:, :C]

            unpack_grads(load, store)
            here, there, start = (first_ref, first_hbm, 9 * dx) if half == 0 else (second_ref, second_hbm, 18 - 9 * dx)
            taps = pl.ds(start, 9)
            stores.append(pltpu.make_async_copy(here.at[taps], there.at[taps], out_sem.at[2 * dx + half]))
            stores[-1].start()
    for copy in stores:
        copy.wait()


def finish(grad, summed):
    anywhere = pl.BlockSpec(memory_space=pl.ANY)
    return pl.pallas_call(
        finish_kernel,
        out_shape=(
            jax.ShapeDtypeStruct((C, 512), BF),
            jax.ShapeDtypeStruct((27, C, C), F32), jax.ShapeDtypeStruct((27, C, C), F32)),
        in_specs=[VMEM, VMEM],
        out_specs=(anywhere,) * 3,
        scratch_shapes=[
            pltpu.VMEM((27, C, C), F32), pltpu.VMEM((27, C, C), F32), pltpu.SemaphoreType.DMA((7,))],
        compiler_params=pltpu.CompilerParams(vmem_limit_bytes=16 * 2 ** 20),
        name="finish",
    )(
        pltpu.with_memory_space_constraint(grad, pltpu.VMEM),
        pltpu.with_memory_space_constraint(summed, pltpu.VMEM))


def shards(features, cotangent, first_weight, second_weight, slot_position, brick_count, column_code):
    devices = lax.axis_size("gx") * lax.axis_size("gy") * lax.axis_size("gz")
    scale = float(devices ** -0.5 / 8.0)
    grad, summed = whole(
        scale, slot_position.reshape(1), brick_count.reshape(1), features.reshape(C, 512),
        cotangent.reshape(C, 512), column_code.reshape(1, 64), first_weight, second_weight)
    grad_input, first_grad, second_grad = finish(grad, summed)
    return grad_input.reshape(1, 1, 1, 1, C, 512), first_grad, second_grad


def solution(mesh):
    placed = (
        P("gx", "gy", "gz", None, None, None),
        P("gx", "gy", "gz", None, None, None),
        P(),
        P(),
        P("gx", "gy", "gz", None),
        P("gx", "gy", "gz"),
        P("gx", "gy", "gz", None, None),
    )
    return jax.shard_map(
        shards,
        mesh=mesh,
        in_specs=placed,
        out_specs=(P("gx", "gy", "gz", None, None, None), P(), P()),
        check_vma=False,
    )
```

```python
import functools

import jax
import jax.numpy as jnp
from jax import lax
from jax.experimental import pallas as pl
from jax.experimental.pallas import tpu as pltpu
from jax.sharding import PartitionSpec as P

MESH = pl.DeviceIdType.MESH
VMEM = pl.BlockSpec(memory_space=pltpu.VMEM)
SMEM = pl.BlockSpec(memory_space=pltpu.SMEM)
C = 96
WIDE = 128
MSG = 512
BF = jnp.bfloat16
F32 = jnp.float32


def message_plan():
    plan = []
    for ix in (0, 1):
        for iy in (0, 1):
            plan.append((13 + 2 * ix + iy, 16, (1 - 2 * ix, 1 - 2 * iy, 1)))
    for iy in (0, 1):
        plan.append((11 + iy, 16, (0, 1 - 2 * iy, 1)))
    for ix in (0, 1):
        plan.append((9 + ix, 16, (1 - 2 * ix, 0, 1)))
    for ix in (0, 1):
        for iy in (0, 1):
            plan.append((5 + 2 * ix + iy, 16, (1 - 2 * ix, 1 - 2 * iy, 0)))
    plan.append((4, 64, (0, 0, 1)))
    for iy in (0, 1):
        plan.append((2 + iy, 64, (0, 1 - 2 * iy, 0)))
    for ix in (0, 1):
        plan.append((ix, 64, (1 - 2 * ix, 0, 0)))
    return plan


def slot_row(slot):
    return slot * 64 if slot < 5 else 320 + (slot - 5) * 16


def pack_messages(wide_ref, msg_ref, q):
    blank = jnp.zeros((8, WIDE), F32)
    only = lax.broadcasted_iota(jnp.int32, (8, WIDE), 0) == 0
    for part in range(wide_ref.shape[0]):

        def rows(*spot, **stride):
            return wide_ref[part, pl.ds(*spot, **stride), :]

        def put(slot, value):
            start = slot_row(slot)
            msg_ref[pl.ds(start, value.shape[0]), pl.ds(part * WIDE, WIDE)] = value.astype(BF)

        def side(low, high):
            return jnp.where(q == 0, high, low)

        for ix in (0, 1):
            put(ix, rows(448 * (1 - ix), 64))
        for iy in (0, 1):
            edge = [rows(64 * i + 56 * (1 - iy), 8) for i in range(8)]
            put(2 + iy, jnp.concatenate(edge, axis=0))
        put(4, side(rows(0, 64, stride=8), rows(7, 64, stride=8)))
        for ix in (0, 1):
            x0 = 448 * (1 - ix)
            for iy in (0, 1):
                column = rows(x0 + 56 * (1 - iy), 8)
                put(5 + 2 * ix + iy, jnp.concatenate([column, blank], axis=0))
                corner = side(column, pltpu.roll(column, 1, 0))
                put(13 + 2 * ix + iy, jnp.concatenate([jnp.where(only, corner, 0.0), blank], axis=0))
            line = side(rows(x0, 8, stride=8), rows(x0 + 7, 8, stride=8))
            put(9 + ix, jnp.concatenate([line, blank], axis=0))
        for iy in (0, 1):
            y0 = 56 * (1 - iy)
            line = side(rows(y0, 8, stride=64), rows(y0 + 7, 8, stride=64))
            put(11 + iy, jnp.concatenate([line, blank], axis=0))


def pack_rows(position, count, x_ref, g_ref, code_ref, wide_ref, rows_ref):
    column = lax.broadcasted_iota(jnp.int32, (64, 512), 0)
    voxel = lax.broadcasted_iota(jnp.int32, (64, 512), 1)
    spread = jnp.where(column == voxel // 8, 1.0, 0.0).astype(BF)
    codes = jnp.broadcast_to(code_ref[...].astype(F32), (16, 64)).astype(BF)
    code = jnp.dot(codes, spread, preferred_element_type=F32).astype(jnp.int32)[:8]
    low = code // 8
    level = lax.broadcasted_iota(jnp.int32, (8, 512), 1) % 8
    live = (level >= low) & (level <= low + code % 8) & (count > 0)
    mask = jnp.where(live, 1.0, 0.0)
    first = lax.broadcasted_iota(jnp.int32, (8, 512), 0)
    place = jnp.where(first == 0, position.astype(F32), jnp.where(first == 1, mask, 0.0))
    blank = jnp.zeros((24, 512), F32)
    inside = jnp.broadcast_to(mask[:1], (C, 512)) > 0.0
    x = jnp.where(inside, x_ref[...].astype(F32), 0.0)
    g = jnp.where(inside, g_ref[...].astype(F32), 0.0)
    wide_ref[0] = jnp.concatenate([x, place, blank], axis=0).T
    wide_ref[1] = jnp.concatenate([g, jnp.zeros((32, 512), F32)], axis=0).T
    rows_ref[:, :WIDE] = wide_ref[0].astype(BF)
    rows_ref[:, WIDE:] = wide_ref[1].astype(BF)


def neighbour(offset):
    u, w, q = lax.axis_index("gx"), lax.axis_index("gy"), lax.axis_index("gz")
    nx, ny = lax.axis_size("gx"), lax.axis_size("gy")
    du, dv, dw = offset
    return ((u + du + nx) % nx, (w + dv + ny) % ny, 1 - q if dw else q)


def halo_copies(msg_ref, into_ref, send_sem, recv_sem):
    copies = []
    for slot, size, offset in message_plan():
        rows = pl.ds(slot_row(slot), size)
        copies.append(pltpu.make_async_remote_copy(
            src_ref=msg_ref.at[rows, :], dst_ref=into_ref.at[rows, :],
            send_sem=send_sem.at[slot], recv_sem=recv_sem.at[slot],
            device_id=neighbour(offset), device_id_type=MESH))
    return copies


def greet_neighbours(barrier):
    for _, _, offset in message_plan():
        pl.semaphore_signal(barrier, inc=1, device_id=neighbour(offset), device_id_type=MESH)


def pick_messages(position, into_ref):
    def bit(size, divisor):
        return jnp.zeros((size, into_ref.shape[1]), jnp.int32) + position // divisor % 2 == 0

    def at(slot):
        return into_ref[pl.ds(slot_row(slot), 64 if slot < 5 else 16), :].astype(F32)

    def two(slot, divisor):
        low = at(slot)
        return jnp.where(bit(low.shape[0], divisor), low, at(slot + 1))

    def four(slot):
        return jnp.where(bit(16, 4), two(slot, 2), two(slot + 2, 2))

    return jnp.concatenate(
        [two(0, 4), two(2, 2), at(4), four(5), two(9, 4), two(11, 2), four(13)], axis=0).astype(BF)


def halo_codes(position, sender):
    u, w, q = (lax.axis_index(axis) for axis in ("gx", "gy", "gz"))
    nx, ny = lax.axis_size("gx"), lax.axis_size("gy")
    own = (position // 4, position // 2 % 2, position % 2)
    theirs = (sender // 4, sender // 2 % 2, sender % 2)
    beyond = (u + 2 * own[0] - 1, w + 2 * own[1] - 1, q + 2 * own[2] - 1)
    sizes = (nx, ny, 2)
    r = lax.broadcasted_iota(jnp.int32, sender.shape, 1)
    face = r < 192
    t = jnp.where(face, r % 64, r % 16)
    high, low = t // 8, t % 8
    past = (
        (r < 64) | ((r >= 192) & (r < 224)) | (r >= 240),
        ((r >= 64) & (r < 128)) | ((r >= 192) & (r < 208)) | (r >= 224),
        ((r >= 128) & (r < 192)) | (r >= 208))
    index = (
        jnp.where(face, high, t),
        jnp.where(r < 64, high, jnp.where(face, low, t)),
        jnp.where(face, low, t))
    valid = face | (t < jnp.where(r < 240, 8, 1))
    spot = []
    for axis in range(3):
        far = 9 * own[axis]
        near = 9 - far
        same = theirs[axis] == own[axis]
        inner = jnp.where(same, 1 + index[axis], near)
        inner_ok = same | (index[axis] == 7 * own[axis])
        there = jnp.zeros_like(r) + beyond[axis]
        outer_ok = (theirs[axis] != own[axis]) & (there >= 0) & (there < sizes[axis])
        spot.append(jnp.where(past[axis], far, inner))
        valid = valid & ((past[axis] & outer_ok) | (jnp.logical_not(past[axis]) & inner_ok))
    return jnp.where(valid, (spot[0] * 10 + spot[1]) * 16 + spot[2], -1)


def build_patch(rows, picked, code, level_ref, patch_refs):
    n = lax.broadcasted_iota(jnp.int32, (800, 256), 0)
    target = n // 8 * 16 + n % 8
    level = lax.broadcasted_iota(jnp.int32, rows.shape, 0) % 8
    for dz in (0, 1, 2):
        pick = jnp.where(target + dz == code, 1.0, 0.0).astype(BF)
        halo = jnp.dot(pick, picked, preferred_element_type=F32)
        if dz == 0:
            mine = jnp.where(level == 0, 0.0, pltpu.roll(rows, 1, 0))
        elif dz == 1:
            mine = rows
        else:
            mine = jnp.where(level == 7, 0.0, pltpu.roll(rows, 511, 0))
        level_ref[...] = halo
        for i in range(8):
            spot = pl.ds(((i + 1) * 10 + 1) * 8, 64)
            level_ref[spot, :] = level_ref[spot, :] + mine[64 * i : 64 * i + 64]
        for part, patch_ref in enumerate(patch_refs):
            for dy in (0, 1, 2):
                tap = dy * 3 + dz
                for x in range(10):
                    patch_ref[pl.ds(64 * x, 64), pl.ds(tap * WIDE, WIDE)] = (
                        level_ref[pl.ds((x * 10 + dy) * 8, 64), pl.ds(part * WIDE, WIDE)].astype(BF))


def convolve(start, patch_ref, weight_ref):
    total = start
    for dx in (0, 1, 2):
        total = total + jnp.dot(patch_ref[pl.ds(64 * dx, 512), :], weight_ref[dx], preferred_element_type=F32)
    return total


def pack_grads(block, store):
    lane = lax.broadcasted_iota(jnp.int32, (C, WIDE), 1)
    for group in range(2):
        last = block(4 * group + 3)
        for t in range(3):
            shifted = pltpu.roll(last, C - 32 * t, 1)
            store(3 * group + t, jnp.where(lane < C, block(4 * group + t), shifted))
    store(6, block(8))


def unpack_grads(load, store):
    lane = lax.broadcasted_iota(jnp.int32, (C, WIDE), 1)
    for group in range(2):
        last = jnp.zeros((C, WIDE), F32)
        for t in range(3):
            tile = load(3 * group + t)
            store(4 * group + t, tile)
            moved = pltpu.roll(tile, 32 + 32 * t, 1)
            last = jnp.where((lane >= 32 * t) & (lane < 32 * t + 32), moved, last)
        store(4 * group + 3, last)
    store(8, load(6))


def square(block):
    gap = WIDE - C
    wide = jnp.concatenate([block.astype(F32), jnp.zeros((C, gap), F32)], axis=1)
    return jnp.concatenate([wide, jnp.zeros((gap, WIDE), F32)], axis=0)


def lay_weights(kernel_ref, weight_ref, turned):
    def step(k, carry):
        rows = pl.ds(pl.multiple_of(k % 9 * WIDE, WIDE), WIDE)
        block = square(kernel_ref[26 - k]).T if turned else square(kernel_ref[k])
        weight_ref[k // 9, rows, :] = block.astype(BF)
        return carry

    lax.fori_loop(0, 27, step, 0)


ROWS = 4096
HALF = ROWS // 2
STRIP = 7 * C
PART = HALF // 16
CELL = PART // 4


def ring(distance, size):
    return min(distance, size - distance)


PLANE = sorted(range(1, 16), key=lambda t: -ring(t // 4, 4) - ring(t % 4, 4))
LINE = sorted(range(1, 16), key=lambda t: -ring(t, 16))


def places():
    u = lax.axis_index("gx")
    w = lax.axis_index("gy")
    q = lax.axis_index("gz")
    core = w % 2
    y = w // 2 % 4
    x = q * 2 + w // 8
    mate = (u, w + 1 - 2 * core, q)

    def plane_peer(t):
        px = (x + t // 4) % 4
        py = (y + t % 4) % 4
        return px * 4 + py, (u, ((px % 2) * 4 + py) * 2 + core, px // 2)

    def near_peer(t):
        r = (u % 4 + t) % 4
        return r, (u // 4 * 4 + r, w, q)

    def line_peer(t):
        return (u + t) % 16, w, q

    return core, x, y, mate, plane_peer, near_peer, line_peer


def greet_sharers(barrier):
    core, x, y, mate, plane_peer, near_peer, line_peer = places()
    for t in LINE:
        pl.semaphore_signal(barrier, inc=1, device_id=line_peer(t), device_id_type=MESH)
    for t in PLANE:
        pl.semaphore_signal(barrier, inc=1, device_id=plane_peer(t)[1], device_id_type=MESH)
    pl.semaphore_signal(barrier, inc=1, device_id=mate, device_id_type=MESH)


def remote(src, dst, sends, recvs, index, device):
    return pltpu.make_async_remote_copy(
        src_ref=src, dst_ref=dst, send_sem=sends.at[index], recv_sem=recvs.at[index],
        device_id=device, device_id_type=MESH)


def swap_copy(strip, half_out, half_in, swap_send, swap_recv):
    rows = pl.ds(strip * STRIP, STRIP)
    return remote(half_out.at[rows, :], half_in.at[rows, :], swap_send, swap_recv, strip, places()[3])


def start_swap(strip, data_ref, half_out, half_in, swap_send, swap_recv):
    core = places()[0]
    theirs = pl.multiple_of((1 - core) * HALF + strip * STRIP, 16)
    half_out[pl.ds(strip * STRIP, STRIP), :] = data_ref[pl.ds(theirs, STRIP), :]
    swap_copy(strip, half_out, half_in, swap_send, swap_recv).start()


def all_sum(fill_plane, fill_line, data_ref, sum_ref, gathered, half_out, half_in, total, plane_out, plane_in,
            near_src, near_in, line_in, own_part, swap_send, swap_recv, plane_send, plane_recv,
            near_send, near_recv, line_send, line_recv, plane_send2, plane_recv2,
            join_send, join_recv):
    core, x, y, mate, plane_peer, near_peer, line_peer = places()
    u = lax.axis_index("gx")
    chip = x * 4 + y
    own = pl.multiple_of(core * HALF, HALF)
    other = pl.multiple_of((1 - core) * HALF, HALF)

    swaps = [swap_copy(strip, half_out, half_in, swap_send, swap_recv) for strip in range(3)]
    for strip in range(3):
        rows = pl.ds(strip * STRIP, STRIP)
        swaps[strip].wait_recv()
        mine = data_ref[pl.ds(pl.multiple_of(own + strip * STRIP, 16), STRIP), :]
        both = mine + half_in[rows, :]
        total[rows, :] = both
        plane_out[rows, :] = both.astype(BF)
    rest = pl.ds(3 * STRIP, HALF - 3 * STRIP)
    total[rest, :] = jnp.zeros((HALF - 3 * STRIP, WIDE), F32)
    plane_out[rest, :] = jnp.zeros((HALF - 3 * STRIP, WIDE), BF)

    def plane_copy(t):
        there, device = plane_peer(t)
        rows = pl.ds(pl.multiple_of(there * PART, PART), PART)
        return remote(plane_out.at[rows, :], plane_in.at[t], plane_send, plane_recv, t, device)

    plane_copies = [plane_copy(t) for t in PLANE]
    for copy in plane_copies:
        copy.start()
    fill_plane()
    part = pl.multiple_of(chip * PART, PART)
    part_sum = total[pl.ds(part, PART), :]
    for t, copy in zip(reversed(PLANE), reversed(plane_copies)):
        copy.wait_recv()
        part_sum = part_sum + plane_in[t].astype(F32)
    near_src[...] = part_sum

    def near_copy(t):
        there, device = near_peer(t)
        rows = pl.ds(pl.multiple_of(there * CELL, CELL), CELL)
        return remote(near_src.at[rows, :], near_in.at[t], near_send, near_recv, t, device)

    near_copies = [near_copy(t) for t in (1, 2, 3)]
    for copy in near_copies:
        copy.start()
    cell_sum = near_src[pl.ds(pl.multiple_of(u % 4 * CELL, CELL), CELL), :]
    for t, copy in zip((1, 2, 3), near_copies):
        copy.wait_recv()
        cell_sum = cell_sum + near_in[t]

    line_in[u] = cell_sum.astype(BF)

    def line_copy(t, slot):
        return remote(line_in.at[u], line_in.at[slot], line_send, line_recv, t, line_peer(t))

    line_copies = [line_copy(t, u) for t in LINE]
    for copy in line_copies:
        copy.start()
    fill_line()
    for t in reversed(LINE):
        line_copy(t, (u - t + 16) % 16).wait_recv()
    for r in range(4):
        cells = [line_in[4 * group + r].astype(F32) for group in range(4)]
        own_part[pl.ds(r * CELL, CELL), :] = ((cells[0] + cells[1]) + (cells[2] + cells[3])).astype(BF)

    place = pl.multiple_of(own + part, PART)

    def plane_back(t):
        return remote(own_part, gathered.at[pl.ds(place, PART), :], plane_send2, plane_recv2, t, plane_peer(t)[1])

    def source_rows(t, base):
        px = (x - t // 4 + 4) % 4
        py = (y - t % 4 + 4) % 4
        return pl.ds(pl.multiple_of(base + (px * 4 + py) * PART, PART), PART)

    def plane_arrive(t):
        return remote(own_part, gathered.at[source_rows(t, own), :], plane_send2, plane_recv2, t, plane_peer(t)[1])

    def join_copy(t, base):
        rows = source_rows(t, base)
        return remote(gathered.at[rows, :], gathered.at[rows, :], join_send, join_recv, t, mate)

    backs = [plane_back(t) for t in PLANE]
    for copy in backs:
        copy.start()
    gathered[pl.ds(place, PART), :] = own_part[...]
    joins = [join_copy(0, own)]
    joins[0].start()
    for t in reversed(PLANE):
        plane_arrive(t).wait_recv()
        joins.append(join_copy(t, own))
        joins[-1].start()
    sum_ref[pl.ds(own, HALF), :] = gathered[pl.ds(own, HALF), :]
    for t in [0, *reversed(PLANE)]:
        join_copy(t, other).wait_recv()
    sum_ref[pl.ds(other, HALF), :] = gathered[pl.ds(other, HALF), :]
    for copy in [*swaps, *plane_copies, *near_copies, *line_copies, *backs, *joins]:
        copy.wait_send()


SHARERS = 1 + 15 + 15


def halo_kernel(position_ref, count_ref, x_hbm, g_hbm, code_hbm, first_hbm, second_hbm,
                rows_ref, halo_ref, x_weight_ref, g_weight_ref, x_ref, g_ref, code_ref, first_ref, second_ref, load_sem,
                wide_ref, msg_ref, into_ref, send_sem, recv_sem):
    q = lax.axis_index("gz")
    barrier = pltpu.get_barrier_semaphore()
    greet_neighbours(barrier)
    loads = [
        pltpu.make_async_copy(src, dst, load_sem.at[i])
        for i, (src, dst) in enumerate((
            (x_hbm, x_ref), (g_hbm, g_ref), (code_hbm, code_ref), (first_hbm, first_ref), (second_hbm, second_ref)))]
    for load in loads:
        load.start()
    for load in loads[:3]:
        load.wait()
    pack_rows(position_ref[0], count_ref[0], x_ref, g_ref, code_ref, wide_ref, rows_ref)
    pack_messages(wide_ref, msg_ref, q)
    pl.semaphore_wait(barrier, 17)
    copies = halo_copies(msg_ref, into_ref, send_sem, recv_sem)
    for copy in copies:
        copy.start()
    for load in loads[3:]:
        load.wait()
    lay_weights(first_ref, x_weight_ref, False)
    lay_weights(second_ref, g_weight_ref, True)
    for copy in copies:
        copy.wait()
    halo_ref[...] = into_ref[...]


def halo(position, count, x, g, codes, first, second):
    sems = lambda n: pltpu.SemaphoreType.DMA((n,))
    taps = 9 * WIDE
    anywhere = pl.BlockSpec(memory_space=pl.ANY)
    return pl.pallas_call(
        halo_kernel,
        out_shape=(
            pltpu.VMEM((512, 2 * WIDE), BF), pltpu.VMEM((MSG, 2 * WIDE), BF),
            pltpu.VMEM((3, taps, WIDE), BF), pltpu.VMEM((3, taps, WIDE), BF)),
        in_specs=[SMEM, SMEM] + [anywhere] * 5,
        out_specs=(VMEM,) * 4,
        scratch_shapes=[
            pltpu.VMEM((C, 512), BF), pltpu.VMEM((C, 512), BF), pltpu.VMEM((1, 64), jnp.int32),
            pltpu.VMEM((27, C, C), BF), pltpu.VMEM((27, C, C), BF), sems(5),
            pltpu.VMEM((2, 512, WIDE), F32), pltpu.VMEM((MSG, 2 * WIDE), BF), pltpu.VMEM((MSG, 2 * WIDE), BF),
            sems(17), sems(17),
        ],
        compiler_params=pltpu.CompilerParams(
            collective_id=2, has_side_effects=True, vmem_limit_bytes=24 * 2 ** 20),
        name="halo",
    )(position, count, *(pltpu.with_memory_space_constraint(a, pltpu.HBM) for a in (x, g, codes, first, second)))


def whole_kernel(scale, position_ref, first_hbm, rows_ref, into_ref, x_weight_ref, g_weight_ref,
                 out_ref, sum_ref, first_ref, load_sem, wide_ref, back_msg_ref, back_into_ref,
                 back_weight_ref, level_ref, x_patch_ref, g_patch_ref,
                 back_level_ref, back_patch_ref, grads_ref, data_ref, delta_ref,
                 back_send_sem, back_recv_sem, *reduce_refs):
    q = lax.axis_index("gz")
    position = position_ref[0]
    barrier = pltpu.get_barrier_semaphore()
    greet_sharers(barrier)
    greet_neighbours(barrier)
    load = pltpu.make_async_copy(first_hbm, first_ref, load_sem.at[0])
    load.start()

    rows = rows_ref[...].astype(F32)
    picked = pick_messages(position, into_ref)
    sender = picked[:, :WIDE].astype(F32).T[C : C + 8].astype(jnp.int32)
    code = halo_codes(position, sender)[:1]
    build_patch(rows, picked, code, level_ref, (x_patch_ref, g_patch_ref))
    nothing = jnp.zeros((512, WIDE), F32)
    pre = convolve(nothing, x_patch_ref, x_weight_ref)
    back = convolve(nothing, g_patch_ref, g_weight_ref)
    mask = jnp.broadcast_to(rows[:, C + 1 : C + 2], (512, WIDE))
    sigma = jax.nn.sigmoid(pre)
    hidden = pre * sigma * mask
    delta = (back * sigma * (1.0 + pre * (1.0 - sigma)) * mask).astype(BF)
    delta_ref[...] = delta
    wide_ref[0] = delta.astype(F32)
    back_copies = halo_copies(back_msg_ref, back_into_ref, back_send_sem, back_recv_sem)

    turned = (delta.astype(F32).T[:C].astype(BF), hidden.T[:C].astype(BF))
    for dx in (0, 1, 2):
        for half, patch_ref in ((0, x_patch_ref), (1, g_patch_ref)):
            grads_ref[half] = jnp.dot(
                turned[half], patch_ref[pl.ds(64 * dx, 512), :], preferred_element_type=F32)

            def block(tap):
                return grads_ref[half, :, pl.ds(tap * WIDE, WIDE)] * scale

            def store(tile, value):
                data_ref[pl.ds(half * HALF + dx * STRIP + tile * C, C), :] = value

            pack_grads(block, store)
        if dx == 0:
            pl.semaphore_wait(barrier, 17 + SHARERS)
        start_swap(dx, data_ref, *reduce_refs[1:3], *reduce_refs[10:12])

    def fill_plane():
        pack_messages(wide_ref, back_msg_ref, q)
        for copy in back_copies:
            copy.start()
        load.wait()
        lay_weights(first_ref, back_weight_ref, True)

    def fill_line():
        for copy in back_copies:
            copy.wait()
        back_picked = pick_messages(position, back_into_ref)
        build_patch(delta_ref[...].astype(F32), back_picked, code, back_level_ref, (back_patch_ref,))
        grad = convolve(rows_ref[:, WIDE:].astype(F32), back_patch_ref, back_weight_ref)
        out_ref[...] = (grad * mask).T[:C].astype(BF)

    all_sum(fill_plane, fill_line, data_ref, sum_ref, *reduce_refs)


def whole(scale, position, first, rows, into, x_weight, g_weight):
    sems = lambda n: pltpu.SemaphoreType.DMA((n,))
    taps = 9 * WIDE
    anywhere = pl.BlockSpec(memory_space=pl.ANY)
    return pl.pallas_call(
        functools.partial(whole_kernel, scale),
        out_shape=(pltpu.VMEM((C, 512), BF), pltpu.VMEM((ROWS, WIDE), BF)),
        in_specs=[SMEM, anywhere] + [VMEM] * 4,
        out_specs=(VMEM, VMEM),
        scratch_shapes=[
            pltpu.VMEM((27, C, C), BF), sems(1), pltpu.VMEM((1, 512, WIDE), F32),
            pltpu.VMEM((MSG, WIDE), BF), pltpu.VMEM((MSG, WIDE), BF), pltpu.VMEM((3, taps, WIDE), BF),
            pltpu.VMEM((800, 2 * WIDE), F32), pltpu.VMEM((640, taps), BF), pltpu.VMEM((640, taps), BF),
            pltpu.VMEM((800, WIDE), F32), pltpu.VMEM((640, taps), BF),
            pltpu.VMEM((2, C, taps), F32), pltpu.VMEM((ROWS, WIDE), F32), pltpu.VMEM((512, WIDE), BF),
            sems(17), sems(17),
            pltpu.VMEM((ROWS, WIDE), BF),
            pltpu.VMEM((HALF, WIDE), F32), pltpu.VMEM((HALF, WIDE), F32),
            pltpu.VMEM((HALF, WIDE), F32), pltpu.VMEM((HALF, WIDE), BF),
            pltpu.VMEM((16, PART, WIDE), BF), pltpu.VMEM((PART, WIDE), F32),
            pltpu.VMEM((4, CELL, WIDE), F32), pltpu.VMEM((16, CELL, WIDE), BF),
            pltpu.VMEM((PART, WIDE), BF),
            sems(3), sems(3), sems(16), sems(16), sems(4), sems(4), sems(16), sems(16),
            sems(16), sems(16), sems(16), sems(16),
        ],
        compiler_params=pltpu.CompilerParams(
            collective_id=1, has_side_effects=True, vmem_limit_bytes=48 * 2 ** 20),
        name="whole",
    )(
        position, pltpu.with_memory_space_constraint(first, pltpu.HBM),
        *(pltpu.with_memory_space_constraint(a, pltpu.VMEM) for a in (rows, into, x_weight, g_weight)))


def finish_kernel(grad_ref, sum_ref, out_hbm, first_hbm, second_hbm, first_ref, second_ref, out_sem):
    stores = [pltpu.make_async_copy(grad_ref, out_hbm, out_sem.at[6])]
    stores[0].start()
    for dx in (0, 1, 2):
        for half in (0, 1):

            def load(tile):
                return sum_ref[pl.ds(half * HALF + dx * STRIP + tile * C, C), :].astype(F32)

            def store(tap, value):
                if half == 0:
                    first_ref[9 * dx + tap] = value.T[:C]
                else:
                    second_ref[26 - 9 * dx - tap] = value[:, :C]

            unpack_grads(load, store)
            here, there, start = (first_ref, first_hbm, 9 * dx) if half == 0 else (second_ref, second_hbm, 18 - 9 * dx)
            taps = pl.ds(start, 9)
            stores.append(pltpu.make_async_copy(here.at[taps], there.at[taps], out_sem.at[2 * dx + half]))
            stores[-1].start()
    for copy in stores:
        copy.wait()


def finish(grad, summed):
    anywhere = pl.BlockSpec(memory_space=pl.ANY)
    return pl.pallas_call(
        finish_kernel,
        out_shape=(
            jax.ShapeDtypeStruct((C, 512), BF),
            jax.ShapeDtypeStruct((27, C, C), F32), jax.ShapeDtypeStruct((27, C, C), F32)),
        in_specs=[VMEM, VMEM],
        out_specs=(anywhere,) * 3,
        scratch_shapes=[
            pltpu.VMEM((27, C, C), F32), pltpu.VMEM((27, C, C), F32), pltpu.SemaphoreType.DMA((7,))],
        compiler_params=pltpu.CompilerParams(vmem_limit_bytes=16 * 2 ** 20),
        name="finish",
    )(
        pltpu.with_memory_space_constraint(grad, pltpu.VMEM),
        pltpu.with_memory_space_constraint(summed, pltpu.VMEM))


def shards(features, cotangent, first_weight, second_weight, slot_position, brick_count, column_code):
    devices = lax.axis_size("gx") * lax.axis_size("gy") * lax.axis_size("gz")
    scale = float(devices ** -0.5 / 8.0)
    position = slot_position.reshape(1)
    handed = halo(
        position, brick_count.reshape(1), features.reshape(C, 512), cotangent.reshape(C, 512),
        column_code.reshape(1, 64), first_weight, second_weight)
    grad, summed = whole(scale, position, first_weight, *handed)
    grad_input, first_grad, second_grad = finish(grad, summed)
    return grad_input.reshape(1, 1, 1, 1, C, 512), first_grad, second_grad


def solution(mesh):
    placed = (
        P("gx", "gy", "gz", None, None, None),
        P("gx", "gy", "gz", None, None, None),
        P(),
        P(),
        P("gx", "gy", "gz", None),
        P("gx", "gy", "gz"),
        P("gx", "gy", "gz", None, None),
    )
    return jax.shard_map(
        shards,
        mesh=mesh,
        in_specs=placed,
        out_specs=(P("gx", "gy", "gz", None, None, None), P(), P()),
        check_vma=False,
    )
```

```python
import functools

import jax
import jax.numpy as jnp
from jax import lax
from jax.experimental import pallas as pl
from jax.experimental.pallas import tpu as pltpu
from jax.sharding import PartitionSpec as P

MESH = pl.DeviceIdType.MESH
VMEM = pl.BlockSpec(memory_space=pltpu.VMEM)
SMEM = pl.BlockSpec(memory_space=pltpu.SMEM)
C = 96
WIDE = 128
MSG = 512
BF = jnp.bfloat16
F32 = jnp.float32


def message_plan():
    plan = []
    for ix in (0, 1):
        for iy in (0, 1):
            plan.append((13 + 2 * ix + iy, 16, (1 - 2 * ix, 1 - 2 * iy, 1)))
    for iy in (0, 1):
        plan.append((11 + iy, 16, (0, 1 - 2 * iy, 1)))
    for ix in (0, 1):
        plan.append((9 + ix, 16, (1 - 2 * ix, 0, 1)))
    for ix in (0, 1):
        for iy in (0, 1):
            plan.append((5 + 2 * ix + iy, 16, (1 - 2 * ix, 1 - 2 * iy, 0)))
    plan.append((4, 64, (0, 0, 1)))
    for iy in (0, 1):
        plan.append((2 + iy, 64, (0, 1 - 2 * iy, 0)))
    for ix in (0, 1):
        plan.append((ix, 64, (1 - 2 * ix, 0, 0)))
    return plan


def slot_row(slot):
    return slot * 64 if slot < 5 else 320 + (slot - 5) * 16


def pack_messages(wide_ref, msg_ref, q):
    blank = jnp.zeros((8, WIDE), F32)
    only = lax.broadcasted_iota(jnp.int32, (8, WIDE), 0) == 0
    for part in range(wide_ref.shape[0]):

        def rows(*spot, **stride):
            return wide_ref[part, pl.ds(*spot, **stride), :]

        def put(slot, value):
            start = slot_row(slot)
            msg_ref[pl.ds(start, value.shape[0]), pl.ds(part * WIDE, WIDE)] = value.astype(BF)

        def side(low, high):
            return jnp.where(q == 0, high, low)

        for ix in (0, 1):
            put(ix, rows(448 * (1 - ix), 64))
        for iy in (0, 1):
            edge = [rows(64 * i + 56 * (1 - iy), 8) for i in range(8)]
            put(2 + iy, jnp.concatenate(edge, axis=0))
        put(4, side(rows(0, 64, stride=8), rows(7, 64, stride=8)))
        for ix in (0, 1):
            x0 = 448 * (1 - ix)
            for iy in (0, 1):
                column = rows(x0 + 56 * (1 - iy), 8)
                put(5 + 2 * ix + iy, jnp.concatenate([column, blank], axis=0))
                corner = side(column, pltpu.roll(column, 1, 0))
                put(13 + 2 * ix + iy, jnp.concatenate([jnp.where(only, corner, 0.0), blank], axis=0))
            line = side(rows(x0, 8, stride=8), rows(x0 + 7, 8, stride=8))
            put(9 + ix, jnp.concatenate([line, blank], axis=0))
        for iy in (0, 1):
            y0 = 56 * (1 - iy)
            line = side(rows(y0, 8, stride=64), rows(y0 + 7, 8, stride=64))
            put(11 + iy, jnp.concatenate([line, blank], axis=0))


def pack_rows(position, count, x_ref, g_ref, code_ref, wide_ref, rows_ref):
    column = lax.broadcasted_iota(jnp.int32, (64, 512), 0)
    voxel = lax.broadcasted_iota(jnp.int32, (64, 512), 1)
    spread = jnp.where(column == voxel // 8, 1.0, 0.0).astype(BF)
    codes = jnp.broadcast_to(code_ref[...].astype(F32), (16, 64)).astype(BF)
    code = jnp.dot(codes, spread, preferred_element_type=F32).astype(jnp.int32)[:8]
    low = code // 8
    level = lax.broadcasted_iota(jnp.int32, (8, 512), 1) % 8
    live = (level >= low) & (level <= low + code % 8) & (count > 0)
    mask = jnp.where(live, 1.0, 0.0)
    first = lax.broadcasted_iota(jnp.int32, (8, 512), 0)
    place = jnp.where(first == 0, position.astype(F32), jnp.where(first == 1, mask, 0.0))
    blank = jnp.zeros((24, 512), F32)
    inside = jnp.broadcast_to(mask[:1], (C, 512)) > 0.0
    x = jnp.where(inside, x_ref[...].astype(F32), 0.0)
    g = jnp.where(inside, g_ref[...].astype(F32), 0.0)
    wide_ref[0] = jnp.concatenate([x, place, blank], axis=0).T
    wide_ref[1] = jnp.concatenate([g, jnp.zeros((32, 512), F32)], axis=0).T
    rows_ref[:, :WIDE] = wide_ref[0].astype(BF)
    rows_ref[:, WIDE:] = wide_ref[1].astype(BF)


def neighbour(offset):
    u, w, q = lax.axis_index("gx"), lax.axis_index("gy"), lax.axis_index("gz")
    nx, ny = lax.axis_size("gx"), lax.axis_size("gy")
    du, dv, dw = offset
    return ((u + du + nx) % nx, (w + dv + ny) % ny, 1 - q if dw else q)


def halo_copies(msg_ref, into_ref, send_sem, recv_sem):
    copies = []
    for slot, size, offset in message_plan():
        rows = pl.ds(slot_row(slot), size)
        copies.append(pltpu.make_async_remote_copy(
            src_ref=msg_ref.at[rows, :], dst_ref=into_ref.at[rows, :],
            send_sem=send_sem.at[slot], recv_sem=recv_sem.at[slot],
            device_id=neighbour(offset), device_id_type=MESH))
    return copies


def greet_neighbours(barrier):
    for _, _, offset in message_plan():
        pl.semaphore_signal(barrier, inc=1, device_id=neighbour(offset), device_id_type=MESH)


def pick_messages(position, into_ref):
    def bit(size, divisor):
        return jnp.zeros((size, into_ref.shape[1]), jnp.int32) + position // divisor % 2 == 0

    def at(slot):
        return into_ref[pl.ds(slot_row(slot), 64 if slot < 5 else 16), :].astype(F32)

    def two(slot, divisor):
        low = at(slot)
        return jnp.where(bit(low.shape[0], divisor), low, at(slot + 1))

    def four(slot):
        return jnp.where(bit(16, 4), two(slot, 2), two(slot + 2, 2))

    return jnp.concatenate(
        [two(0, 4), two(2, 2), at(4), four(5), two(9, 4), two(11, 2), four(13)], axis=0).astype(BF)


def halo_codes(position, sender):
    u, w, q = (lax.axis_index(axis) for axis in ("gx", "gy", "gz"))
    nx, ny = lax.axis_size("gx"), lax.axis_size("gy")
    own = (position // 4, position // 2 % 2, position % 2)
    theirs = (sender // 4, sender // 2 % 2, sender % 2)
    beyond = (u + 2 * own[0] - 1, w + 2 * own[1] - 1, q + 2 * own[2] - 1)
    sizes = (nx, ny, 2)
    r = lax.broadcasted_iota(jnp.int32, sender.shape, 1)
    face = r < 192
    t = jnp.where(face, r % 64, r % 16)
    high, low = t // 8, t % 8
    past = (
        (r < 64) | ((r >= 192) & (r < 224)) | (r >= 240),
        ((r >= 64) & (r < 128)) | ((r >= 192) & (r < 208)) | (r >= 224),
        ((r >= 128) & (r < 192)) | (r >= 208))
    index = (
        jnp.where(face, high, t),
        jnp.where(r < 64, high, jnp.where(face, low, t)),
        jnp.where(face, low, t))
    valid = face | (t < jnp.where(r < 240, 8, 1))
    spot = []
    for axis in range(3):
        far = 9 * own[axis]
        near = 9 - far
        same = theirs[axis] == own[axis]
        inner = jnp.where(same, 1 + index[axis], near)
        inner_ok = same | (index[axis] == 7 * own[axis])
        there = jnp.zeros_like(r) + beyond[axis]
        outer_ok = (theirs[axis] != own[axis]) & (there >= 0) & (there < sizes[axis])
        spot.append(jnp.where(past[axis], far, inner))
        valid = valid & ((past[axis] & outer_ok) | (jnp.logical_not(past[axis]) & inner_ok))
    return jnp.where(valid, (spot[0] * 10 + spot[1]) * 16 + spot[2], -1)


def build_patch(rows, picked, code, level_ref, patch_refs):
    n = lax.broadcasted_iota(jnp.int32, (800, 256), 0)
    target = n // 8 * 16 + n % 8
    level = lax.broadcasted_iota(jnp.int32, rows.shape, 0) % 8
    for dz in (0, 1, 2):
        pick = jnp.where(target + dz == code, 1.0, 0.0).astype(BF)
        halo = jnp.dot(pick, picked, preferred_element_type=F32)
        if dz == 0:
            mine = jnp.where(level == 0, 0.0, pltpu.roll(rows, 1, 0))
        elif dz == 1:
            mine = rows
        else:
            mine = jnp.where(level == 7, 0.0, pltpu.roll(rows, 511, 0))
        level_ref[...] = halo
        for i in range(8):
            spot = pl.ds(((i + 1) * 10 + 1) * 8, 64)
            level_ref[spot, :] = level_ref[spot, :] + mine[64 * i : 64 * i + 64]
        for part, patch_ref in enumerate(patch_refs):
            for dy in (0, 1, 2):
                tap = dy * 3 + dz
                for x in range(10):
                    patch_ref[pl.ds(64 * x, 64), pl.ds(tap * WIDE, WIDE)] = (
                        level_ref[pl.ds((x * 10 + dy) * 8, 64), pl.ds(part * WIDE, WIDE)].astype(BF))


def convolve(start, patch_ref, weight_ref):
    total = start
    for dx in (0, 1, 2):
        total = total + jnp.dot(patch_ref[pl.ds(64 * dx, 512), :], weight_ref[dx], preferred_element_type=F32)
    return total


def pack_grads(block, store):
    lane = lax.broadcasted_iota(jnp.int32, (C, WIDE), 1)
    for group in range(2):
        last = block(4 * group + 3)
        for t in range(3):
            shifted = pltpu.roll(last, C - 32 * t, 1)
            store(3 * group + t, jnp.where(lane < C, block(4 * group + t), shifted))
    store(6, block(8))


def unpack_grads(load, store):
    lane = lax.broadcasted_iota(jnp.int32, (C, WIDE), 1)
    for group in range(2):
        last = jnp.zeros((C, WIDE), F32)
        for t in range(3):
            tile = load(3 * group + t)
            store(4 * group + t, tile)
            moved = pltpu.roll(tile, 32 + 32 * t, 1)
            last = jnp.where((lane >= 32 * t) & (lane < 32 * t + 32), moved, last)
        store(4 * group + 3, last)
    store(8, load(6))


def square(block):
    gap = WIDE - C
    wide = jnp.concatenate([block.astype(F32), jnp.zeros((C, gap), F32)], axis=1)
    return jnp.concatenate([wide, jnp.zeros((gap, WIDE), F32)], axis=0)


def lay_weights(kernel_ref, weight_ref, turned):
    def step(k, carry):
        rows = pl.ds(pl.multiple_of(k % 9 * WIDE, WIDE), WIDE)
        block = square(kernel_ref[26 - k]).T if turned else square(kernel_ref[k])
        weight_ref[k // 9, rows, :] = block.astype(BF)
        return carry

    lax.fori_loop(0, 27, step, 0)


ROWS = 4096
HALF = ROWS // 2
STRIP = 7 * C
PART = HALF // 16
CELL = PART // 4


def ring(distance, size):
    return min(distance, size - distance)


PLANE = sorted(range(1, 16), key=lambda t: -ring(t // 4, 4) - ring(t % 4, 4))
LINE = sorted(range(1, 16), key=lambda t: -ring(t, 16))


def places():
    u = lax.axis_index("gx")
    w = lax.axis_index("gy")
    q = lax.axis_index("gz")
    core = w % 2
    y = w // 2 % 4
    x = q * 2 + w // 8
    mate = (u, w + 1 - 2 * core, q)

    def plane_peer(t):
        px = (x + t // 4) % 4
        py = (y + t % 4) % 4
        return px * 4 + py, (u, ((px % 2) * 4 + py) * 2 + core, px // 2)

    def near_peer(t):
        r = (u % 4 + t) % 4
        return r, (u // 4 * 4 + r, w, q)

    def line_peer(t):
        return (u + t) % 16, w, q

    return core, x, y, mate, plane_peer, near_peer, line_peer


def greet_sharers(barrier):
    core, x, y, mate, plane_peer, near_peer, line_peer = places()
    for t in LINE:
        pl.semaphore_signal(barrier, inc=1, device_id=line_peer(t), device_id_type=MESH)
    for t in PLANE:
        pl.semaphore_signal(barrier, inc=1, device_id=plane_peer(t)[1], device_id_type=MESH)
    pl.semaphore_signal(barrier, inc=1, device_id=mate, device_id_type=MESH)


def remote(src, dst, sends, recvs, index, device):
    return pltpu.make_async_remote_copy(
        src_ref=src, dst_ref=dst, send_sem=sends.at[index], recv_sem=recvs.at[index],
        device_id=device, device_id_type=MESH)


def swap_copy(strip, half_out, half_in, swap_send, swap_recv):
    rows = pl.ds(strip * STRIP, STRIP)
    return remote(half_out.at[rows, :], half_in.at[rows, :], swap_send, swap_recv, strip, places()[3])


def start_swap(strip, data_ref, half_out, half_in, swap_send, swap_recv):
    core = places()[0]
    theirs = pl.multiple_of((1 - core) * HALF + strip * STRIP, 16)
    half_out[pl.ds(strip * STRIP, STRIP), :] = data_ref[pl.ds(theirs, STRIP), :]
    swap_copy(strip, half_out, half_in, swap_send, swap_recv).start()


def all_sum(fill_plane, fill_line, data_ref, spread, gathered, half_out, half_in, total, plane_out, plane_in,
            near_src, near_in, line_in, own_part, swap_send, swap_recv, plane_send, plane_recv,
            near_send, near_recv, line_send, line_recv, plane_send2, plane_recv2,
            join_send, join_recv):
    core, x, y, mate, plane_peer, near_peer, line_peer = places()
    u = lax.axis_index("gx")
    chip = x * 4 + y
    own = pl.multiple_of(core * HALF, HALF)
    other = pl.multiple_of((1 - core) * HALF, HALF)

    swaps = [swap_copy(strip, half_out, half_in, swap_send, swap_recv) for strip in range(3)]
    for strip in range(3):
        rows = pl.ds(strip * STRIP, STRIP)
        swaps[strip].wait_recv()
        mine = data_ref[pl.ds(pl.multiple_of(own + strip * STRIP, 16), STRIP), :]
        both = mine + half_in[rows, :]
        total[rows, :] = both
        plane_out[rows, :] = both.astype(BF)
    rest = pl.ds(3 * STRIP, HALF - 3 * STRIP)
    total[rest, :] = jnp.zeros((HALF - 3 * STRIP, WIDE), F32)
    plane_out[rest, :] = jnp.zeros((HALF - 3 * STRIP, WIDE), BF)

    def plane_copy(t):
        there, device = plane_peer(t)
        rows = pl.ds(pl.multiple_of(there * PART, PART), PART)
        return remote(plane_out.at[rows, :], plane_in.at[t], plane_send, plane_recv, t, device)

    plane_copies = [plane_copy(t) for t in PLANE]
    for copy in plane_copies:
        copy.start()
    fill_plane()
    part = pl.multiple_of(chip * PART, PART)
    part_sum = total[pl.ds(part, PART), :]
    for t, copy in zip(reversed(PLANE), reversed(plane_copies)):
        copy.wait_recv()
        part_sum = part_sum + plane_in[t].astype(F32)
    near_src[...] = part_sum

    def near_copy(t):
        there, device = near_peer(t)
        rows = pl.ds(pl.multiple_of(there * CELL, CELL), CELL)
        return remote(near_src.at[rows, :], near_in.at[t], near_send, near_recv, t, device)

    near_copies = [near_copy(t) for t in (1, 2, 3)]
    for copy in near_copies:
        copy.start()
    cell_sum = near_src[pl.ds(pl.multiple_of(u % 4 * CELL, CELL), CELL), :]
    for t, copy in zip((1, 2, 3), near_copies):
        copy.wait_recv()
        cell_sum = cell_sum + near_in[t]

    line_in[u] = cell_sum.astype(BF)

    def line_copy(t, slot):
        return remote(line_in.at[u], line_in.at[slot], line_send, line_recv, t, line_peer(t))

    line_copies = [line_copy(t, u) for t in LINE]
    for copy in line_copies:
        copy.start()
    fill_line()
    for t in reversed(LINE):
        line_copy(t, (u - t + 16) % 16).wait_recv()
    for r in range(4):
        cells = [line_in[4 * group + r].astype(F32) for group in range(4)]
        own_part[pl.ds(r * CELL, CELL), :] = ((cells[0] + cells[1]) + (cells[2] + cells[3])).astype(BF)

    place = pl.multiple_of(own + part, PART)

    def plane_back(t):
        return remote(own_part, gathered.at[pl.ds(place, PART), :], plane_send2, plane_recv2, t, plane_peer(t)[1])

    def source_rows(t, base):
        px = (x - t // 4 + 4) % 4
        py = (y - t % 4 + 4) % 4
        return pl.ds(pl.multiple_of(base + (px * 4 + py) * PART, PART), PART)

    def plane_arrive(t):
        return remote(own_part, gathered.at[source_rows(t, own), :], plane_send2, plane_recv2, t, plane_peer(t)[1])

    def join_copy(t, base):
        rows = source_rows(t, base)
        return remote(gathered.at[rows, :], gathered.at[rows, :], join_send, join_recv, t, mate)

    backs = [plane_back(t) for t in PLANE]
    for copy in backs:
        copy.start()
    gathered[pl.ds(place, PART), :] = own_part[...]
    joins = [join_copy(0, own)]
    joins[0].start()
    for t in reversed(PLANE):
        plane_arrive(t).wait_recv()
        joins.append(join_copy(t, own))
        joins[-1].start()
    spread(core)
    for t in [0, *reversed(PLANE)]:
        join_copy(t, other).wait_recv()
    spread(1 - core)
    for copy in [*swaps, *plane_copies, *near_copies, *line_copies, *backs, *joins]:
        copy.wait_send()


SHARERS = 1 + 15 + 15


def halo_kernel(position_ref, count_ref, x_hbm, g_hbm, code_hbm, first_hbm, second_hbm,
                rows_ref, halo_ref, x_weight_ref, g_weight_ref, x_ref, g_ref, code_ref, first_ref, second_ref, load_sem,
                wide_ref, msg_ref, into_ref, send_sem, recv_sem):
    q = lax.axis_index("gz")
    barrier = pltpu.get_barrier_semaphore()
    greet_neighbours(barrier)
    loads = [
        pltpu.make_async_copy(src, dst, load_sem.at[i])
        for i, (src, dst) in enumerate((
            (x_hbm, x_ref), (g_hbm, g_ref), (code_hbm, code_ref), (first_hbm, first_ref), (second_hbm, second_ref)))]
    for load in loads:
        load.start()
    for load in loads[:3]:
        load.wait()
    pack_rows(position_ref[0], count_ref[0], x_ref, g_ref, code_ref, wide_ref, rows_ref)
    pack_messages(wide_ref, msg_ref, q)
    pl.semaphore_wait(barrier, 17)
    copies = halo_copies(msg_ref, into_ref, send_sem, recv_sem)
    for copy in copies:
        copy.start()
    for load in loads[3:]:
        load.wait()
    lay_weights(first_ref, x_weight_ref, False)
    lay_weights(second_ref, g_weight_ref, True)
    for copy in copies:
        copy.wait()
    halo_ref[...] = into_ref[...]


def halo(position, count, x, g, codes, first, second):
    sems = lambda n: pltpu.SemaphoreType.DMA((n,))
    taps = 9 * WIDE
    anywhere = pl.BlockSpec(memory_space=pl.ANY)
    return pl.pallas_call(
        halo_kernel,
        out_shape=(
            pltpu.VMEM((512, 2 * WIDE), BF), pltpu.VMEM((MSG, 2 * WIDE), BF),
            pltpu.VMEM((3, taps, WIDE), BF), pltpu.VMEM((3, taps, WIDE), BF)),
        in_specs=[SMEM, SMEM] + [anywhere] * 5,
        out_specs=(VMEM,) * 4,
        scratch_shapes=[
            pltpu.VMEM((C, 512), BF), pltpu.VMEM((C, 512), BF), pltpu.VMEM((1, 64), jnp.int32),
            pltpu.VMEM((27, C, C), BF), pltpu.VMEM((27, C, C), BF), sems(5),
            pltpu.VMEM((2, 512, WIDE), F32), pltpu.VMEM((MSG, 2 * WIDE), BF), pltpu.VMEM((MSG, 2 * WIDE), BF),
            sems(17), sems(17),
        ],
        compiler_params=pltpu.CompilerParams(
            collective_id=2, has_side_effects=True, vmem_limit_bytes=24 * 2 ** 20),
        name="halo",
    )(position, count, *(pltpu.with_memory_space_constraint(a, pltpu.HBM) for a in (x, g, codes, first, second)))


def whole_kernel(scale, position_ref, first_hbm, rows_ref, into_ref, x_weight_ref, g_weight_ref,
                 out_ref, first_out_ref, second_out_ref, first_ref, load_sem, wide_ref, back_msg_ref, back_into_ref,
                 back_weight_ref, level_ref, x_patch_ref, g_patch_ref,
                 back_level_ref, back_patch_ref, grads_ref, data_ref, delta_ref,
                 back_send_sem, back_recv_sem, *reduce_refs):
    q = lax.axis_index("gz")
    position = position_ref[0]
    barrier = pltpu.get_barrier_semaphore()
    greet_sharers(barrier)
    greet_neighbours(barrier)
    load = pltpu.make_async_copy(first_hbm, first_ref, load_sem.at[0])
    load.start()

    rows = rows_ref[...].astype(F32)
    picked = pick_messages(position, into_ref)
    sender = picked[:, :WIDE].astype(F32).T[C : C + 8].astype(jnp.int32)
    code = halo_codes(position, sender)[:1]
    build_patch(rows, picked, code, level_ref, (x_patch_ref, g_patch_ref))
    nothing = jnp.zeros((512, WIDE), F32)
    pre = convolve(nothing, x_patch_ref, x_weight_ref)
    back = convolve(nothing, g_patch_ref, g_weight_ref)
    mask = jnp.broadcast_to(rows[:, C + 1 : C + 2], (512, WIDE))
    sigma = jax.nn.sigmoid(pre)
    hidden = pre * sigma * mask
    delta = (back * sigma * (1.0 + pre * (1.0 - sigma)) * mask).astype(BF)
    delta_ref[...] = delta
    wide_ref[0] = delta.astype(F32)
    back_copies = halo_copies(back_msg_ref, back_into_ref, back_send_sem, back_recv_sem)

    turned = (delta.astype(F32).T[:C].astype(BF), hidden.T[:C].astype(BF))
    for dx in (0, 1, 2):
        for half, patch_ref in ((0, x_patch_ref), (1, g_patch_ref)):
            grads_ref[half] = jnp.dot(
                turned[half], patch_ref[pl.ds(64 * dx, 512), :], preferred_element_type=F32)

            def block(tap):
                return grads_ref[half, :, pl.ds(tap * WIDE, WIDE)] * scale

            def store(tile, value):
                data_ref[pl.ds(half * HALF + dx * STRIP + tile * C, C), :] = value

            pack_grads(block, store)
        if dx == 1:
            pl.semaphore_wait(barrier, 17 + SHARERS)
            start_swap(0, data_ref, *reduce_refs[1:3], *reduce_refs[10:12])
        if dx > 0:
            start_swap(dx, data_ref, *reduce_refs[1:3], *reduce_refs[10:12])

    def fill_plane():
        pack_messages(wide_ref, back_msg_ref, q)
        for copy in back_copies:
            copy.start()
        load.wait()
        lay_weights(first_ref, back_weight_ref, True)

    def fill_line():
        for copy in back_copies:
            copy.wait()
        back_picked = pick_messages(position, back_into_ref)
        build_patch(delta_ref[...].astype(F32), back_picked, code, back_level_ref, (back_patch_ref,))
        grad = convolve(rows_ref[:, WIDE:].astype(F32), back_patch_ref, back_weight_ref)
        out_ref[...] = (grad * mask).T[:C].astype(BF)

    def spread(half):
        for which in (0, 1):

            @pl.when(half == which)
            def _():
                for dx in (0, 1, 2):

                    def load(tile):
                        return reduce_refs[0][pl.ds(which * HALF + dx * STRIP + tile * C, C), :].astype(F32)

                    def store(tap, value):
                        if which == 0:
                            first_out_ref[9 * dx + tap] = value.T[:C]
                        else:
                            second_out_ref[26 - 9 * dx - tap] = value[:, :C]

                    unpack_grads(load, store)

    all_sum(fill_plane, fill_line, data_ref, spread, *reduce_refs)


def whole(scale, position, first, rows, into, x_weight, g_weight):
    sems = lambda n: pltpu.SemaphoreType.DMA((n,))
    taps = 9 * WIDE
    anywhere = pl.BlockSpec(memory_space=pl.ANY)
    return pl.pallas_call(
        functools.partial(whole_kernel, scale),
        out_shape=(pltpu.VMEM((C, 512), BF), pltpu.VMEM((27, C, C), F32), pltpu.VMEM((27, C, C), F32)),
        in_specs=[SMEM, anywhere] + [VMEM] * 4,
        out_specs=(VMEM,) * 3,
        scratch_shapes=[
            pltpu.VMEM((27, C, C), BF), sems(1), pltpu.VMEM((1, 512, WIDE), F32),
            pltpu.VMEM((MSG, WIDE), BF), pltpu.VMEM((MSG, WIDE), BF), pltpu.VMEM((3, taps, WIDE), BF),
            pltpu.VMEM((800, 2 * WIDE), F32), pltpu.VMEM((640, taps), BF), pltpu.VMEM((640, taps), BF),
            pltpu.VMEM((800, WIDE), F32), pltpu.VMEM((640, taps), BF),
            pltpu.VMEM((2, C, taps), F32), pltpu.VMEM((ROWS, WIDE), F32), pltpu.VMEM((512, WIDE), BF),
            sems(17), sems(17),
            pltpu.VMEM((ROWS, WIDE), BF),
            pltpu.VMEM((HALF, WIDE), F32), pltpu.VMEM((HALF, WIDE), F32),
            pltpu.VMEM((HALF, WIDE), F32), pltpu.VMEM((HALF, WIDE), BF),
            pltpu.VMEM((16, PART, WIDE), BF), pltpu.VMEM((PART, WIDE), F32),
            pltpu.VMEM((4, CELL, WIDE), F32), pltpu.VMEM((16, CELL, WIDE), BF),
            pltpu.VMEM((PART, WIDE), BF),
            sems(3), sems(3), sems(16), sems(16), sems(4), sems(4), sems(16), sems(16),
            sems(16), sems(16), sems(16), sems(16),
        ],
        compiler_params=pltpu.CompilerParams(
            collective_id=1, has_side_effects=True, vmem_limit_bytes=48 * 2 ** 20),
        name="whole",
    )(
        position, pltpu.with_memory_space_constraint(first, pltpu.HBM),
        *(pltpu.with_memory_space_constraint(a, pltpu.VMEM) for a in (rows, into, x_weight, g_weight)))


def finish_kernel(grad_ref, first_ref, second_ref, grad_hbm, first_hbm, second_hbm, out_sem):
    stores = []
    for start in (0, 9, 18):
        taps = pl.ds(start, 9)
        stores.append((first_ref.at[taps], first_hbm.at[taps]))
        stores.append((second_ref.at[taps], second_hbm.at[taps]))
    stores.append((grad_ref, grad_hbm))
    copies = [pltpu.make_async_copy(here, there, out_sem.at[i]) for i, (here, there) in enumerate(stores)]
    for copy in copies:
        copy.start()
    for copy in copies:
        copy.wait()


def finish(grad, first, second):
    anywhere = pl.BlockSpec(memory_space=pl.ANY)
    return pl.pallas_call(
        finish_kernel,
        out_shape=(
            jax.ShapeDtypeStruct((C, 512), BF),
            jax.ShapeDtypeStruct((27, C, C), F32), jax.ShapeDtypeStruct((27, C, C), F32)),
        in_specs=[VMEM] * 3,
        out_specs=(anywhere,) * 3,
        scratch_shapes=[pltpu.SemaphoreType.DMA((7,))],
        compiler_params=pltpu.CompilerParams(vmem_limit_bytes=16 * 2 ** 20),
        name="finish",
    )(*(pltpu.with_memory_space_constraint(a, pltpu.VMEM) for a in (grad, first, second)))


def shards(features, cotangent, first_weight, second_weight, slot_position, brick_count, column_code):
    devices = lax.axis_size("gx") * lax.axis_size("gy") * lax.axis_size("gz")
    scale = float(devices ** -0.5 / 8.0)
    position = slot_position.reshape(1)
    handed = halo(
        position, brick_count.reshape(1), features.reshape(C, 512), cotangent.reshape(C, 512),
        column_code.reshape(1, 64), first_weight, second_weight)
    grad_input, first_grad, second_grad = finish(*whole(scale, position, first_weight, *handed))
    return grad_input.reshape(1, 1, 1, 1, C, 512), first_grad, second_grad


def solution(mesh):
    placed = (
        P("gx", "gy", "gz", None, None, None),
        P("gx", "gy", "gz", None, None, None),
        P(),
        P(),
        P("gx", "gy", "gz", None),
        P("gx", "gy", "gz"),
        P("gx", "gy", "gz", None, None),
    )
    return jax.shard_map(
        shards,
        mesh=mesh,
        in_specs=placed,
        out_specs=(P("gx", "gy", "gz", None, None, None), P(), P()),
        check_vma=False,
    )
```

```python
import functools

import jax
import jax.numpy as jnp
from jax import lax
from jax.experimental import pallas as pl
from jax.experimental.pallas import tpu as pltpu
from jax.sharding import PartitionSpec as P

MESH = pl.DeviceIdType.MESH
VMEM = pl.BlockSpec(memory_space=pltpu.VMEM)
SMEM = pl.BlockSpec(memory_space=pltpu.SMEM)
C = 96
WIDE = 128
MSG = 512
BF = jnp.bfloat16
F32 = jnp.float32


def message_plan():
    plan = []
    for ix in (0, 1):
        for iy in (0, 1):
            plan.append((13 + 2 * ix + iy, 16, (1 - 2 * ix, 1 - 2 * iy, 1)))
    for iy in (0, 1):
        plan.append((11 + iy, 16, (0, 1 - 2 * iy, 1)))
    for ix in (0, 1):
        plan.append((9 + ix, 16, (1 - 2 * ix, 0, 1)))
    for ix in (0, 1):
        for iy in (0, 1):
            plan.append((5 + 2 * ix + iy, 16, (1 - 2 * ix, 1 - 2 * iy, 0)))
    plan.append((4, 64, (0, 0, 1)))
    for iy in (0, 1):
        plan.append((2 + iy, 64, (0, 1 - 2 * iy, 0)))
    for ix in (0, 1):
        plan.append((ix, 64, (1 - 2 * ix, 0, 0)))
    return plan


def slot_row(slot):
    return slot * 64 if slot < 5 else 320 + (slot - 5) * 16


def pack_messages(wide_ref, msg_ref, q):
    blank = jnp.zeros((8, WIDE), F32)
    only = lax.broadcasted_iota(jnp.int32, (8, WIDE), 0) == 0
    for part in range(wide_ref.shape[0]):

        def rows(*spot, **stride):
            return wide_ref[part, pl.ds(*spot, **stride), :]

        def put(slot, value):
            start = slot_row(slot)
            msg_ref[pl.ds(start, value.shape[0]), pl.ds(part * WIDE, WIDE)] = value.astype(BF)

        def side(low, high):
            return jnp.where(q == 0, high, low)

        for ix in (0, 1):
            put(ix, rows(448 * (1 - ix), 64))
        for iy in (0, 1):
            edge = [rows(64 * i + 56 * (1 - iy), 8) for i in range(8)]
            put(2 + iy, jnp.concatenate(edge, axis=0))
        put(4, side(rows(0, 64, stride=8), rows(7, 64, stride=8)))
        for ix in (0, 1):
            x0 = 448 * (1 - ix)
            for iy in (0, 1):
                column = rows(x0 + 56 * (1 - iy), 8)
                put(5 + 2 * ix + iy, jnp.concatenate([column, blank], axis=0))
                corner = side(column, pltpu.roll(column, 1, 0))
                put(13 + 2 * ix + iy, jnp.concatenate([jnp.where(only, corner, 0.0), blank], axis=0))
            line = side(rows(x0, 8, stride=8), rows(x0 + 7, 8, stride=8))
            put(9 + ix, jnp.concatenate([line, blank], axis=0))
        for iy in (0, 1):
            y0 = 56 * (1 - iy)
            line = side(rows(y0, 8, stride=64), rows(y0 + 7, 8, stride=64))
            put(11 + iy, jnp.concatenate([line, blank], axis=0))


def pack_rows(position, count, x_ref, g_ref, code_ref, wide_ref, rows_ref):
    column = lax.broadcasted_iota(jnp.int32, (64, 512), 0)
    voxel = lax.broadcasted_iota(jnp.int32, (64, 512), 1)
    spread = jnp.where(column == voxel // 8, 1.0, 0.0).astype(BF)
    codes = jnp.broadcast_to(code_ref[...].astype(F32), (16, 64)).astype(BF)
    code = jnp.dot(codes, spread, preferred_element_type=F32).astype(jnp.int32)[:8]
    low = code // 8
    level = lax.broadcasted_iota(jnp.int32, (8, 512), 1) % 8
    live = (level >= low) & (level <= low + code % 8) & (count > 0)
    mask = jnp.where(live, 1.0, 0.0)
    first = lax.broadcasted_iota(jnp.int32, (8, 512), 0)
    place = jnp.where(first == 0, position.astype(F32), jnp.where(first == 1, mask, 0.0))
    blank = jnp.zeros((24, 512), F32)
    inside = jnp.broadcast_to(mask[:1], (C, 512)) > 0.0
    x = jnp.where(inside, x_ref[...].astype(F32), 0.0)
    g = jnp.where(inside, g_ref[...].astype(F32), 0.0)
    wide_ref[0] = jnp.concatenate([x, place, blank], axis=0).T
    wide_ref[1] = jnp.concatenate([g, jnp.zeros((32, 512), F32)], axis=0).T
    rows_ref[:, :WIDE] = wide_ref[0].astype(BF)
    rows_ref[:, WIDE:] = wide_ref[1].astype(BF)


def neighbour(offset):
    u, w, q = lax.axis_index("gx"), lax.axis_index("gy"), lax.axis_index("gz")
    nx, ny = lax.axis_size("gx"), lax.axis_size("gy")
    du, dv, dw = offset
    return ((u + du + nx) % nx, (w + dv + ny) % ny, 1 - q if dw else q)


def halo_copies(msg_ref, into_ref, send_sem, recv_sem):
    copies = []
    for slot, size, offset in message_plan():
        rows = pl.ds(slot_row(slot), size)
        copies.append(pltpu.make_async_remote_copy(
            src_ref=msg_ref.at[rows, :], dst_ref=into_ref.at[rows, :],
            send_sem=send_sem.at[slot], recv_sem=recv_sem.at[slot],
            device_id=neighbour(offset), device_id_type=MESH))
    return copies


def greet_neighbours(barrier):
    for _, _, offset in message_plan():
        pl.semaphore_signal(barrier, inc=1, device_id=neighbour(offset), device_id_type=MESH)


def pick_messages(position, into_ref):
    def bit(size, divisor):
        return jnp.zeros((size, into_ref.shape[1]), jnp.int32) + position // divisor % 2 == 0

    def at(slot):
        return into_ref[pl.ds(slot_row(slot), 64 if slot < 5 else 16), :].astype(F32)

    def two(slot, divisor):
        low = at(slot)
        return jnp.where(bit(low.shape[0], divisor), low, at(slot + 1))

    def four(slot):
        return jnp.where(bit(16, 4), two(slot, 2), two(slot + 2, 2))

    return jnp.concatenate(
        [two(0, 4), two(2, 2), at(4), four(5), two(9, 4), two(11, 2), four(13)], axis=0).astype(BF)


def halo_codes(position, sender):
    u, w, q = (lax.axis_index(axis) for axis in ("gx", "gy", "gz"))
    nx, ny = lax.axis_size("gx"), lax.axis_size("gy")
    own = (position // 4, position // 2 % 2, position % 2)
    theirs = (sender // 4, sender // 2 % 2, sender % 2)
    beyond = (u + 2 * own[0] - 1, w + 2 * own[1] - 1, q + 2 * own[2] - 1)
    sizes = (nx, ny, 2)
    r = lax.broadcasted_iota(jnp.int32, sender.shape, 1)
    face = r < 192
    t = jnp.where(face, r % 64, r % 16)
    high, low = t // 8, t % 8
    past = (
        (r < 64) | ((r >= 192) & (r < 224)) | (r >= 240),
        ((r >= 64) & (r < 128)) | ((r >= 192) & (r < 208)) | (r >= 224),
        ((r >= 128) & (r < 192)) | (r >= 208))
    index = (
        jnp.where(face, high, t),
        jnp.where(r < 64, high, jnp.where(face, low, t)),
        jnp.where(face, low, t))
    valid = face | (t < jnp.where(r < 240, 8, 1))
    spot = []
    for axis in range(3):
        far = 9 * own[axis]
        near = 9 - far
        same = theirs[axis] == own[axis]
        inner = jnp.where(same, 1 + index[axis], near)
        inner_ok = same | (index[axis] == 7 * own[axis])
        there = jnp.zeros_like(r) + beyond[axis]
        outer_ok = (theirs[axis] != own[axis]) & (there >= 0) & (there < sizes[axis])
        spot.append(jnp.where(past[axis], far, inner))
        valid = valid & ((past[axis] & outer_ok) | (jnp.logical_not(past[axis]) & inner_ok))
    return jnp.where(valid, (spot[0] * 10 + spot[1]) * 16 + spot[2], -1)


def build_patch(rows, picked, code, level_ref, patch_refs):
    n = lax.broadcasted_iota(jnp.int32, (800, 256), 0)
    target = n // 8 * 16 + n % 8
    level = lax.broadcasted_iota(jnp.int32, rows.shape, 0) % 8
    for dz in (0, 1, 2):
        pick = jnp.where(target + dz == code, 1.0, 0.0).astype(BF)
        halo = jnp.dot(pick, picked, preferred_element_type=F32)
        if dz == 0:
            mine = jnp.where(level == 0, 0.0, pltpu.roll(rows, 1, 0))
        elif dz == 1:
            mine = rows
        else:
            mine = jnp.where(level == 7, 0.0, pltpu.roll(rows, 511, 0))
        level_ref[...] = halo
        for i in range(8):
            spot = pl.ds(((i + 1) * 10 + 1) * 8, 64)
            level_ref[spot, :] = level_ref[spot, :] + mine[64 * i : 64 * i + 64]
        for part, patch_ref in enumerate(patch_refs):
            for dy in (0, 1, 2):
                tap = dy * 3 + dz
                for x in range(10):
                    patch_ref[pl.ds(64 * x, 64), pl.ds(tap * WIDE, WIDE)] = (
                        level_ref[pl.ds((x * 10 + dy) * 8, 64), pl.ds(part * WIDE, WIDE)].astype(BF))


def convolve(start, patch_ref, weight_ref):
    total = start
    for dx in (0, 1, 2):
        total = total + jnp.dot(patch_ref[pl.ds(64 * dx, 512), :], weight_ref[dx], preferred_element_type=F32)
    return total


def pack_grads(block, store):
    lane = lax.broadcasted_iota(jnp.int32, (C, WIDE), 1)
    for group in range(2):
        last = block(4 * group + 3)
        for t in range(3):
            shifted = pltpu.roll(last, C - 32 * t, 1)
            store(3 * group + t, jnp.where(lane < C, block(4 * group + t), shifted))
    store(6, block(8))


def unpack_grads(load, store):
    lane = lax.broadcasted_iota(jnp.int32, (C, WIDE), 1)
    for group in range(2):
        last = jnp.zeros((C, WIDE), F32)
        for t in range(3):
            tile = load(3 * group + t)
            store(4 * group + t, tile)
            moved = pltpu.roll(tile, 32 + 32 * t, 1)
            last = jnp.where((lane >= 32 * t) & (lane < 32 * t + 32), moved, last)
        store(4 * group + 3, last)
    store(8, load(6))


def square(block):
    gap = WIDE - C
    wide = jnp.concatenate([block.astype(F32), jnp.zeros((C, gap), F32)], axis=1)
    return jnp.concatenate([wide, jnp.zeros((gap, WIDE), F32)], axis=0)


def lay_weights(kernel_ref, weight_ref, turned):
    def step(k, carry):
        rows = pl.ds(pl.multiple_of(k % 9 * WIDE, WIDE), WIDE)
        block = square(kernel_ref[26 - k]).T if turned else square(kernel_ref[k])
        weight_ref[k // 9, rows, :] = block.astype(BF)
        return carry

    lax.fori_loop(0, 27, step, 0)


ROWS = 4096
HALF = ROWS // 2
STRIP = 7 * C
PART = HALF // 16
CELL = PART // 4


def ring(distance, size):
    return min(distance, size - distance)


PLANE = sorted(range(1, 16), key=lambda t: -ring(t // 4, 4) - ring(t % 4, 4))
LINE = sorted(range(1, 16), key=lambda t: -ring(t, 16))


def places():
    u = lax.axis_index("gx")
    w = lax.axis_index("gy")
    q = lax.axis_index("gz")
    core = w % 2
    y = w // 2 % 4
    x = q * 2 + w // 8
    mate = (u, w + 1 - 2 * core, q)

    def plane_peer(t):
        px = (x + t // 4) % 4
        py = (y + t % 4) % 4
        return px * 4 + py, (u, ((px % 2) * 4 + py) * 2 + core, px // 2)

    def near_peer(t):
        r = (u % 4 + t) % 4
        return r, (u // 4 * 4 + r, w, q)

    def line_peer(t):
        return (u + t) % 16, w, q

    return core, x, y, mate, plane_peer, near_peer, line_peer


def greet_sharers(barrier):
    core, x, y, mate, plane_peer, near_peer, line_peer = places()
    for t in LINE:
        pl.semaphore_signal(barrier, inc=1, device_id=line_peer(t), device_id_type=MESH)
    for t in PLANE:
        pl.semaphore_signal(barrier, inc=1, device_id=plane_peer(t)[1], device_id_type=MESH)
    pl.semaphore_signal(barrier, inc=1, device_id=mate, device_id_type=MESH)


def remote(src, dst, sends, recvs, index, device):
    return pltpu.make_async_remote_copy(
        src_ref=src, dst_ref=dst, send_sem=sends.at[index], recv_sem=recvs.at[index],
        device_id=device, device_id_type=MESH)


def swap_copy(strip, half_out, half_in, swap_send, swap_recv):
    rows = pl.ds(strip * STRIP, STRIP)
    return remote(half_out.at[rows, :], half_in.at[rows, :], swap_send, swap_recv, strip, places()[3])


def start_swap(strip, data_ref, half_out, half_in, swap_send, swap_recv):
    core = places()[0]
    theirs = pl.multiple_of((1 - core) * HALF + strip * STRIP, 16)
    half_out[pl.ds(strip * STRIP, STRIP), :] = data_ref[pl.ds(theirs, STRIP), :]
    swap_copy(strip, half_out, half_in, swap_send, swap_recv).start()


def all_sum(fill_plane, fill_line, data_ref, spread, gathered, half_out, half_in, total, plane_out, plane_in,
            near_src, near_in, line_in, own_part, swap_send, swap_recv, plane_send, plane_recv,
            near_send, near_recv, line_send, line_recv, plane_send2, plane_recv2,
            join_send, join_recv):
    core, x, y, mate, plane_peer, near_peer, line_peer = places()
    u = lax.axis_index("gx")
    chip = x * 4 + y
    own = pl.multiple_of(core * HALF, HALF)
    other = pl.multiple_of((1 - core) * HALF, HALF)

    def plane_copy(t):
        there, device = plane_peer(t)
        rows = pl.ds(pl.multiple_of(there * PART, PART), PART)
        return remote(plane_out.at[rows, :], plane_in.at[t], plane_send, plane_recv, t, device)

    plane_copies = [plane_copy(t) for t in PLANE]
    early = 2 * STRIP // PART
    swaps = [swap_copy(strip, half_out, half_in, swap_send, swap_recv) for strip in range(3)]

    def join_strip(strip):
        rows = pl.ds(strip * STRIP, STRIP)
        swaps[strip].wait_recv()
        mine = data_ref[pl.ds(pl.multiple_of(own + strip * STRIP, 16), STRIP), :]
        both = mine + half_in[rows, :]
        total[rows, :] = both
        plane_out[rows, :] = both.astype(BF)

    join_strip(0)
    join_strip(1)
    for t, copy in zip(PLANE, plane_copies):
        pl.when(plane_peer(t)[0] < early)(copy.start)
    join_strip(2)
    rest = pl.ds(3 * STRIP, HALF - 3 * STRIP)
    total[rest, :] = jnp.zeros((HALF - 3 * STRIP, WIDE), F32)
    plane_out[rest, :] = jnp.zeros((HALF - 3 * STRIP, WIDE), BF)
    for t, copy in zip(PLANE, plane_copies):
        pl.when(plane_peer(t)[0] >= early)(copy.start)
    fill_plane()
    part = pl.multiple_of(chip * PART, PART)
    part_sum = total[pl.ds(part, PART), :]
    for t, copy in zip(reversed(PLANE), reversed(plane_copies)):
        copy.wait_recv()
        part_sum = part_sum + plane_in[t].astype(F32)
    near_src[...] = part_sum

    def near_copy(t):
        there, device = near_peer(t)
        rows = pl.ds(pl.multiple_of(there * CELL, CELL), CELL)
        return remote(near_src.at[rows, :], near_in.at[t], near_send, near_recv, t, device)

    near_copies = [near_copy(t) for t in (1, 2, 3)]
    for copy in near_copies:
        copy.start()
    cell_sum = near_src[pl.ds(pl.multiple_of(u % 4 * CELL, CELL), CELL), :]
    for t, copy in zip((1, 2, 3), near_copies):
        copy.wait_recv()
        cell_sum = cell_sum + near_in[t]

    line_in[u] = cell_sum.astype(BF)

    def line_copy(t, slot):
        return remote(line_in.at[u], line_in.at[slot], line_send, line_recv, t, line_peer(t))

    line_copies = [line_copy(t, u) for t in LINE]
    for copy in line_copies:
        copy.start()
    fill_line()
    for t in reversed(LINE):
        line_copy(t, (u - t + 16) % 16).wait_recv()
    for r in range(4):
        cells = [line_in[4 * group + r].astype(F32) for group in range(4)]
        own_part[pl.ds(r * CELL, CELL), :] = ((cells[0] + cells[1]) + (cells[2] + cells[3])).astype(BF)

    place = pl.multiple_of(own + part, PART)

    def plane_back(t):
        return remote(own_part, gathered.at[pl.ds(place, PART), :], plane_send2, plane_recv2, t, plane_peer(t)[1])

    def source_rows(t, base):
        px = (x - t // 4 + 4) % 4
        py = (y - t % 4 + 4) % 4
        return pl.ds(pl.multiple_of(base + (px * 4 + py) * PART, PART), PART)

    def plane_arrive(t):
        return remote(own_part, gathered.at[source_rows(t, own), :], plane_send2, plane_recv2, t, plane_peer(t)[1])

    def join_copy(t, base):
        rows = source_rows(t, base)
        return remote(gathered.at[rows, :], gathered.at[rows, :], join_send, join_recv, t, mate)

    backs = [plane_back(t) for t in PLANE]
    for copy in backs:
        copy.start()
    gathered[pl.ds(place, PART), :] = own_part[...]
    joins = [join_copy(0, own)]
    joins[0].start()
    for t in reversed(PLANE):
        plane_arrive(t).wait_recv()
        joins.append(join_copy(t, own))
        joins[-1].start()
    spread(core)
    for t in [0, *reversed(PLANE)]:
        join_copy(t, other).wait_recv()
    spread(1 - core)
    for copy in [*swaps, *plane_copies, *near_copies, *line_copies, *backs, *joins]:
        copy.wait_send()


SHARERS = 1 + 15 + 15


def halo_kernel(position_ref, count_ref, x_hbm, g_hbm, code_hbm, first_hbm, second_hbm,
                rows_ref, halo_ref, x_weight_ref, g_weight_ref, x_ref, g_ref, code_ref, first_ref, second_ref, load_sem,
                wide_ref, msg_ref, into_ref, send_sem, recv_sem):
    q = lax.axis_index("gz")
    barrier = pltpu.get_barrier_semaphore()
    greet_neighbours(barrier)
    loads = [
        pltpu.make_async_copy(src, dst, load_sem.at[i])
        for i, (src, dst) in enumerate((
            (x_hbm, x_ref), (g_hbm, g_ref), (code_hbm, code_ref), (first_hbm, first_ref), (second_hbm, second_ref)))]
    for load in loads:
        load.start()
    for load in loads[:3]:
        load.wait()
    pack_rows(position_ref[0], count_ref[0], x_ref, g_ref, code_ref, wide_ref, rows_ref)
    pack_messages(wide_ref, msg_ref, q)
    pl.semaphore_wait(barrier, 17)
    copies = halo_copies(msg_ref, into_ref, send_sem, recv_sem)
    for copy in copies:
        copy.start()
    for load in loads[3:]:
        load.wait()
    lay_weights(first_ref, x_weight_ref, False)
    lay_weights(second_ref, g_weight_ref, True)
    for copy in copies:
        copy.wait()
    halo_ref[...] = into_ref[...]


def halo(position, count, x, g, codes, first, second):
    sems = lambda n: pltpu.SemaphoreType.DMA((n,))
    taps = 9 * WIDE
    anywhere = pl.BlockSpec(memory_space=pl.ANY)
    return pl.pallas_call(
        halo_kernel,
        out_shape=(
            pltpu.VMEM((512, 2 * WIDE), BF), pltpu.VMEM((MSG, 2 * WIDE), BF),
            pltpu.VMEM((3, taps, WIDE), BF), pltpu.VMEM((3, taps, WIDE), BF)),
        in_specs=[SMEM, SMEM] + [anywhere] * 5,
        out_specs=(VMEM,) * 4,
        scratch_shapes=[
            pltpu.VMEM((C, 512), BF), pltpu.VMEM((C, 512), BF), pltpu.VMEM((1, 64), jnp.int32),
            pltpu.VMEM((27, C, C), BF), pltpu.VMEM((27, C, C), BF), sems(5),
            pltpu.VMEM((2, 512, WIDE), F32), pltpu.VMEM((MSG, 2 * WIDE), BF), pltpu.VMEM((MSG, 2 * WIDE), BF),
            sems(17), sems(17),
        ],
        compiler_params=pltpu.CompilerParams(
            collective_id=2, has_side_effects=True, vmem_limit_bytes=24 * 2 ** 20),
        name="halo",
    )(position, count, *(pltpu.with_memory_space_constraint(a, pltpu.HBM) for a in (x, g, codes, first, second)))


def whole_kernel(scale, position_ref, first_hbm, rows_ref, into_ref, x_weight_ref, g_weight_ref,
                 out_ref, first_out_ref, second_out_ref, first_ref, load_sem, wide_ref, back_msg_ref, back_into_ref,
                 back_weight_ref, level_ref, x_patch_ref, g_patch_ref,
                 back_level_ref, back_patch_ref, grads_ref, data_ref, delta_ref,
                 back_send_sem, back_recv_sem, *reduce_refs):
    q = lax.axis_index("gz")
    position = position_ref[0]
    barrier = pltpu.get_barrier_semaphore()
    greet_sharers(barrier)
    greet_neighbours(barrier)
    load = pltpu.make_async_copy(first_hbm, first_ref, load_sem.at[0])
    load.start()

    rows = rows_ref[...].astype(F32)
    picked = pick_messages(position, into_ref)
    sender = picked[:, :WIDE].astype(F32).T[C : C + 8].astype(jnp.int32)
    code = halo_codes(position, sender)[:1]
    build_patch(rows, picked, code, level_ref, (x_patch_ref, g_patch_ref))
    nothing = jnp.zeros((512, WIDE), F32)
    pre = convolve(nothing, x_patch_ref, x_weight_ref)
    back = convolve(nothing, g_patch_ref, g_weight_ref)
    mask = jnp.broadcast_to(rows[:, C + 1 : C + 2], (512, WIDE))
    sigma = jax.nn.sigmoid(pre)
    hidden = pre * sigma * mask
    delta = (back * sigma * (1.0 + pre * (1.0 - sigma)) * mask).astype(BF)
    delta_ref[...] = delta
    wide_ref[0] = delta.astype(F32)
    back_copies = halo_copies(back_msg_ref, back_into_ref, back_send_sem, back_recv_sem)

    turned = (delta.astype(F32).T[:C].astype(BF), hidden.T[:C].astype(BF))
    for dx in (0, 1, 2):
        for half, patch_ref in ((0, x_patch_ref), (1, g_patch_ref)):
            grads_ref[half] = jnp.dot(
                turned[half], patch_ref[pl.ds(64 * dx, 512), :], preferred_element_type=F32)

            def block(tap):
                return grads_ref[half, :, pl.ds(tap * WIDE, WIDE)] * scale

            def store(tile, value):
                data_ref[pl.ds(half * HALF + dx * STRIP + tile * C, C), :] = value

            pack_grads(block, store)
        if dx == 1:
            pl.semaphore_wait(barrier, 17 + SHARERS)
            start_swap(0, data_ref, *reduce_refs[1:3], *reduce_refs[10:12])
        if dx > 0:
            start_swap(dx, data_ref, *reduce_refs[1:3], *reduce_refs[10:12])

    def fill_plane():
        pack_messages(wide_ref, back_msg_ref, q)
        for copy in back_copies:
            copy.start()
        load.wait()
        lay_weights(first_ref, back_weight_ref, True)

    def fill_line():
        for copy in back_copies:
            copy.wait()
        back_picked = pick_messages(position, back_into_ref)
        build_patch(delta_ref[...].astype(F32), back_picked, code, back_level_ref, (back_patch_ref,))
        grad = convolve(rows_ref[:, WIDE:].astype(F32), back_patch_ref, back_weight_ref)
        out_ref[...] = (grad * mask).T[:C].astype(BF)

    def spread(half):
        for which in (0, 1):

            @pl.when(half == which)
            def _():
                for dx in (0, 1, 2):

                    def load(tile):
                        return reduce_refs[0][pl.ds(which * HALF + dx * STRIP + tile * C, C), :].astype(F32)

                    def store(tap, value):
                        if which == 0:
                            first_out_ref[9 * dx + tap] = value.T[:C]
                        else:
                            second_out_ref[26 - 9 * dx - tap] = value[:, :C]

                    unpack_grads(load, store)

    all_sum(fill_plane, fill_line, data_ref, spread, *reduce_refs)


def whole(scale, position, first, rows, into, x_weight, g_weight):
    sems = lambda n: pltpu.SemaphoreType.DMA((n,))
    taps = 9 * WIDE
    anywhere = pl.BlockSpec(memory_space=pl.ANY)
    return pl.pallas_call(
        functools.partial(whole_kernel, scale),
        out_shape=(pltpu.VMEM((C, 512), BF), pltpu.VMEM((27, C, C), F32), pltpu.VMEM((27, C, C), F32)),
        in_specs=[SMEM, anywhere] + [VMEM] * 4,
        out_specs=(VMEM,) * 3,
        scratch_shapes=[
            pltpu.VMEM((27, C, C), BF), sems(1), pltpu.VMEM((1, 512, WIDE), F32),
            pltpu.VMEM((MSG, WIDE), BF), pltpu.VMEM((MSG, WIDE), BF), pltpu.VMEM((3, taps, WIDE), BF),
            pltpu.VMEM((800, 2 * WIDE), F32), pltpu.VMEM((640, taps), BF), pltpu.VMEM((640, taps), BF),
            pltpu.VMEM((800, WIDE), F32), pltpu.VMEM((640, taps), BF),
            pltpu.VMEM((2, C, taps), F32), pltpu.VMEM((ROWS, WIDE), F32), pltpu.VMEM((512, WIDE), BF),
            sems(17), sems(17),
            pltpu.VMEM((ROWS, WIDE), BF),
            pltpu.VMEM((HALF, WIDE), F32), pltpu.VMEM((HALF, WIDE), F32),
            pltpu.VMEM((HALF, WIDE), F32), pltpu.VMEM((HALF, WIDE), BF),
            pltpu.VMEM((16, PART, WIDE), BF), pltpu.VMEM((PART, WIDE), F32),
            pltpu.VMEM((4, CELL, WIDE), F32), pltpu.VMEM((16, CELL, WIDE), BF),
            pltpu.VMEM((PART, WIDE), BF),
            sems(3), sems(3), sems(16), sems(16), sems(4), sems(4), sems(16), sems(16),
            sems(16), sems(16), sems(16), sems(16),
        ],
        compiler_params=pltpu.CompilerParams(
            collective_id=1, has_side_effects=True, vmem_limit_bytes=48 * 2 ** 20),
        name="whole",
    )(
        position, pltpu.with_memory_space_constraint(first, pltpu.HBM),
        *(pltpu.with_memory_space_constraint(a, pltpu.VMEM) for a in (rows, into, x_weight, g_weight)))


def finish_kernel(grad_ref, first_ref, second_ref, grad_hbm, first_hbm, second_hbm, out_sem):
    stores = []
    for start in (0, 9, 18):
        taps = pl.ds(start, 9)
        stores.append((first_ref.at[taps], first_hbm.at[taps]))
        stores.append((second_ref.at[taps], second_hbm.at[taps]))
    stores.append((grad_ref, grad_hbm))
    copies = [pltpu.make_async_copy(here, there, out_sem.at[i]) for i, (here, there) in enumerate(stores)]
    for copy in copies:
        copy.start()
    for copy in copies:
        copy.wait()


def finish(grad, first, second):
    anywhere = pl.BlockSpec(memory_space=pl.ANY)
    return pl.pallas_call(
        finish_kernel,
        out_shape=(
            jax.ShapeDtypeStruct((C, 512), BF),
            jax.ShapeDtypeStruct((27, C, C), F32), jax.ShapeDtypeStruct((27, C, C), F32)),
        in_specs=[VMEM] * 3,
        out_specs=(anywhere,) * 3,
        scratch_shapes=[pltpu.SemaphoreType.DMA((7,))],
        compiler_params=pltpu.CompilerParams(vmem_limit_bytes=16 * 2 ** 20),
        name="finish",
    )(*(pltpu.with_memory_space_constraint(a, pltpu.VMEM) for a in (grad, first, second)))


def shards(features, cotangent, first_weight, second_weight, slot_position, brick_count, column_code):
    devices = lax.axis_size("gx") * lax.axis_size("gy") * lax.axis_size("gz")
    scale = float(devices ** -0.5 / 8.0)
    position = slot_position.reshape(1)
    handed = halo(
        position, brick_count.reshape(1), features.reshape(C, 512), cotangent.reshape(C, 512),
        column_code.reshape(1, 64), first_weight, second_weight)
    grad_input, first_grad, second_grad = finish(*whole(scale, position, first_weight, *handed))
    return grad_input.reshape(1, 1, 1, 1, C, 512), first_grad, second_grad


def solution(mesh):
    placed = (
        P("gx", "gy", "gz", None, None, None),
        P("gx", "gy", "gz", None, None, None),
        P(),
        P(),
        P("gx", "gy", "gz", None),
        P("gx", "gy", "gz"),
        P("gx", "gy", "gz", None, None),
    )
    return jax.shard_map(
        shards,
        mesh=mesh,
        in_specs=placed,
        out_specs=(P("gx", "gy", "gz", None, None, None), P(), P()),
        check_vma=False,
    )
```

```python
import functools

import jax
import jax.numpy as jnp
from jax import lax
from jax.experimental import pallas as pl
from jax.experimental.pallas import tpu as pltpu
from jax.sharding import PartitionSpec as P

MESH = pl.DeviceIdType.MESH
VMEM = pl.BlockSpec(memory_space=pltpu.VMEM)
SMEM = pl.BlockSpec(memory_space=pltpu.SMEM)
C = 96
WIDE = 128
MSG = 512
BF = jnp.bfloat16
F32 = jnp.float32


def message_plan():
    plan = []
    for ix in (0, 1):
        for iy in (0, 1):
            plan.append((13 + 2 * ix + iy, 16, (1 - 2 * ix, 1 - 2 * iy, 1)))
    for iy in (0, 1):
        plan.append((11 + iy, 16, (0, 1 - 2 * iy, 1)))
    for ix in (0, 1):
        plan.append((9 + ix, 16, (1 - 2 * ix, 0, 1)))
    for ix in (0, 1):
        for iy in (0, 1):
            plan.append((5 + 2 * ix + iy, 16, (1 - 2 * ix, 1 - 2 * iy, 0)))
    plan.append((4, 64, (0, 0, 1)))
    for iy in (0, 1):
        plan.append((2 + iy, 64, (0, 1 - 2 * iy, 0)))
    for ix in (0, 1):
        plan.append((ix, 64, (1 - 2 * ix, 0, 0)))
    return plan


def slot_row(slot):
    return slot * 64 if slot < 5 else 320 + (slot - 5) * 16


def pack_messages(wide_ref, msg_ref, q):
    blank = jnp.zeros((8, WIDE), F32)
    only = lax.broadcasted_iota(jnp.int32, (8, WIDE), 0) == 0
    for part in range(wide_ref.shape[0]):

        def rows(*spot, **stride):
            return wide_ref[part, pl.ds(*spot, **stride), :]

        def put(slot, value):
            start = slot_row(slot)
            msg_ref[pl.ds(start, value.shape[0]), pl.ds(part * WIDE, WIDE)] = value.astype(BF)

        def side(low, high):
            return jnp.where(q == 0, high, low)

        for ix in (0, 1):
            put(ix, rows(448 * (1 - ix), 64))
        for iy in (0, 1):
            edge = [rows(64 * i + 56 * (1 - iy), 8) for i in range(8)]
            put(2 + iy, jnp.concatenate(edge, axis=0))
        put(4, side(rows(0, 64, stride=8), rows(7, 64, stride=8)))
        for ix in (0, 1):
            x0 = 448 * (1 - ix)
            for iy in (0, 1):
                column = rows(x0 + 56 * (1 - iy), 8)
                put(5 + 2 * ix + iy, jnp.concatenate([column, blank], axis=0))
                corner = side(column, pltpu.roll(column, 1, 0))
                put(13 + 2 * ix + iy, jnp.concatenate([jnp.where(only, corner, 0.0), blank], axis=0))
            line = side(rows(x0, 8, stride=8), rows(x0 + 7, 8, stride=8))
            put(9 + ix, jnp.concatenate([line, blank], axis=0))
        for iy in (0, 1):
            y0 = 56 * (1 - iy)
            line = side(rows(y0, 8, stride=64), rows(y0 + 7, 8, stride=64))
            put(11 + iy, jnp.concatenate([line, blank], axis=0))


def pack_rows(position, count, x_ref, g_ref, code_ref, wide_ref, rows_ref):
    column = lax.broadcasted_iota(jnp.int32, (64, 512), 0)
    voxel = lax.broadcasted_iota(jnp.int32, (64, 512), 1)
    spread = jnp.where(column == voxel // 8, 1.0, 0.0).astype(BF)
    codes = jnp.broadcast_to(code_ref[...].astype(F32), (16, 64)).astype(BF)
    code = jnp.dot(codes, spread, preferred_element_type=F32).astype(jnp.int32)[:8]
    low = code // 8
    level = lax.broadcasted_iota(jnp.int32, (8, 512), 1) % 8
    live = (level >= low) & (level <= low + code % 8) & (count > 0)
    mask = jnp.where(live, 1.0, 0.0)
    first = lax.broadcasted_iota(jnp.int32, (8, 512), 0)
    place = jnp.where(first == 0, position.astype(F32), jnp.where(first == 1, mask, 0.0))
    blank = jnp.zeros((24, 512), F32)
    inside = jnp.broadcast_to(mask[:1], (C, 512)) > 0.0
    x = jnp.where(inside, x_ref[...].astype(F32), 0.0)
    g = jnp.where(inside, g_ref[...].astype(F32), 0.0)
    wide_ref[0] = jnp.concatenate([x, place, blank], axis=0).T
    wide_ref[1] = jnp.concatenate([g, jnp.zeros((32, 512), F32)], axis=0).T
    rows_ref[:, :WIDE] = wide_ref[0].astype(BF)
    rows_ref[:, WIDE:] = wide_ref[1].astype(BF)


def neighbour(offset):
    u, w, q = lax.axis_index("gx"), lax.axis_index("gy"), lax.axis_index("gz")
    nx, ny = lax.axis_size("gx"), lax.axis_size("gy")
    du, dv, dw = offset
    return ((u + du + nx) % nx, (w + dv + ny) % ny, 1 - q if dw else q)


def halo_copies(msg_ref, into_ref, send_sem, recv_sem):
    copies = []
    for slot, size, offset in message_plan():
        rows = pl.ds(slot_row(slot), size)
        copies.append(pltpu.make_async_remote_copy(
            src_ref=msg_ref.at[rows, :], dst_ref=into_ref.at[rows, :],
            send_sem=send_sem.at[slot], recv_sem=recv_sem.at[slot],
            device_id=neighbour(offset), device_id_type=MESH))
    return copies


def greet_neighbours(barrier):
    for _, _, offset in message_plan():
        pl.semaphore_signal(barrier, inc=1, device_id=neighbour(offset), device_id_type=MESH)


def pick_messages(position, into_ref):
    def bit(size, divisor):
        return jnp.zeros((size, into_ref.shape[1]), jnp.int32) + position // divisor % 2 == 0

    def at(slot):
        return into_ref[pl.ds(slot_row(slot), 64 if slot < 5 else 16), :].astype(F32)

    def two(slot, divisor):
        low = at(slot)
        return jnp.where(bit(low.shape[0], divisor), low, at(slot + 1))

    def four(slot):
        return jnp.where(bit(16, 4), two(slot, 2), two(slot + 2, 2))

    return jnp.concatenate(
        [two(0, 4), two(2, 2), at(4), four(5), two(9, 4), two(11, 2), four(13)], axis=0).astype(BF)


def halo_codes(position, sender):
    u, w, q = (lax.axis_index(axis) for axis in ("gx", "gy", "gz"))
    nx, ny = lax.axis_size("gx"), lax.axis_size("gy")
    own = (position // 4, position // 2 % 2, position % 2)
    theirs = (sender // 4, sender // 2 % 2, sender % 2)
    beyond = (u + 2 * own[0] - 1, w + 2 * own[1] - 1, q + 2 * own[2] - 1)
    sizes = (nx, ny, 2)
    r = lax.broadcasted_iota(jnp.int32, sender.shape, 1)
    face = r < 192
    t = jnp.where(face, r % 64, r % 16)
    high, low = t // 8, t % 8
    past = (
        (r < 64) | ((r >= 192) & (r < 224)) | (r >= 240),
        ((r >= 64) & (r < 128)) | ((r >= 192) & (r < 208)) | (r >= 224),
        ((r >= 128) & (r < 192)) | (r >= 208))
    index = (
        jnp.where(face, high, t),
        jnp.where(r < 64, high, jnp.where(face, low, t)),
        jnp.where(face, low, t))
    valid = face | (t < jnp.where(r < 240, 8, 1))
    spot = []
    for axis in range(3):
        far = 9 * own[axis]
        near = 9 - far
        same = theirs[axis] == own[axis]
        inner = jnp.where(same, 1 + index[axis], near)
        inner_ok = same | (index[axis] == 7 * own[axis])
        there = jnp.zeros_like(r) + beyond[axis]
        outer_ok = (theirs[axis] != own[axis]) & (there >= 0) & (there < sizes[axis])
        spot.append(jnp.where(past[axis], far, inner))
        valid = valid & ((past[axis] & outer_ok) | (jnp.logical_not(past[axis]) & inner_ok))
    return jnp.where(valid, (spot[0] * 10 + spot[1]) * 16 + spot[2], -1)


def build_patch(rows, picked, code, level_ref, patch_refs):
    n = lax.broadcasted_iota(jnp.int32, (800, 256), 0)
    target = n // 8 * 16 + n % 8
    level = lax.broadcasted_iota(jnp.int32, rows.shape, 0) % 8
    for dz in (0, 1, 2):
        pick = jnp.where(target + dz == code, 1.0, 0.0).astype(BF)
        halo = jnp.dot(pick, picked, preferred_element_type=F32)
        if dz == 0:
            mine = jnp.where(level == 0, 0.0, pltpu.roll(rows, 1, 0))
        elif dz == 1:
            mine = rows
        else:
            mine = jnp.where(level == 7, 0.0, pltpu.roll(rows, 511, 0))
        level_ref[...] = halo
        for i in range(8):
            spot = pl.ds(((i + 1) * 10 + 1) * 8, 64)
            level_ref[spot, :] = level_ref[spot, :] + mine[64 * i : 64 * i + 64]
        for part, patch_ref in enumerate(patch_refs):
            for dy in (0, 1, 2):
                tap = dy * 3 + dz
                for x in range(10):
                    patch_ref[pl.ds(64 * x, 64), pl.ds(tap * WIDE, WIDE)] = (
                        level_ref[pl.ds((x * 10 + dy) * 8, 64), pl.ds(part * WIDE, WIDE)].astype(BF))


def convolve(start, patch_ref, weight_ref):
    total = start
    for dx in (0, 1, 2):
        total = total + jnp.dot(patch_ref[pl.ds(64 * dx, 512), :], weight_ref[dx], preferred_element_type=F32)
    return total


def pack_grads(block, store):
    lane = lax.broadcasted_iota(jnp.int32, (C, WIDE), 1)
    for group in range(2):
        last = block(4 * group + 3)
        for t in range(3):
            shifted = pltpu.roll(last, C - 32 * t, 1)
            store(3 * group + t, jnp.where(lane < C, block(4 * group + t), shifted))
    store(6, block(8))


def unpack_grads(load, store):
    lane = lax.broadcasted_iota(jnp.int32, (C, WIDE), 1)
    for group in range(2):
        last = jnp.zeros((C, WIDE), F32)
        for t in range(3):
            tile = load(3 * group + t)
            store(4 * group + t, tile)
            moved = pltpu.roll(tile, 32 + 32 * t, 1)
            last = jnp.where((lane >= 32 * t) & (lane < 32 * t + 32), moved, last)
        store(4 * group + 3, last)
    store(8, load(6))


def square(block):
    gap = WIDE - C
    wide = jnp.concatenate([block.astype(F32), jnp.zeros((C, gap), F32)], axis=1)
    return jnp.concatenate([wide, jnp.zeros((gap, WIDE), F32)], axis=0)


def lay_weights(kernel_ref, weight_ref, turned):
    def step(k, carry):
        rows = pl.ds(pl.multiple_of(k % 9 * WIDE, WIDE), WIDE)
        block = square(kernel_ref[26 - k]).T if turned else square(kernel_ref[k])
        weight_ref[k // 9, rows, :] = block.astype(BF)
        return carry

    lax.fori_loop(0, 27, step, 0)


ROWS = 4096
HALF = ROWS // 2
STRIP = 7 * C
PART = HALF // 16
CELL = PART // 4


def ring(distance, size):
    return min(distance, size - distance)


PLANE = sorted(range(1, 16), key=lambda t: -ring(t // 4, 4) - ring(t % 4, 4))
LINE = sorted(range(1, 16), key=lambda t: -ring(t, 16))


def places():
    u = lax.axis_index("gx")
    w = lax.axis_index("gy")
    q = lax.axis_index("gz")
    core = w % 2
    y = w // 2 % 4
    x = q * 2 + w // 8
    mate = (u, w + 1 - 2 * core, q)

    def plane_peer(t):
        px = (x + t // 4) % 4
        py = (y + t % 4) % 4
        return px * 4 + py, (u, ((px % 2) * 4 + py) * 2 + core, px // 2)

    def near_peer(t):
        r = (u % 4 + t) % 4
        return r, (u // 4 * 4 + r, w, q)

    def line_peer(t):
        return (u + t) % 16, w, q

    return core, x, y, mate, plane_peer, near_peer, line_peer


def greet_sharers(barrier):
    core, x, y, mate, plane_peer, near_peer, line_peer = places()
    for t in LINE:
        pl.semaphore_signal(barrier, inc=1, device_id=line_peer(t), device_id_type=MESH)
    for t in PLANE:
        pl.semaphore_signal(barrier, inc=1, device_id=plane_peer(t)[1], device_id_type=MESH)
    pl.semaphore_signal(barrier, inc=1, device_id=mate, device_id_type=MESH)


def remote(src, dst, sends, recvs, index, device):
    return pltpu.make_async_remote_copy(
        src_ref=src, dst_ref=dst, send_sem=sends.at[index], recv_sem=recvs.at[index],
        device_id=device, device_id_type=MESH)


def swap_copy(strip, half_out, half_in, swap_send, swap_recv):
    rows = pl.ds(strip * STRIP, STRIP)
    return remote(half_out.at[rows, :], half_in.at[rows, :], swap_send, swap_recv, strip, places()[3])


def start_swap(strip, data_ref, half_out, half_in, swap_send, swap_recv):
    core = places()[0]
    theirs = pl.multiple_of((1 - core) * HALF + strip * STRIP, 16)
    half_out[pl.ds(strip * STRIP, STRIP), :] = data_ref[pl.ds(theirs, STRIP), :]
    swap_copy(strip, half_out, half_in, swap_send, swap_recv).start()


def all_sum(fill_plane, fill_line, data_ref, spread, gathered, half_out, half_in, total, plane_out, plane_in,
            near_src, near_in, line_in, own_part, swap_send, swap_recv, plane_send, plane_recv,
            near_send, near_recv, line_send, line_recv, plane_send2, plane_recv2,
            join_send, join_recv):
    core, x, y, mate, plane_peer, near_peer, line_peer = places()
    u = lax.axis_index("gx")
    chip = x * 4 + y
    own = pl.multiple_of(core * HALF, HALF)
    other = pl.multiple_of((1 - core) * HALF, HALF)

    swaps = [swap_copy(strip, half_out, half_in, swap_send, swap_recv) for strip in range(3)]
    for strip in range(3):
        rows = pl.ds(strip * STRIP, STRIP)
        swaps[strip].wait_recv()
        mine = data_ref[pl.ds(pl.multiple_of(own + strip * STRIP, 16), STRIP), :]
        both = mine + half_in[rows, :]
        total[rows, :] = both
        plane_out[rows, :] = both.astype(BF)
    rest = pl.ds(3 * STRIP, HALF - 3 * STRIP)
    total[rest, :] = jnp.zeros((HALF - 3 * STRIP, WIDE), F32)
    plane_out[rest, :] = jnp.zeros((HALF - 3 * STRIP, WIDE), BF)

    def plane_copy(t):
        there, device = plane_peer(t)
        rows = pl.ds(pl.multiple_of(there * PART, PART), PART)
        return remote(plane_out.at[rows, :], plane_in.at[t], plane_send, plane_recv, t, device)

    plane_copies = [plane_copy(t) for t in PLANE]
    for copy in plane_copies:
        copy.start()
    fill_plane()
    part = pl.multiple_of(chip * PART, PART)
    part_sum = total[pl.ds(part, PART), :]
    for t, copy in zip(reversed(PLANE), reversed(plane_copies)):
        copy.wait_recv()
        part_sum = part_sum + plane_in[t].astype(F32)
    near_src[...] = part_sum

    def near_copy(t):
        there, device = near_peer(t)
        rows = pl.ds(pl.multiple_of(there * CELL, CELL), CELL)
        return remote(near_src.at[rows, :], near_in.at[t], near_send, near_recv, t, device)

    near_copies = [near_copy(t) for t in (1, 2, 3)]
    for copy in near_copies:
        copy.start()
    cell_sum = near_src[pl.ds(pl.multiple_of(u % 4 * CELL, CELL), CELL), :]
    for t, copy in zip((1, 2, 3), near_copies):
        copy.wait_recv()
        cell_sum = cell_sum + near_in[t]

    line_in[u] = cell_sum.astype(BF)

    def line_copy(t, slot):
        return remote(line_in.at[u], line_in.at[slot], line_send, line_recv, t, line_peer(t))

    line_copies = [line_copy(t, u) for t in LINE]
    for copy in line_copies:
        copy.start()
    fill_line()
    for t in reversed(LINE):
        line_copy(t, (u - t + 16) % 16).wait_recv()
    for r in range(4):
        cells = [line_in[4 * group + r].astype(F32) for group in range(4)]
        own_part[pl.ds(r * CELL, CELL), :] = ((cells[0] + cells[1]) + (cells[2] + cells[3])).astype(BF)

    place = pl.multiple_of(own + part, PART)

    def plane_back(t):
        return remote(own_part, gathered.at[pl.ds(place, PART), :], plane_send2, plane_recv2, t, plane_peer(t)[1])

    def source_rows(t, base):
        px = (x - t // 4 + 4) % 4
        py = (y - t % 4 + 4) % 4
        return pl.ds(pl.multiple_of(base + (px * 4 + py) * PART, PART), PART)

    def plane_arrive(t):
        return remote(own_part, gathered.at[source_rows(t, own), :], plane_send2, plane_recv2, t, plane_peer(t)[1])

    def join_copy(t, base):
        rows = source_rows(t, base)
        return remote(gathered.at[rows, :], gathered.at[rows, :], join_send, join_recv, t, mate)

    backs = [plane_back(t) for t in PLANE]
    for copy in backs:
        copy.start()
    gathered[pl.ds(place, PART), :] = own_part[...]
    joins = [join_copy(0, own)]
    joins[0].start()
    for t in reversed(PLANE):
        plane_arrive(t).wait_recv()
        joins.append(join_copy(t, own))
        joins[-1].start()
    spread(core)
    for t in [0, *reversed(PLANE)]:
        join_copy(t, other).wait_recv()
    spread(1 - core)
    for copy in [*swaps, *plane_copies, *near_copies, *line_copies, *backs, *joins]:
        copy.wait_send()


SHARERS = 1 + 15 + 15


def halo_kernel(position_ref, count_ref, x_hbm, g_hbm, code_hbm, first_hbm, second_hbm,
                rows_ref, halo_ref, x_weight_ref, g_weight_ref, x_ref, g_ref, code_ref, first_ref, second_ref, load_sem,
                wide_ref, msg_ref, into_ref, send_sem, recv_sem):
    q = lax.axis_index("gz")
    barrier = pltpu.get_barrier_semaphore()
    greet_neighbours(barrier)
    loads = [
        pltpu.make_async_copy(src, dst, load_sem.at[i])
        for i, (src, dst) in enumerate((
            (x_hbm, x_ref), (g_hbm, g_ref), (code_hbm, code_ref), (first_hbm, first_ref), (second_hbm, second_ref)))]
    for load in loads:
        load.start()
    for load in loads[:3]:
        load.wait()
    pack_rows(position_ref[0], count_ref[0], x_ref, g_ref, code_ref, wide_ref, rows_ref)
    pack_messages(wide_ref, msg_ref, q)
    pl.semaphore_wait(barrier, 17)
    copies = halo_copies(msg_ref, into_ref, send_sem, recv_sem)
    for copy in copies:
        copy.start()
    for load in loads[3:]:
        load.wait()
    lay_weights(first_ref, x_weight_ref, False)
    lay_weights(second_ref, g_weight_ref, True)
    for copy in copies:
        copy.wait()
    halo_ref[...] = pick_messages(position_ref[0], into_ref)


def halo(position, count, x, g, codes, first, second):
    sems = lambda n: pltpu.SemaphoreType.DMA((n,))
    taps = 9 * WIDE
    anywhere = pl.BlockSpec(memory_space=pl.ANY)
    return pl.pallas_call(
        halo_kernel,
        out_shape=(
            pltpu.VMEM((512, 2 * WIDE), BF), pltpu.VMEM((256, 2 * WIDE), BF),
            pltpu.VMEM((3, taps, WIDE), BF), pltpu.VMEM((3, taps, WIDE), BF)),
        in_specs=[SMEM, SMEM] + [anywhere] * 5,
        out_specs=(VMEM,) * 4,
        scratch_shapes=[
            pltpu.VMEM((C, 512), BF), pltpu.VMEM((C, 512), BF), pltpu.VMEM((1, 64), jnp.int32),
            pltpu.VMEM((27, C, C), BF), pltpu.VMEM((27, C, C), BF), sems(5),
            pltpu.VMEM((2, 512, WIDE), F32), pltpu.VMEM((MSG, 2 * WIDE), BF), pltpu.VMEM((MSG, 2 * WIDE), BF),
            sems(17), sems(17),
        ],
        compiler_params=pltpu.CompilerParams(
            collective_id=2, has_side_effects=True, vmem_limit_bytes=24 * 2 ** 20),
        name="halo",
    )(position, count, *(pltpu.with_memory_space_constraint(a, pltpu.HBM) for a in (x, g, codes, first, second)))


def whole_kernel(scale, position_ref, first_hbm, rows_ref, into_ref, x_weight_ref, g_weight_ref,
                 out_ref, first_out_ref, second_out_ref, first_ref, load_sem, wide_ref, back_msg_ref, back_into_ref,
                 back_weight_ref, level_ref, x_patch_ref, g_patch_ref,
                 back_level_ref, back_patch_ref, grads_ref, data_ref, delta_ref,
                 back_send_sem, back_recv_sem, *reduce_refs):
    q = lax.axis_index("gz")
    position = position_ref[0]
    barrier = pltpu.get_barrier_semaphore()
    greet_sharers(barrier)
    greet_neighbours(barrier)
    load = pltpu.make_async_copy(first_hbm, first_ref, load_sem.at[0])
    load.start()

    rows = rows_ref[...].astype(F32)
    picked = into_ref[...]
    sender = picked[:, :WIDE].astype(F32).T[C : C + 8].astype(jnp.int32)
    code = halo_codes(position, sender)[:1]
    build_patch(rows, picked, code, level_ref, (x_patch_ref, g_patch_ref))
    nothing = jnp.zeros((512, WIDE), F32)
    pre = convolve(nothing, x_patch_ref, x_weight_ref)
    back = convolve(nothing, g_patch_ref, g_weight_ref)
    mask = jnp.broadcast_to(rows[:, C + 1 : C + 2], (512, WIDE))
    sigma = jax.nn.sigmoid(pre)
    hidden = pre * sigma * mask
    delta = (back * sigma * (1.0 + pre * (1.0 - sigma)) * mask).astype(BF)
    delta_ref[...] = delta
    wide_ref[0] = delta.astype(F32)
    back_copies = halo_copies(back_msg_ref, back_into_ref, back_send_sem, back_recv_sem)

    turned = (delta.astype(F32).T[:C].astype(BF), hidden.T[:C].astype(BF))
    for dx in (0, 1, 2):
        for half, patch_ref in ((0, x_patch_ref), (1, g_patch_ref)):
            grads_ref[half] = jnp.dot(
                turned[half], patch_ref[pl.ds(64 * dx, 512), :], preferred_element_type=F32)

            def block(tap):
                return grads_ref[half, :, pl.ds(tap * WIDE, WIDE)] * scale

            def store(tile, value):
                data_ref[pl.ds(half * HALF + dx * STRIP + tile * C, C), :] = value

            pack_grads(block, store)
        if dx == 1:
            pl.semaphore_wait(barrier, 17 + SHARERS)
            start_swap(0, data_ref, *reduce_refs[1:3], *reduce_refs[10:12])
        if dx > 0:
            start_swap(dx, data_ref, *reduce_refs[1:3], *reduce_refs[10:12])

    def fill_plane():
        pack_messages(wide_ref, back_msg_ref, q)
        for copy in back_copies:
            copy.start()
        load.wait()
        lay_weights(first_ref, back_weight_ref, True)

    def fill_line():
        for copy in back_copies:
            copy.wait()
        back_picked = pick_messages(position, back_into_ref)
        build_patch(delta_ref[...].astype(F32), back_picked, code, back_level_ref, (back_patch_ref,))
        grad = convolve(rows_ref[:, WIDE:].astype(F32), back_patch_ref, back_weight_ref)
        out_ref[...] = (grad * mask).T[:C].astype(BF)

    def spread(half):
        for which in (0, 1):

            @pl.when(half == which)
            def _():
                for dx in (0, 1, 2):

                    def load(tile):
                        return reduce_refs[0][pl.ds(which * HALF + dx * STRIP + tile * C, C), :].astype(F32)

                    def store(tap, value):
                        if which == 0:
                            first_out_ref[9 * dx + tap] = value.T[:C]
                        else:
                            second_out_ref[26 - 9 * dx - tap] = value[:, :C]

                    unpack_grads(load, store)

    all_sum(fill_plane, fill_line, data_ref, spread, *reduce_refs)


def whole(scale, position, first, rows, into, x_weight, g_weight):
    sems = lambda n: pltpu.SemaphoreType.DMA((n,))
    taps = 9 * WIDE
    anywhere = pl.BlockSpec(memory_space=pl.ANY)
    return pl.pallas_call(
        functools.partial(whole_kernel, scale),
        out_shape=(pltpu.VMEM((C, 512), BF), pltpu.VMEM((27, C, C), F32), pltpu.VMEM((27, C, C), F32)),
        in_specs=[SMEM, anywhere] + [VMEM] * 4,
        out_specs=(VMEM,) * 3,
        scratch_shapes=[
            pltpu.VMEM((27, C, C), BF), sems(1), pltpu.VMEM((1, 512, WIDE), F32),
            pltpu.VMEM((MSG, WIDE), BF), pltpu.VMEM((MSG, WIDE), BF), pltpu.VMEM((3, taps, WIDE), BF),
            pltpu.VMEM((800, 2 * WIDE), F32), pltpu.VMEM((640, taps), BF), pltpu.VMEM((640, taps), BF),
            pltpu.VMEM((800, WIDE), F32), pltpu.VMEM((640, taps), BF),
            pltpu.VMEM((2, C, taps), F32), pltpu.VMEM((ROWS, WIDE), F32), pltpu.VMEM((512, WIDE), BF),
            sems(17), sems(17),
            pltpu.VMEM((ROWS, WIDE), BF),
            pltpu.VMEM((HALF, WIDE), F32), pltpu.VMEM((HALF, WIDE), F32),
            pltpu.VMEM((HALF, WIDE), F32), pltpu.VMEM((HALF, WIDE), BF),
            pltpu.VMEM((16, PART, WIDE), BF), pltpu.VMEM((PART, WIDE), F32),
            pltpu.VMEM((4, CELL, WIDE), F32), pltpu.VMEM((16, CELL, WIDE), BF),
            pltpu.VMEM((PART, WIDE), BF),
            sems(3), sems(3), sems(16), sems(16), sems(4), sems(4), sems(16), sems(16),
            sems(16), sems(16), sems(16), sems(16),
        ],
        compiler_params=pltpu.CompilerParams(
            collective_id=1, has_side_effects=True, vmem_limit_bytes=48 * 2 ** 20),
        name="whole",
    )(
        position, pltpu.with_memory_space_constraint(first, pltpu.HBM),
        *(pltpu.with_memory_space_constraint(a, pltpu.VMEM) for a in (rows, into, x_weight, g_weight)))


def finish_kernel(grad_ref, first_ref, second_ref, grad_hbm, first_hbm, second_hbm, out_sem):
    stores = []
    for start in (0, 9, 18):
        taps = pl.ds(start, 9)
        stores.append((first_ref.at[taps], first_hbm.at[taps]))
        stores.append((second_ref.at[taps], second_hbm.at[taps]))
    stores.append((grad_ref, grad_hbm))
    copies = [pltpu.make_async_copy(here, there, out_sem.at[i]) for i, (here, there) in enumerate(stores)]
    for copy in copies:
        copy.start()
    for copy in copies:
        copy.wait()


def finish(grad, first, second):
    anywhere = pl.BlockSpec(memory_space=pl.ANY)
    return pl.pallas_call(
        finish_kernel,
        out_shape=(
            jax.ShapeDtypeStruct((C, 512), BF),
            jax.ShapeDtypeStruct((27, C, C), F32), jax.ShapeDtypeStruct((27, C, C), F32)),
        in_specs=[VMEM] * 3,
        out_specs=(anywhere,) * 3,
        scratch_shapes=[pltpu.SemaphoreType.DMA((7,))],
        compiler_params=pltpu.CompilerParams(vmem_limit_bytes=16 * 2 ** 20),
        name="finish",
    )(*(pltpu.with_memory_space_constraint(a, pltpu.VMEM) for a in (grad, first, second)))


def shards(features, cotangent, first_weight, second_weight, slot_position, brick_count, column_code):
    devices = lax.axis_size("gx") * lax.axis_size("gy") * lax.axis_size("gz")
    scale = float(devices ** -0.5 / 8.0)
    position = slot_position.reshape(1)
    handed = halo(
        position, brick_count.reshape(1), features.reshape(C, 512), cotangent.reshape(C, 512),
        column_code.reshape(1, 64), first_weight, second_weight)
    grad_input, first_grad, second_grad = finish(*whole(scale, position, first_weight, *handed))
    return grad_input.reshape(1, 1, 1, 1, C, 512), first_grad, second_grad


def solution(mesh):
    placed = (
        P("gx", "gy", "gz", None, None, None),
        P("gx", "gy", "gz", None, None, None),
        P(),
        P(),
        P("gx", "gy", "gz", None),
        P("gx", "gy", "gz"),
        P("gx", "gy", "gz", None, None),
    )
    return jax.shard_map(
        shards,
        mesh=mesh,
        in_specs=placed,
        out_specs=(P("gx", "gy", "gz", None, None, None), P(), P()),
        check_vma=False,
    )
```
